32 devices in a mesh: section: 4 (over x, core), dp: 8 (over z, y).
Axes of the slice: x: 2, y: 2, z: 4, core: 2. Of those that a mesh axis runs over, the one named last changes fastest.
Arguments:
- token_ids: int32 [32, 192], P('dp', 'section'), may hold values from 0 to 31999
- noise: float32 [32, 192, 256], P('dp', 'section'), may hold values from -6 to 6
- loss_mask: int32 [32, 192], P('dp', 'section'), may hold values 0 or 1
- time_index: int32 [32], P('dp'), may hold values from 0 to 999
- seq_counts: int32 [8], replicated, may hold values from 1 to 4
- table: bfloat16 [32000, 256], P(('section', 'dp')), may hold values from -6 to 6
- proj: bfloat16 [256, 1024], P(('section', 'dp')), may hold values from -0.375 to 0.375
- w_time: bfloat16 [4, 256, 1024], P('section'), may hold values from -0.375 to 0.375
- gain_attn: bfloat16 [4, 1024], P('section'), may hold values from 0.25 to 1.75
- w_qkv: bfloat16 [4, 1024, 3072], P('section'), may hold values from -0.1875 to 0.1875
- w_out: bfloat16 [4, 1024, 1024], P('section'), may hold values from -0.75 to 0.75
- gain_mlp: bfloat16 [4, 1024], P('section'), may hold values from 0.25 to 1.75
- w_up: bfloat16 [4, 1024, 4096], P('section'), may hold values from -0.1875 to 0.1875
- w_down: bfloat16 [4, 4096, 1024], P('section'), may hold values from -0.09375 to 0.09375
Outputs:
- seq_loss: float32 [32], P('dp')
- layer_rms: float32 [4, 3], P('section')
- noise_grad: float32 [32, 192, 256], P('dp', 'section')
- table_grad: float32 [32000, 256], P(('section', 'dp'))
- proj_grad: float32 [256, 1024], P(('section', 'dp'))
- w_time_grad: float32 [4, 256, 1024], P('section', 'dp')
- gain_attn_grad: float32 [4, 1024], P('section', 'dp')
- w_qkv_grad: float32 [4, 1024, 3072], P('section', 'dp')
- w_out_grad: float32 [4, 1024, 1024], P('section', 'dp')
- perceptron_gain_gradient: float32 [4, 1024], P('section', 'dp')
- w_up_grad: float32 [4, 1024, 4096], P('section', 'dp')
- w_down_grad: float32 [4, 4096, 1024], P('section', 'dp')
The draws below stay inside these ranges and needn't reach their ends.
Inputs may be any that keep to these rules, and one draw needn't show every extreme that they name: Index d of dp holds seq_counts[d] real sequences in its first slots; its other slots are padding, left out of the loss and the root mean squares.
All inputs are finite; a program needn't handle non-finite values. No bound on the sum of `loss_mask` on one device may be relied on, other than what follows from the above.
Results may differ from the reference program's by a relative error of at most 0.014.
Values may be sent and summed in bfloat16 or wider, within the bound.
No kernel may reach another device: no remote copies, remote signals or barrier semaphores. Data moves between devices by JAX's collectives and lax.ppermute only.
A program may use at most 256 MiB of HBM per device.

```python
import math
import jax
import jax.numpy as jnp
import numpy as np
from jax import lax

D = 1024
HEADS = 16
HEAD = 64
FF = 4096
EMB = 256
VOCAB = 32000
NOISE_LEVELS = 1000
MICRO = 4
LEN = 192
LAYERS = 4
SEQS = 32
N_DP = 8


def plant(array, key, low, largest):
    index_at = [jax.random.randint(jax.random.fold_in(key, axis), (), 0, length) for axis, length in enumerate(array.shape)]
    main_axis = array.shape.index(max(array.shape))
    beside = index_at[:main_axis] + [(index_at[main_axis] + 1) % array.shape[main_axis]] + index_at[main_axis + 1:]
    return array.at[tuple(index_at)].set(low).at[tuple(beside)].set(largest)


def block_levels(key, shape, split, smallest, largest):
    def one(dim, parts):
        steps = jax.random.uniform(jax.random.fold_in(jax.random.fold_in(key, 6), dim), (parts,), jnp.float32, smallest / len(split), largest / len(split))
        return jnp.repeat(jnp.exp(steps), shape[dim] // parts).reshape((-1,) + (1,) * (len(shape) - dim - 1))

    factor_of = one(*split[0])
    for cut in split[1:]:
        factor_of = factor_of * one(*cut)
    return factor_of


def rank_table(count, lean):
    loads = [(1 << 20) // math.isqrt(grade ** lean) + 1 for grade in range(1, count + 1)]
    scale = 1 + sum(loads) // (1 << 30)
    return np.cumsum(np.array([max(1, weight // scale) for weight in loads]))


def ranked_ids(key, dims, amount, slope):
    grid = rank_table(amount, slope)
    pick = jax.random.randint(jax.random.fold_in(key, 1), dims, 0, int(grid[amount - 1]))
    grade = jnp.searchsorted(jnp.asarray(grid, jnp.int32), pick, side="right")
    return jax.random.permutation(jax.random.fold_in(key, 2), amount)[grade].astype(jnp.int32)


def gaussian(key, extent, spread, reach, split=(), held_as=jnp.bfloat16):
    array = jax.random.normal(key, extent, jnp.float32) * spread
    if len(split) > 0:
        array = block_levels(key, extent, split, -0.22, 0.18) * array
    return jnp.clip(array, min=-reach, max=reach).astype(held_as)


def setup_inputs(seed: int = 0) -> dict:
    key_list = jax.random.split(jax.random.key(seed), 15)
    return {
        "token_ids": plant(ranked_ids(key_list[0], (SEQS, LEN), VOCAB, 2), jax.random.fold_in(key_list[0], 3), 0, VOCAB - 1).astype(jnp.int32),
        "noise": gaussian(key_list[1], (SEQS, LEN, EMB), 1.0, 6.0, ((0, 8), (1, 4)), jnp.float32),
        "loss_mask": plant((jax.random.randint(key_list[2], (SEQS, LEN), 0, 4) < 3).astype(jnp.int32), jax.random.fold_in(key_list[2], 1), 0, 1),
        "time_index": plant(jax.random.randint(key_list[3], (SEQS,), 0, NOISE_LEVELS), jax.random.fold_in(key_list[3], 1), 0, NOISE_LEVELS - 1).astype(jnp.int32),
        "seq_counts": plant(jax.random.randint(key_list[4], (N_DP,), 1, MICRO + 1), jax.random.fold_in(key_list[4], 1), 1, MICRO).astype(jnp.int32),
        "table": gaussian(key_list[5], (VOCAB, EMB), 1.0, 6.0, ((0, 32),)),
        "proj": gaussian(key_list[6], (EMB, D), EMB ** -0.5, 0.375, ((0, 32),)),
        "w_time": gaussian(key_list[7], (LAYERS, EMB, D), EMB ** -0.5, 0.375, ((0, 4),)),
        "gain_attn": jnp.clip(1.0 + 0.15 * jax.random.normal(key_list[8], (LAYERS, D), jnp.float32), 0.25, 1.75).astype(jnp.bfloat16),
        "w_qkv": gaussian(key_list[9], (LAYERS, D, 3 * D), D ** -0.5, 0.1875, ((0, 4),)),
        "w_out": gaussian(key_list[10], (LAYERS, D, D), (D // 16) ** -0.5, 0.75, ((0, 4),)),
        "gain_mlp": jnp.clip(1.0 + 0.15 * jax.random.normal(key_list[11], (LAYERS, D), jnp.float32), 0.25, 1.75).astype(jnp.bfloat16),
        "w_up": gaussian(key_list[12], (LAYERS, D, FF), D ** -0.5, 0.1875, ((0, 4),)),
        "w_down": gaussian(key_list[13], (LAYERS, FF, D), FF ** -0.5, 0.09375, ((0, 4),)),
    }


@jax.custom_vjp
def low(v):
    return lax.optimization_barrier(v.astype(jnp.bfloat16)).astype(jnp.float32)

@jax.custom_vjp
def low_back(v):
    return v

def low_keep(v):
    return (low(v), None)

def low_pass(kept, grad):
    return (grad,)

def back_keep(v):
    return (v, None)

def back_low(kept, grad):
    return (low(grad),)
low.defvjp(low_keep, low_pass)
low_back.defvjp(back_keep, back_low)
NORM_EPSILON = 1e-06
SCORE_SCALE = 0.125
LOGIT_SCALE = 0.0625
SIGMA_LOW_LOG = math.log(0.5)
SIGMA_HIGH_LOG = math.log(50.0)
TIME_ANGLE = 64.0
PRECISION_MAXIMAL = lax.Precision.HIGHEST

def matmul(left_operand, right_operand):
    return jnp.dot(left_operand, right_operand, precision=PRECISION_MAXIMAL)

def rms_scale(values):
    return values * lax.rsqrt(lax.optimization_barrier(jnp.mean(values * values, axis=-1, keepdims=True)) + NORM_EPSILON)

def noise_level(time_index):
    fraction = time_index.astype(jnp.float32) / (NOISE_LEVELS - 1)
    return jnp.exp(SIGMA_LOW_LOG + (SIGMA_HIGH_LOG - SIGMA_LOW_LOG) * fraction)

def time_features(sigma, width):
    half = width // 2
    rates = jnp.exp(-math.log(10000.0) * jnp.arange(half, dtype=jnp.float32) / half)
    angles = jnp.log(sigma)[..., None] * TIME_ANGLE * rates
    return jnp.concatenate([jnp.cos(angles), jnp.sin(angles)], axis=-1)

def rotary_tables(length, head_size):
    half = head_size // 2
    rates = jnp.exp(-math.log(10000.0) * jnp.arange(half, dtype=jnp.float32) / half)
    angles = jnp.arange(length, dtype=jnp.float32)[:, None] * rates[None, :]
    return (jnp.cos(angles)[:, None, :], jnp.sin(angles)[:, None, :])

def rotate(values, cosines, sines):
    half = values.shape[-1] // 2
    first, second = (values[..., :half], values[..., half:])
    return jnp.concatenate([first * cosines - second * sines, second * cosines + first * sines], axis=-1)

def block_ref(hidden, time_row, layer_params, cosines, sines):
    w_time, gain_attn, w_qkv, w_out, gain_mlp, w_up, w_down = layer_params
    seq_len = hidden.shape[0]
    h_first = hidden + matmul(time_row, w_time)[None, :]
    attn_in = low(rms_scale(h_first) * gain_attn)
    mixed = low_back(matmul(attn_in, w_qkv))
    queries = low(rotate(mixed[:, :D].reshape(seq_len, HEADS, HEAD), cosines, sines))
    keys = low(rotate(mixed[:, D:2 * D].reshape(seq_len, HEADS, HEAD), cosines, sines))
    values = low(mixed[:, 2 * D:].reshape(seq_len, HEADS, HEAD))
    scores = low_back(jnp.einsum('qhd,khd->hqk', queries, keys, precision=PRECISION_MAXIMAL) * SCORE_SCALE)
    weights = low(jax.nn.softmax(scores, axis=-1))
    context = low(low_back(jnp.einsum('hqk,khd->qhd', weights, values, precision=PRECISION_MAXIMAL).reshape(seq_len, D)))
    attn_out = low_back(matmul(context, w_out))
    h_second = h_first + attn_out
    mlp_in = low(rms_scale(h_second) * gain_mlp)
    pre_act = low_back(matmul(mlp_in, w_up))
    activated = low(jax.nn.gelu(pre_act, approximate=True))
    mlp_out = low_back(matmul(activated, w_down))
    h_third = h_second + mlp_out
    squares = jnp.stack([jnp.sum(h_third * h_third), jnp.sum(attn_out * attn_out), jnp.sum(mlp_out * mlp_out)])
    return (low(low_back(h_third)), squares)

def forward(table, proj, w_time, gain_attn, w_qkv, w_out, gain_mlp, w_up, w_down, noise, token_ids, loss_mask, time_index, valid):
    norm_table = low(rms_scale(table))
    cosines, sines = rotary_tables(LEN, HEAD)
    layer_stack = (w_time, gain_attn, w_qkv, w_out, gain_mlp, w_up, w_down)

    def one_sequence(total, row):
        token_row, noise_row, mask_row, level, keep = row
        sigma = noise_level(level)
        shrink = lax.rsqrt(1.0 + sigma * sigma)
        inputs = low((jnp.take(norm_table, token_row, axis=0) + sigma * noise_row) * shrink)
        hidden = low(low_back(matmul(inputs, proj)))
        time_row = low(time_features(sigma, EMB))
        square_rows = []
        for layer in range(LAYERS):
            layer_params = tuple((weight[layer] for weight in layer_stack))
            hidden, squares = block_ref(hidden, time_row, layer_params, cosines, sines)
            square_rows.append(squares * keep)
        feats = low(rms_scale(hidden))
        latent = low(low_back(matmul(feats, proj.T)))
        logits = low_back(matmul(latent, norm_table.T) * LOGIT_SCALE)
        log_total = jax.nn.logsumexp(logits, axis=-1)
        target = jnp.take_along_axis(logits, token_row[:, None], axis=1)[:, 0]
        token_loss = (log_total - target) * mask_row * keep
        seq_sum = jnp.sum(token_loss)
        return (total + seq_sum, (seq_sum, jnp.stack(square_rows)))
    rows = (token_ids, noise, loss_mask.astype(noise.dtype), time_index, valid)
    total, (seq_sums, squares) = lax.scan(jax.checkpoint(one_sequence), jnp.zeros((), noise.dtype), rows)
    return (total, (seq_sums, squares))

def reference(token_ids, noise, loss_mask, time_index, seq_counts, table, proj, w_time, gain_attn, w_qkv, w_out, gain_mlp, w_up, w_down):
    slots = jnp.arange(SEQS, dtype=jnp.int32)
    owners = slots // MICRO
    valid = (slots % MICRO < jnp.take(seq_counts, owners)).astype(jnp.float32)
    params = tuple((weight.astype(jnp.float32) for weight in (table, proj, w_time, gain_attn, w_qkv, w_out, gain_mlp, w_up, w_down)))
    noise_values = noise.astype(jnp.float32)

    def objective(*args):
        return forward(*args, token_ids, loss_mask, time_index, valid)
    total, pullback, (seq_sums, squares) = jax.vjp(objective, *params, noise_values, has_aux=True)
    grads = pullback(jnp.ones_like(total))
    table_grad, proj_grad, w_time_grad, gain_attn_grad, w_qkv_grad, w_out_grad, perceptron_gain_gradient, w_up_grad, w_down_grad, noise_grad = grads
    seq_loss = seq_sums / LEN
    count_all = jnp.sum(seq_counts).astype(jnp.float32)
    layer_rms = jnp.sqrt(lax.optimization_barrier(jnp.sum(squares, axis=0)) / (count_all * LEN * D))
    return (seq_loss, layer_rms, noise_grad, table_grad, proj_grad, w_time_grad, gain_attn_grad, w_qkv_grad, w_out_grad, perceptron_gain_gradient, w_up_grad, w_down_grad)
```

```python
import functools, math
import jax
import jax.numpy as jnp
from jax import lax
from jax.experimental import pallas as pl
from jax.experimental.pallas import tpu as pltpu
from jax.sharding import PartitionSpec as P
HEADS=16
NOISE_LEVELS = 1000
LOGIT_SCALE = 0.0625
SIGMA_LOW_LOG = math.log(0.5)
SIGMA_HIGH_LOG = math.log(50.0)
TIME_ANGLE = 64.0
PRECISION_MAXIMAL = lax.Precision.HIGHEST
NORM_EPSILON=1e-6
SCORE_SCALE=0.125
DEPTH=3
F32=jnp.float32; BF=jnp.bfloat16
VMEM_LIMIT=60*1024*1024
GELU_A=math.sqrt(2.0/math.pi); GELU_B=0.044715

def dot(a,b): return jnp.dot(a,b,preferred_element_type=F32)
def dot_nt(a,b): return lax.dot_general(a,b,(((1,),(1,)),((),())),preferred_element_type=F32)
def dot_tn(a,b): return lax.dot_general(a,b,(((0,),(0,)),((),())),preferred_element_type=F32)

def swap_halves(x,mask):
    return jnp.where(mask,pltpu.roll(x,96,1),pltpu.roll(x,32,1))

class Loads:
    def __init__(self,sem,ahead):
        self.sem,self.ahead,self.copies,self.next=sem,ahead,[],0
    def add(self,src,dst):
        k=len(self.copies); self.copies.append(pltpu.make_async_copy(src,dst,self.sem.at[k])); return k
    def fill(self,upto):
        while self.next<min(upto,len(self.copies)):
            self.copies[self.next].start(); self.next+=1
    def wait(self,k):
        self.fill(k+1)
        self.copies[k].wait()
        self.fill(k+1+self.ahead)
class Puts:
    def __init__(self,sem): self.sem,self.copies=sem,[]
    def add(self,src,dst):
        c=pltpu.make_async_copy(src,dst,self.sem.at[len(self.copies)]); c.start(); self.copies.append(c)
    def wait(self):
        for c in self.copies: c.wait()

def fwd_kernel(info,hid_in,far_in,entry,time_rows,gain_attn,gain_mlp,cos,sin,w_qkv,w_out,w_up,w_down,
               s_hid,s_attn,s_qkv,s_prob,s_ctx,s_second,s_mlp,s_gp,s_act,
               o_next,o_sums,o_hid,o_attn,o_qkv,o_prob,o_ctx,o_second,o_mlp,o_gp,o_act,
               b_hid,b_qkvw,b_outw,b_upw,b_downw,b_attn,b_qkv,b_prob,b_ctx,b_second,b_low,b_mlp,b_gp,b_act,wsem,hsem,osem):
    active=info[0]; slot=info[1]; source=info[2]
    width=b_hid.shape[1]; T=b_hid.shape[0]
    nw=w_up.shape[1]//width
    npair=width//128
    @pl.when(active==0)
    def _():
        o_sums[...]=jnp.zeros_like(o_sums)
        o_next[...]=jnp.zeros_like(o_next)
    @pl.when(active==1)
    def _():
        src_copy=pltpu.make_async_copy(entry.at[slot],b_hid,hsem)
        in_copy=pltpu.make_async_copy(hid_in,b_hid,hsem)
        far_copy=pltpu.make_async_copy(far_in,b_hid,hsem)
        @pl.when(source==0)
        def _(): src_copy.start()
        @pl.when(source==1)
        def _(): in_copy.start()
        @pl.when(source==2)
        def _(): far_copy.start()
        ld=Loads(wsem,DEPTH)
        kq=[ld.add(w_qkv.at[:,pl.ds(i*width,width)],b_qkvw.at[i]) for i in range(3)]
        ko=ld.add(w_out,b_outw)
        ku,kd=[],[]
        for i in range(nw):
            ku.append(ld.add(w_up.at[:,pl.ds(i*width,width)],b_upw.at[i]))
            kd.append(ld.add(w_down.at[pl.ds(i*width,width),:],b_downw.at[i]))
        ld.fill(DEPTH)
        outs=Puts(osem)
        in_copy.wait()
        outs.add(b_hid,o_hid.at[slot])
        first=b_hid[...].astype(F32)+time_rows[pl.ds(slot,1),:]
        r1=lax.rsqrt(jnp.mean(first*first,axis=1,keepdims=True)+NORM_EPSILON)
        b_attn[...]=(first*r1*gain_attn[...].astype(F32)).astype(BF)
        outs.add(b_attn,o_attn.at[slot])
        lane=lax.broadcasted_iota(jnp.int32,(T,128),1)
        low=(lane%64)<32
        head0=lane<64
        c_=cos[...]; s_=sin[...]
        a=b_attn[...]
        for i in range(3):
            ld.wait(kq[i])
            m=dot(a,b_qkvw[i])
            if i<2:
                for p in range(npair):
                    x=m[:,p*128:(p+1)*128]
                    b_qkv[:,i*width+p*128:i*width+(p+1)*128]=(x*c_+swap_halves(x,low)*s_).astype(BF)
            else:
                b_qkv[:,i*width:(i+1)*width]=m.astype(BF)
        outs.add(b_qkv,o_qkv.at[slot])
        for p in range(npair):
            q=b_qkv[:,p*128:(p+1)*128]; k=b_qkv[:,width+p*128:width+(p+1)*128]; v=b_qkv[:,2*width+p*128:2*width+(p+1)*128]
            z=jnp.zeros_like(q)
            qs=jnp.concatenate([jnp.where(head0,q,z),jnp.where(head0,z,q)],axis=0)
            s=dot_nt(qs,k)*SCORE_SCALE
            e=jnp.exp(s-jnp.max(s,axis=1,keepdims=True))
            pr=(e*(1.0/jnp.sum(e,axis=1,keepdims=True))).astype(BF)
            b_prob[p]=pr
            c=dot(pr,v)
            b_ctx[:,p*128:(p+1)*128]=jnp.where(head0,c[:T],c[T:]).astype(BF)
        outs.add(b_prob,o_prob.at[slot])
        outs.add(b_ctx,o_ctx.at[slot])
        ld.wait(ko)
        ao=dot(b_ctx[...],b_outw[...])
        second=b_hid[...].astype(F32)+time_rows[pl.ds(slot,1),:]+ao
        b_second[...]=second
        b_low[...]=second.astype(BF)
        outs.add(b_low,o_second.at[slot])
        sum_a=jnp.sum(ao*ao,axis=0,keepdims=True)
        r2=lax.rsqrt(jnp.mean(second*second,axis=1,keepdims=True)+NORM_EPSILON)
        b_mlp[...]=(second*r2*gain_mlp[...].astype(F32)).astype(BF)
        outs.add(b_mlp,o_mlp.at[slot])
        acc=None
        for i in range(nw):
            cols=pl.ds(i*width,width)
            ld.wait(ku[i])
            u=dot(b_mlp[...],b_upw[i])
            u2=u*u
            th=jnp.tanh(GELU_A*(u+GELU_B*u2*u))
            h=0.5*(1.0+th)
            act=(u*h).astype(BF)
            gp=h+0.5*u*(1.0-th*th)*(GELU_A*(1.0+3.0*GELU_B*u2))
            b_act[i]=act
            b_gp[i]=gp.astype(BF)
            outs.add(b_act.at[i],o_act.at[slot,:,cols])
            outs.add(b_gp.at[i],o_gp.at[slot,:,cols])
            ld.wait(kd[i])
            d=dot(act,b_downw[i])
            acc=d if acc is None else acc+d
        third=b_second[...]+acc
        o_next[...]=third.astype(BF)
        o_sums[...]=jnp.concatenate([jnp.sum(third*third,axis=0,keepdims=True),sum_a,jnp.sum(acc*acc,axis=0,keepdims=True)],axis=0)
        outs.wait()

def store_shapes(micro,T,width,hidden):
    npair=width//128
    B=lambda *s: jax.ShapeDtypeStruct((micro,)+s,BF)
    return [B(T,width),B(T,width),B(T,3*width),B(npair,2*T,T),B(T,width),B(T,width),B(T,width),B(T,hidden),B(T,hidden)]

ANY=pl.BlockSpec(memory_space=pl.ANY)
VM=pl.BlockSpec(memory_space=pltpu.VMEM)
SM=pl.BlockSpec(memory_space=pltpu.SMEM)
def layer_forward(info,hid,far,entry,time_rows,ga,gm,cos,sin,w_qkv,w_out,w_up,w_down,stores):
    T,width=hid.shape; hidden=w_up.shape[1]; micro=entry.shape[0]; nw=hidden//width; npair=width//128
    V=lambda *s: pltpu.VMEM(s,BF)
    scratch=[V(T,width),V(3,width,width),V(width,width),V(nw,width,width),V(nw,width,width),
             V(T,width),V(T,3*width),V(npair,2*T,T),V(T,width),pltpu.VMEM((T,width),F32),V(T,width),
             V(T,width),V(nw,T,width),V(nw,T,width),
             pltpu.SemaphoreType.DMA((4+2*nw,)),pltpu.SemaphoreType.DMA,pltpu.SemaphoreType.DMA((7+2*nw,))]
    out=pl.pallas_call(fwd_kernel,
        in_specs=[SM,ANY,ANY,ANY,VM,VM,VM,VM,VM,ANY,ANY,ANY,ANY]+[ANY]*9,
        out_specs=[VM,VM]+[ANY]*9,
        out_shape=[jax.ShapeDtypeStruct((T,width),BF),jax.ShapeDtypeStruct((3,width),F32)]+store_shapes(micro,T,width,hidden),
        input_output_aliases={13+i:2+i for i in range(9)},
        scratch_shapes=scratch,
        compiler_params=pltpu.CompilerParams(vmem_limit_bytes=VMEM_LIMIT),
        cost_estimate=pl.CostEstimate(flops=2*T*width*(4*width+2*hidden),bytes_accessed=2*width*(4*width+2*hidden)+8*1024*1024,transcendentals=0),
        name="layer_fwd",
    )(info,hid,far,entry,time_rows,ga,gm,cos,sin,w_qkv,w_out,w_up,w_down,*stores)
    return out[0],out[1],out[2:]

def bwd_kernel(info,g_in,far_in,exits,time_rows,gain_attn,gain_mlp,cos,sin,w_qkv,w_out,w_up,w_down,
               hid,qkv,prob,sec,gps,
               s_g,s_pre,s_gattn,s_mixed,s_first,
               o_next,o_vec,o_g,o_pre,o_gattn,o_mixed,o_first,
               b_g,b_qkvw,b_outw,b_upw,b_downw,b_hid,b_qkv,b_prob,b_sec,b_gp,b_pre,b_gattn,b_gctx,b_second,b_mixed,wsem,hsem,osem):
    active=info[0]; slot=info[1]; source=info[2]
    width=b_hid.shape[1]; T=b_hid.shape[0]
    nw=w_up.shape[1]//width
    npair=width//128
    @pl.when(active==0)
    def _():
        o_vec[...]=jnp.zeros_like(o_vec)
        o_next[...]=jnp.zeros_like(o_next)
    @pl.when(active==1)
    def _():
        src_copy=pltpu.make_async_copy(exits.at[slot],b_g,hsem)
        in_copy=pltpu.make_async_copy(g_in,b_g,hsem)
        far_copy=pltpu.make_async_copy(far_in,b_g,hsem)
        @pl.when(source==0)
        def _(): src_copy.start()
        @pl.when(source==1)
        def _(): in_copy.start()
        @pl.when(source==2)
        def _(): far_copy.start()
        ld=Loads(wsem,DEPTH)
        kd,kg,ku=[],[],[]
        for i in range(nw):
            cols=pl.ds(i*width,width)
            kd.append(ld.add(w_down.at[cols,:],b_downw.at[i]))
            kg.append(ld.add(gps.at[slot,:,cols],b_gp.at[i]))
            ku.append(ld.add(w_up.at[:,cols],b_upw.at[i]))
        ks=ld.add(sec.at[slot],b_sec)
        ko=ld.add(w_out,b_outw)
        kqkv=ld.add(qkv.at[slot],b_qkv)
        kp=ld.add(prob.at[slot],b_prob)
        kq=[ld.add(w_qkv.at[:,pl.ds(i*width,width)],b_qkvw.at[i]) for i in range(3)]
        kh=ld.add(hid.at[slot],b_hid)
        ld.fill(DEPTH)
        outs=Puts(osem)
        in_copy.wait()
        outs.add(b_g,o_g.at[slot])
        g=b_g[...]
        acc=None
        for i in range(nw):
            ld.wait(kd[i])
            ga=dot_nt(g,b_downw[i])
            ld.wait(kg[i])
            pre=(ga*b_gp[i].astype(F32)).astype(BF)
            b_pre[i]=pre
            outs.add(b_pre.at[i],o_pre.at[slot,:,pl.ds(i*width,width)])
            ld.wait(ku[i])
            d=dot_nt(pre,b_upw[i])
            acc=d if acc is None else acc+d
        ld.wait(ks)
        second=b_sec[...].astype(F32)
        r2=lax.rsqrt(jnp.mean(second*second,axis=1,keepdims=True)+NORM_EPSILON)
        n2=second*r2
        gain_row=jnp.sum(acc*n2,axis=0,keepdims=True)
        gn=acc*gain_mlp[...].astype(F32)
        gs=b_g[...].astype(F32)+r2*(gn-n2*jnp.mean(gn*n2,axis=1,keepdims=True))
        b_second[...]=gs
        b_gattn[...]=gs.astype(BF)
        outs.add(b_gattn,o_gattn.at[slot])
        ld.wait(ko)
        b_gctx[...]=dot_nt(b_gattn[...],b_outw[...]).astype(BF)
        lane=lax.broadcasted_iota(jnp.int32,(T,128),1)
        low=(lane%64)<32
        head0=lane<64
        c_=cos[...]; s_=sin[...]
        ld.wait(kqkv); ld.wait(kp)
        for p in range(npair):
            sl=[slice(i*width+p*128,i*width+(p+1)*128) for i in range(3)]
            q=b_qkv[:,sl[0]]; k=b_qkv[:,sl[1]]; v=b_qkv[:,sl[2]]
            gc=b_gctx[:,p*128:(p+1)*128]
            z=jnp.zeros_like(q)
            qs=jnp.concatenate([jnp.where(head0,q,z),jnp.where(head0,z,q)],axis=0)
            gcs=jnp.concatenate([jnp.where(head0,gc,z),jnp.where(head0,z,gc)],axis=0)
            pl_=b_prob[p]
            b_mixed[:,sl[2]]=dot_tn(pl_,gcs).astype(BF)
            gp=dot_nt(gcs,v)
            pf=pl_.astype(F32)
            gsc=(pf*(gp-jnp.sum(gp*pf,axis=1,keepdims=True))).astype(BF)
            gq=dot(gsc,k)
            gq=jnp.where(head0,gq[:T],gq[T:])*SCORE_SCALE
            gk=dot_tn(gsc,qs)*SCORE_SCALE
            b_mixed[:,sl[0]]=(gq*c_-swap_halves(gq,low)*s_).astype(BF)
            b_mixed[:,sl[1]]=(gk*c_-swap_halves(gk,low)*s_).astype(BF)
        outs.add(b_mixed,o_mixed.at[slot])
        acc=None
        for i in range(3):
            ld.wait(kq[i])
            d=dot_nt(b_mixed[:,i*width:(i+1)*width],b_qkvw[i])
            acc=d if acc is None else acc+d
        ld.wait(kh)
        first=b_hid[...].astype(F32)+time_rows[pl.ds(slot,1),:]
        r1=lax.rsqrt(jnp.mean(first*first,axis=1,keepdims=True)+NORM_EPSILON)
        n1=first*r1
        attn_row=jnp.sum(acc*n1,axis=0,keepdims=True)
        gm=acc*gain_attn[...].astype(F32)
        gf=b_second[...]+r1*(gm-n1*jnp.mean(gm*n1,axis=1,keepdims=True))
        o_next[...]=gf.astype(BF)
        outs.add(o_next,o_first.at[slot])
        o_vec[...]=jnp.concatenate([attn_row,gain_row,jnp.sum(gf,axis=0,keepdims=True)],axis=0)
        outs.wait()

def grad_shapes(micro,T,width,hidden):
    B=lambda *s: jax.ShapeDtypeStruct((micro,)+s,BF)
    return [B(T,width),B(T,hidden),B(T,width),B(T,3*width),B(T,width)]

def layer_backward(info,g,far,exits,time_rows,ga,gm,cos,sin,w_qkv,w_out,w_up,w_down,saved,stores):
    T,width=g.shape; hidden=w_up.shape[1]; micro=exits.shape[0]; nw=hidden//width; npair=width//128
    V=lambda *s: pltpu.VMEM(s,BF)
    scratch=[V(T,width),V(3,width,width),V(width,width),V(nw,width,width),V(nw,width,width),
             V(T,width),V(T,3*width),V(npair,2*T,T),V(T,width),V(nw,T,width),V(nw,T,width),V(T,width),V(T,width),pltpu.VMEM((T,width),F32),V(T,3*width),
             pltpu.SemaphoreType.DMA((8+3*nw,)),pltpu.SemaphoreType.DMA,pltpu.SemaphoreType.DMA((4+nw,))]
    out=pl.pallas_call(bwd_kernel,
        in_specs=[SM,ANY,ANY,ANY,VM,VM,VM,VM,VM]+[ANY]*4+[ANY]*5+[ANY]*5,
        out_specs=[VM,VM]+[ANY]*5,
        out_shape=[jax.ShapeDtypeStruct((T,width),BF),jax.ShapeDtypeStruct((3,width),F32)]+grad_shapes(micro,T,width,hidden),
        input_output_aliases={18+i:2+i for i in range(5)},
        scratch_shapes=scratch,
        compiler_params=pltpu.CompilerParams(vmem_limit_bytes=VMEM_LIMIT),
        cost_estimate=pl.CostEstimate(flops=2*T*width*(4*width+2*hidden),bytes_accessed=2*width*(4*width+2*hidden)+8*1024*1024,transcendentals=0),
        name="layer_bwd",
    )(info,g,far,exits,time_rows,ga,gm,cos,sin,w_qkv,w_out,w_up,w_down,*saved,*stores)
    return out[0],out[1],out[2:]

def rope_tables(T,head):
    half=head//2
    rates=jnp.exp(-math.log(10000.0)*jnp.arange(half,dtype=F32)/half)
    ang=jnp.arange(T,dtype=F32)[:,None]*rates[None,:]
    c=jnp.cos(ang); s=jnp.sin(ang)
    return jnp.concatenate([c,c,c,c],1),jnp.concatenate([-s,s,-s,s],1)


def rms_scale(values):
    return values * lax.rsqrt(jnp.mean(values * values, axis=-1, keepdims=True) + NORM_EPSILON)


def noise_level(time_index):
    fraction = time_index.astype(jnp.float32) / (NOISE_LEVELS - 1)
    return jnp.exp(SIGMA_LOW_LOG + (SIGMA_HIGH_LOG - SIGMA_LOW_LOG) * fraction)


def time_features(sigma, width):
    half = width // 2
    rates = jnp.exp(-math.log(10000.0) * jnp.arange(half, dtype=jnp.float32) / half)
    angles = jnp.log(sigma)[..., None] * TIME_ANGLE * rates
    return jnp.concatenate([jnp.cos(angles), jnp.sin(angles)], axis=-1)


def head_forward_kernel(table, latent, o_mean, o_stats, top, total, mixed):
    step = pl.program_id(0)

    @pl.when(step == 0)
    def _():
        top[...] = jnp.full_like(top, -jnp.inf)
        total[...] = jnp.zeros_like(total)
        mixed[...] = jnp.zeros_like(mixed)

    rows = table[...]
    logits = dot_nt(rows, latent[...])
    peak = jnp.maximum(top[...], jnp.max(logits, axis=0, keepdims=True))
    fade = jnp.exp(top[...] - peak)
    e = jnp.exp(logits - peak)
    total[...] = total[...] * fade + jnp.sum(e, axis=0, keepdims=True)
    mixed[...] = mixed[...] * fade + dot_tn(rows, e.astype(BF))
    top[...] = peak

    @pl.when(step == pl.num_programs(0) - 1)
    def _():
        o_mean[...] = (mixed[...] / total[...]).astype(BF)
        o_stats[...] = jnp.concatenate([top[...], total[...]], axis=0)


def vocab_tile(rows):
    for tile in (800, 500, 400):
        if rows % tile == 0 and tile % 16 == 0:
            return tile
    return rows


def head_forward(table, latent):
    rows, emb = table.shape
    tokens = latent.shape[0]
    tile = vocab_tile(rows)
    return pl.pallas_call(
        head_forward_kernel,
        grid=(rows // tile,),
        in_specs=[pl.BlockSpec((tile, emb), lambda i: (i, 0)), pl.BlockSpec((tokens, emb), lambda i: (0, 0))],
        out_specs=[pl.BlockSpec((emb, tokens), lambda i: (0, 0)), pl.BlockSpec((2, tokens), lambda i: (0, 0))],
        out_shape=[jax.ShapeDtypeStruct((emb, tokens), BF), jax.ShapeDtypeStruct((2, tokens), F32)],
        scratch_shapes=[pltpu.VMEM((1, tokens), F32), pltpu.VMEM((1, tokens), F32), pltpu.VMEM((emb, tokens), F32)],
        compiler_params=pltpu.CompilerParams(vmem_limit_bytes=VMEM_LIMIT),
        cost_estimate=pl.CostEstimate(flops=4 * rows * emb * tokens, bytes_accessed=2 * rows * emb, transcendentals=rows * tokens),
        name="head_fwd",
    )(table, latent)


def head_backward_kernel(table, latent, log_total, weight, o_grad):
    logits = dot_nt(table[...], latent[...])
    g = (jnp.exp(logits - log_total[...]) * weight[...]).astype(BF)
    o_grad[...] = dot(g, latent[...]).astype(BF)


def head_backward(table, latent, log_total, weight):
    rows, emb = table.shape
    tokens = latent.shape[0]
    tile = vocab_tile(rows)
    return pl.pallas_call(
        head_backward_kernel,
        grid=(rows // tile,),
        in_specs=[
            pl.BlockSpec((tile, emb), lambda i: (i, 0)),
            pl.BlockSpec((tokens, emb), lambda i: (0, 0)),
            pl.BlockSpec((1, tokens), lambda i: (0, 0)),
            pl.BlockSpec((1, tokens), lambda i: (0, 0)),
        ],
        out_specs=pl.BlockSpec((tile, emb), lambda i: (i, 0)),
        out_shape=jax.ShapeDtypeStruct((rows, emb), BF),
        compiler_params=pltpu.CompilerParams(vmem_limit_bytes=VMEM_LIMIT),
        cost_estimate=pl.CostEstimate(flops=4 * rows * emb * tokens, bytes_accessed=4 * rows * emb, transcendentals=rows * tokens),
        name="head_bwd",
    )(table, latent, log_total, weight)


def blank_kernel(*refs):
    pass


def blanks(shapes):
    return pl.pallas_call(blank_kernel, out_specs=[ANY] * len(shapes), out_shape=shapes, name="blanks")()


def bits_of(size):
    bits = size.bit_length() - 1
    if 1 << bits != size:
        raise ValueError("axis size")
    return bits


def dp_orders(size):
    bits = bits_of(size)
    low = bits // 2
    return list(range(bits)), list(range(low, bits)) + list(range(low))


def swap(x, axis, bit):
    pairs = [(i, i ^ (1 << bit)) for i in range(lax.axis_size(axis))]
    return lax.ppermute(x, axis, pairs)


def gather(x, axis, order):
    index = lax.axis_index(axis)
    held = []
    for bit in order:
        other = swap(x, axis, bit)
        at = sum(1 for b in held if b > bit)
        mine = (index >> bit) & 1
        x = jnp.where(mine == 0, jnp.stack([x, other], at), jnp.stack([other, x], at))
        held.append(bit)
    size = lax.axis_size(axis)
    return x.reshape((size,) + x.shape[len(order):])


def scatter_sum(x, axis, order):
    index = lax.axis_index(axis)
    bits = bits_of(lax.axis_size(axis))
    x = x.reshape((2,) * bits + x.shape[1:])
    left = list(range(bits - 1, -1, -1))
    for n, bit in enumerate(order):
        at = left.index(bit)
        mine = (index >> bit) & 1
        sent = lax.dynamic_index_in_dim(x, 1 - mine, at, keepdims=False)
        kept = lax.dynamic_index_in_dim(x, mine, at, keepdims=False)
        got = swap(sent, axis, bit)
        x = kept.astype(F32) + got.astype(F32)
        if n + 1 < len(order):
            x = x.astype(BF)
        left.remove(bit)
    return x


def sum_all(x, axis):
    for bit in range(bits_of(lax.axis_size(axis))):
        x = x + swap(x, axis, bit)
    return x


def spread(x, axis, root):
    index = lax.axis_index(axis)
    holders = [root]
    for bit in range(bits_of(lax.axis_size(axis))):
        pairs = [(h, h ^ (1 << bit)) for h in holders]
        got = lax.ppermute(x, axis, pairs)
        fresh = [b for a, b in pairs]
        new = jnp.zeros((), jnp.bool_)
        for f in fresh:
            new = new | (index == f)
        x = jnp.where(new, got, x)
        holders = holders + fresh
    return x


def delay(section):
    return section + section // 2


def body(
    token_ids,
    noise,
    loss_mask,
    time_index,
    seq_counts,
    table,
    proj,
    w_time,
    gain_attn,
    w_qkv,
    w_out,
    gain_mlp,
    w_up,
    w_down,
):
    sections = lax.axis_size("section")
    section = lax.axis_index("section")
    groups = lax.axis_size("dp")
    micro, shard = token_ids.shape
    seq_len = shard * sections
    tokens = micro * seq_len
    width = w_qkv.shape[1]
    hidden = w_up.shape[2]
    emb = table.shape[1]
    last = sections - 1
    count = seq_counts[lax.axis_index("dp")]
    count_all = jnp.sum(seq_counts).astype(F32)
    valid = (jnp.arange(micro) < count).astype(F32)
    low_first, high_first = dp_orders(groups)
    gather_order = high_first[::-1] if False else low_first[::-1]
    section_order = list(range(bits_of(sections)))

    own_rows, table_back = jax.vjp(rms_scale, table.astype(F32))
    own_low = own_rows.astype(BF)
    own_count = own_low.shape[0]
    rows_sec = gather(own_low, "dp", gather_order).reshape(groups * own_count, emb)
    vocab_sec = groups * own_count
    proj_sec = gather(proj, "dp", gather_order)
    proj_full = gather(proj_sec, "section", section_order).reshape(emb, width)
    both = gather(jnp.stack([token_ids, loss_mask]), "section", section_order)
    ids_blocks = both[:, 0].reshape(-1) - section * vocab_sec
    both_rows = jnp.transpose(both, (1, 2, 0, 3)).reshape(2, tokens)
    ids_rows = both_rows[0] - section * vocab_sec
    weight = both_rows[1].astype(F32) * jnp.repeat(valid, seq_len)
    onehot = (ids_blocks[:, None] == jnp.arange(vocab_sec)[None, :]).astype(BF)
    partial = dot(onehot, rows_sec).astype(BF).reshape(sections, micro * shard, emb)
    picked = scatter_sum(partial, "section", section_order[::-1])
    sigma = noise_level(time_index)
    shrink = lax.rsqrt(1.0 + sigma * sigma)
    inputs = (
        (picked.reshape(micro, shard, emb) + sigma[:, None, None] * noise) * shrink[:, None, None]
    ).astype(BF)
    inputs_all = gather(inputs, "section", section_order)
    inputs_all = jnp.transpose(inputs_all, (1, 0, 2, 3)).reshape(tokens, emb)
    entry = dot(inputs_all, proj_full).astype(BF).reshape(micro, seq_len, width)
    picked_all = gather(picked.astype(BF).reshape(micro, shard, emb), "section", section_order)
    picked_all = jnp.transpose(picked_all, (1, 0, 2, 3)).reshape(tokens, emb)
    time_low = time_features(sigma, emb).astype(BF)
    time_rows = dot(time_low, w_time[0])
    cosines, sines = rope_tables(seq_len, width // HEADS)
    weights = (w_qkv[0], w_out[0], w_up[0], w_down[0])

    stores = blanks(store_shapes(micro, seq_len, width, hidden))
    offset = delay(section)
    ticks = micro + delay(last)
    core_in = entry[0]
    x_next = x_in = entry[0]
    square_sums = jnp.zeros((3,), F32)
    finals = []
    for tick in range(ticks):
        slot = tick - offset
        active = (slot >= 0) & (slot < micro)
        safe = jnp.clip(slot, 0, micro - 1)
        source = jnp.where(section == 0, 0, jnp.where(section % 2 == 1, 1, 2))
        info = jnp.stack([active.astype(jnp.int32), safe, source]).astype(jnp.int32)
        sent, sums, stores = layer_forward(
            info, core_in, x_in, entry, time_rows, gain_attn, gain_mlp, cosines, sines, *weights, stores
        )
        square_sums = square_sums + jnp.sum(sums, axis=1) * valid[safe]
        if tick - delay(last) >= 0:
            finals.append(sent)
        going = [s for s in range(last) if 0 <= tick - delay(s) < micro]
        core_pairs = [(s, s + 1) for s in going if s % 2 == 0]
        x_pairs = [(s, s + 1) for s in going if s % 2 == 1]
        core_in = lax.ppermute(sent, "section", core_pairs) if core_pairs else sent
        x_in = x_next
        x_next = lax.ppermute(sent, "section", x_pairs) if x_pairs else sent
    total_sums = sum_all(square_sums, "dp")
    layer_rms = jnp.sqrt(total_sums / (count_all * seq_len * width))[None, :]

    final = jnp.concatenate(finals, axis=0).astype(F32)
    normalized, head_back = jax.vjp(rms_scale, final)
    feats = normalized.astype(BF)
    latent = (dot_nt(feats, proj_full).astype(BF).astype(F32) * LOGIT_SCALE).astype(BF)
    latent = spread(latent, "section", last)
    mean, stats = head_forward(rows_sec, latent)
    for bit in section_order:
        other_mean, other_stats = swap(mean, "section", bit), swap(stats, "section", bit)
        peak = jnp.maximum(stats[0], other_stats[0])
        mine_part = stats[1] * jnp.exp(stats[0] - peak)
        other_part = other_stats[1] * jnp.exp(other_stats[0] - peak)
        total = mine_part + other_part
        mean = (mean.astype(F32) * (mine_part / total) + other_mean.astype(F32) * (other_part / total))
        if bit != section_order[-1]:
            mean = mean.astype(BF)
        stats = jnp.stack([peak, total])
    log_total = stats[0] + jnp.log(stats[1])
    target_logit = jnp.sum(latent.astype(F32) * picked_all.astype(F32), axis=1)
    token_loss = (log_total - target_logit) * weight
    seq_loss = jnp.sum(token_loss.reshape(micro, seq_len), axis=1) / seq_len
    grad_latent = ((mean.T - picked_all.astype(F32)) * (weight * LOGIT_SCALE)[:, None]).astype(BF)
    grad_table_head = head_backward(rows_sec, latent, log_total[None, :], weight[None, :])
    grad_final = head_back(dot(grad_latent, proj_full))[0].astype(BF)
    exit_grad = grad_final.reshape(micro, seq_len, width)
    grad_proj = jnp.where(section == last, dot_tn(grad_latent, feats), 0.0)

    saved = [stores[0], stores[2], stores[3], stores[5], stores[7]]
    grads = blanks(grad_shapes(micro, seq_len, width, hidden))
    core_in = exit_grad[0]
    x_next = x_in = exit_grad[0]
    gain_sums = jnp.zeros((2, width), F32)
    time_terms = []
    time_sum = jnp.zeros((micro, width), F32)
    for tick in range(ticks):
        slot = tick - (delay(last) - offset)
        active = (slot >= 0) & (slot < micro)
        safe = jnp.clip(slot, 0, micro - 1)
        source = jnp.where(section == last, 0, jnp.where(section % 2 == 0, 1, 2))
        info = jnp.stack([active.astype(jnp.int32), safe, source]).astype(jnp.int32)
        sent, rows, grads = layer_backward(
            info, core_in, x_in, exit_grad, time_rows, gain_attn, gain_mlp, cosines, sines, *weights, saved, grads
        )
        gain_sums = gain_sums + rows[:2]
        time_sum = time_sum + jnp.where((jnp.arange(micro) == safe)[:, None], rows[2:3], 0.0)
        going = [s for s in range(1, sections) if 0 <= tick - (delay(last) - delay(s)) < micro]
        core_pairs = [(s, s - 1) for s in going if s % 2 == 1]
        x_pairs = [(s, s - 1) for s in going if s % 2 == 0]
        core_in = lax.ppermute(sent, "section", core_pairs) if core_pairs else sent
        x_in = x_next
        x_next = lax.ppermute(sent, "section", x_pairs) if x_pairs else sent
    grad_out_all, grad_pre_all, grad_attn_all, grad_mixed_all, grad_first_all = (
        g.reshape(tokens, g.shape[2]) for g in grads
    )
    attn_in_all, context_all, mlp_in_all, activated_all = (
        stores[i].reshape(tokens, stores[i].shape[2]) for i in (1, 4, 6, 8)
    )

    def scattered(x, order):
        return scatter_sum(x.astype(BF).reshape((groups, x.shape[0] // groups) + x.shape[1:]), "dp", order)

    w_down_grad = scattered(dot_tn(activated_all, grad_out_all), low_first)
    w_up_grad = scattered(dot_tn(mlp_in_all, grad_pre_all), low_first)
    w_qkv_grad = scattered(dot_tn(attn_in_all, grad_mixed_all), low_first)
    grad_entry = spread(grad_first_all, "section", 0)
    grad_inputs = dot_nt(grad_entry, proj_full)
    grad_proj = grad_proj + jnp.where(section == 0, dot_tn(inputs_all, grad_entry), 0.0)
    proj_part = scatter_sum(grad_proj.astype(BF).reshape(sections, emb // sections, width), "section", section_order[::-1])
    w_time_term = jnp.dot(time_low.astype(F32).T, time_sum, precision=PRECISION_MAXIMAL)
    gain_rows = jnp.transpose(gain_sums.reshape(2, groups, width // groups), (1, 0, 2)).reshape(groups, 1, -1)
    gain_rows = jnp.pad(gain_rows, ((0, 0), (0, 0), (0, width - gain_rows.shape[2])))
    packed = jnp.concatenate(
        [
            dot_tn(context_all, grad_attn_all).astype(BF).reshape(groups, -1, width),
            w_time_term.astype(BF).reshape(groups, -1, width),
            proj_part.astype(BF).reshape(groups, -1, width),
            gain_rows.astype(BF),
        ],
        axis=1,
    )
    packed = scatter_sum(packed, "dp", high_first)
    at = [width // groups, emb // groups, emb // sections // groups]
    w_out_grad = packed[: at[0]]
    w_time_grad = packed[at[0] : at[0] + at[1]]
    proj_grad = packed[at[0] + at[1] : sum(at)]
    gains = packed[-1, : 2 * width // groups].reshape(2, width // groups)
    row_terms = grad_inputs * jnp.repeat(shrink, seq_len)[:, None] - latent.astype(F32) * weight[:, None]
    onehot_rows = (jnp.arange(vocab_sec)[:, None] == ids_rows[None, :]).astype(BF)
    grad_table = grad_table_head.astype(F32) + dot(onehot_rows, row_terms.astype(BF))
    table_sum = scattered(grad_table, low_first)
    table_grad = table_back(table_sum)[0]
    grad_mine = lax.dynamic_slice_in_dim(
        grad_inputs.reshape(micro, seq_len, emb), section * shard, shard, 1
    )
    noise_grad = grad_mine * (sigma * shrink)[:, None, None]
    return (
        seq_loss,
        layer_rms,
        noise_grad,
        table_grad,
        proj_grad,
        w_time_grad[None],
        gains[0][None],
        w_qkv_grad[None],
        w_out_grad[None],
        gains[1][None],
        w_up_grad[None],
        w_down_grad[None],
    )


def solution(mesh):
    return jax.shard_map(
        body,
        mesh=mesh,
        in_specs=(
            P("dp", "section"),
            P("dp", "section", None),
            P("dp", "section"),
            P("dp"),
            P(),
            P(("section", "dp"), None),
            P(("section", "dp"), None),
            P("section", None, None),
            P("section", None),
            P("section", None, None),
            P("section", None, None),
            P("section", None),
            P("section", None, None),
            P("section", None, None),
        ),
        out_specs=(
            P("dp"),
            P("section", None),
            P("dp", "section", None),
            P(("section", "dp"), None),
            P(("section", "dp"), None),
            P("section", "dp", None),
            P("section", "dp"),
            P("section", "dp", None),
            P("section", "dp", None),
            P("section", "dp"),
            P("section", "dp", None),
            P("section", "dp", None),
        ),
        check_vma=False,
    )
```

```python
import functools, math
import jax
import jax.numpy as jnp
from jax import lax
from jax.experimental import pallas as pl
from jax.experimental.pallas import tpu as pltpu
from jax.sharding import PartitionSpec as P
HEADS=16
NOISE_LEVELS = 1000
LOGIT_SCALE = 0.0625
SIGMA_LOW_LOG = math.log(0.5)
SIGMA_HIGH_LOG = math.log(50.0)
TIME_ANGLE = 64.0
PRECISION_MAXIMAL = lax.Precision.HIGHEST
NORM_EPSILON=1e-6
SCORE_SCALE=0.125
DEPTH=3
F32=jnp.float32; BF=jnp.bfloat16
VMEM_LIMIT=34*1024*1024
GELU_A=math.sqrt(2.0/math.pi); GELU_B=0.044715

def dot(a,b): return jnp.dot(a,b,preferred_element_type=F32)
def dot_nt(a,b): return lax.dot_general(a,b,(((1,),(1,)),((),())),preferred_element_type=F32)
def dot_tn(a,b): return lax.dot_general(a,b,(((0,),(0,)),((),())),preferred_element_type=F32)

def swap_halves(x,mask):
    return jnp.where(mask,pltpu.roll(x,96,1),pltpu.roll(x,32,1))

class Loads:
    def __init__(self,sem,ahead):
        self.sem,self.ahead,self.copies,self.next=sem,ahead,[],0
    def add(self,src,dst):
        k=len(self.copies); self.copies.append(pltpu.make_async_copy(src,dst,self.sem.at[k])); return k
    def fill(self,upto):
        while self.next<min(upto,len(self.copies)):
            self.copies[self.next].start(); self.next+=1
    def wait(self,k):
        self.fill(k+1)
        self.copies[k].wait()
        self.fill(k+1+self.ahead)
class Puts:
    def __init__(self,sem): self.sem,self.copies=sem,[]
    def add(self,src,dst):
        c=pltpu.make_async_copy(src,dst,self.sem.at[len(self.copies)]); c.start(); self.copies.append(c)
    def wait(self):
        for c in self.copies: c.wait()

def fwd_kernel(tick,info,hid_in,far_in,entry,time_rows,gain_attn,gain_mlp,cos,sin,w_qkv,w_out,w_up,w_down,
               s_hid,s_attn,s_qkv,s_prob,s_ctx,s_second,s_mlp,s_gp,s_act,
               o_next,o_sums,o_hid,o_attn,o_qkv,o_prob,o_ctx,o_second,o_mlp,o_gp,o_act,
               b_hid,b_attn,b_qkv,b_prob,b_ctx,b_second,b_low,b_mlp,b_gp,b_act,hsem,osem):
    active=info[tick,0]; slot=info[tick,1]; source=info[tick,2]
    width=b_hid.shape[1]; T=b_hid.shape[0]
    nw=w_up.shape[1]//width
    npair=width//128
    @pl.when(active==1)
    def _():
        src_copy=pltpu.make_async_copy(entry.at[slot],b_hid,hsem)
        @pl.when(source==0)
        def _(): src_copy.start()
        @pl.when(source==1)
        def _(): b_hid[...]=hid_in[...]
        @pl.when(source==2)
        def _(): b_hid[...]=far_in[...]
        outs=Puts(osem)
        @pl.when(source==0)
        def _(): src_copy.wait()
        outs.add(b_hid,o_hid.at[slot])
        first=b_hid[...].astype(F32)+time_rows[pl.ds(slot,1),:]
        r1=lax.rsqrt(jnp.mean(first*first,axis=1,keepdims=True)+NORM_EPSILON)
        b_attn[...]=(first*r1*gain_attn[...].astype(F32)).astype(BF)
        outs.add(b_attn,o_attn.at[slot])
        lane=lax.broadcasted_iota(jnp.int32,(T,128),1)
        low=(lane%64)<32
        head0=lane<64
        c_=cos[...]; s_=sin[...]
        a=b_attn[...]
        for i in range(3):
            m=dot(a,w_qkv[:,i*width:(i+1)*width])
            if i<2:
                for p in range(npair):
                    x=m[:,p*128:(p+1)*128]
                    b_qkv[:,i*width+p*128:i*width+(p+1)*128]=(x*c_+swap_halves(x,low)*s_).astype(BF)
            else:
                b_qkv[:,i*width:(i+1)*width]=m.astype(BF)
        outs.add(b_qkv,o_qkv.at[slot])
        for p in range(npair):
            q=b_qkv[:,p*128:(p+1)*128]; k=b_qkv[:,width+p*128:width+(p+1)*128]; v=b_qkv[:,2*width+p*128:2*width+(p+1)*128]
            z=jnp.zeros_like(q)
            qs=jnp.concatenate([jnp.where(head0,q,z),jnp.where(head0,z,q)],axis=0)
            s=dot_nt(qs,k)*SCORE_SCALE
            e=jnp.exp(s-jnp.max(s,axis=1,keepdims=True))
            pr=(e*(1.0/jnp.sum(e,axis=1,keepdims=True))).astype(BF)
            b_prob[p]=pr
            c=dot(pr,v)
            b_ctx[:,p*128:(p+1)*128]=jnp.where(head0,c[:T],c[T:]).astype(BF)
        outs.add(b_prob,o_prob.at[slot])
        outs.add(b_ctx,o_ctx.at[slot])
        ao=dot(b_ctx[...],w_out[...])
        second=b_hid[...].astype(F32)+time_rows[pl.ds(slot,1),:]+ao
        b_second[...]=second
        b_low[...]=second.astype(BF)
        outs.add(b_low,o_second.at[slot])
        sum_a=jnp.sum(ao*ao,axis=0,keepdims=True)
        r2=lax.rsqrt(jnp.mean(second*second,axis=1,keepdims=True)+NORM_EPSILON)
        b_mlp[...]=(second*r2*gain_mlp[...].astype(F32)).astype(BF)
        outs.add(b_mlp,o_mlp.at[slot])
        acc=None
        for i in range(nw):
            cols=pl.ds(i*width,width)
            u=dot(b_mlp[...],w_up[:,i*width:(i+1)*width])
            u2=u*u
            th=jnp.tanh(GELU_A*(u+GELU_B*u2*u))
            h=0.5*(1.0+th)
            act=(u*h).astype(BF)
            gp=h+0.5*u*(1.0-th*th)*(GELU_A*(1.0+3.0*GELU_B*u2))
            b_act[i]=act
            b_gp[i]=gp.astype(BF)
            outs.add(b_act.at[i],o_act.at[slot,:,cols])
            outs.add(b_gp.at[i],o_gp.at[slot,:,cols])
            d=dot(act,w_down[i*width:(i+1)*width,:])
            acc=d if acc is None else acc+d
        third=b_second[...]+acc
        o_next[...]=third.astype(BF)
        o_sums[...]=jnp.concatenate([jnp.sum(third*third,axis=0,keepdims=True),sum_a,jnp.sum(acc*acc,axis=0,keepdims=True)],axis=0)
        outs.wait()

def store_shapes(micro,T,width,hidden):
    npair=width//128
    B=lambda *s: jax.ShapeDtypeStruct((micro,)+s,BF)
    return [B(T,width),B(T,width),B(T,3*width),B(npair,2*T,T),B(T,width),B(T,width),B(T,width),B(T,hidden),B(T,hidden)]

ANY=pl.BlockSpec(memory_space=pl.ANY)
HB=pl.BlockSpec(memory_space=pltpu.HBM)
LAYER_LIMIT=22*1024*1024
VM=pl.BlockSpec(memory_space=pltpu.VMEM)
SM=pl.BlockSpec(memory_space=pltpu.SMEM)
def in_hbm(x): return pltpu.with_memory_space_constraint(x,pltpu.HBM)

def layer_forward(tick,info,hid,far,entry,time_rows,ga,gm,cos,sin,w_qkv,w_out,w_up,w_down,stores):
    T,width=hid.shape; hidden=w_up.shape[1]; micro=entry.shape[0]; nw=hidden//width; npair=width//128
    V=lambda *s: pltpu.VMEM(s,BF)
    scratch=[V(T,width),
             V(T,width),V(T,3*width),V(npair,2*T,T),V(T,width),pltpu.VMEM((T,width),F32),V(T,width),
             V(T,width),V(nw,T,width),V(nw,T,width),
             pltpu.SemaphoreType.DMA,pltpu.SemaphoreType.DMA((7+2*nw,))]
    out=pl.pallas_call(functools.partial(fwd_kernel,tick),
        in_specs=[SM,VM,VM,HB,VM,VM,VM,VM,VM,VM,VM,VM,VM]+[HB]*9,
        out_specs=[VM,VM]+[HB]*9,
        out_shape=[jax.ShapeDtypeStruct((T,width),BF),jax.ShapeDtypeStruct((3,width),F32)]+[pltpu.HBM(s.shape,s.dtype) for s in store_shapes(micro,T,width,hidden)],
        input_output_aliases={13+i:2+i for i in range(9)},
        scratch_shapes=scratch,
        compiler_params=pltpu.CompilerParams(vmem_limit_bytes=LAYER_LIMIT),
        cost_estimate=pl.CostEstimate(flops=2*T*width*(4*width+2*hidden),bytes_accessed=2*width*(4*width+2*hidden)+8*1024*1024,transcendentals=0),
        name="layer_fwd",
    )(info,hid,far,in_hbm(entry),time_rows,ga,gm,cos,sin,w_qkv,w_out,w_up,w_down,*map(in_hbm,stores))
    return out[0],out[1],out[2:]

def bwd_kernel(tick,info,g_in,far_in,exits,time_rows,gain_attn,gain_mlp,cos,sin,w_qkv,w_out,w_up,w_down,
               hid,qkv,prob,sec,gps,
               s_g,s_pre,s_gattn,s_mixed,s_first,
               o_next,o_vec,o_g,o_pre,o_gattn,o_mixed,o_first,
               b_g,b_hid,b_qkv,b_prob,b_sec,b_gp,b_pre,b_gattn,b_gctx,b_second,b_mixed,wsem,hsem,osem):
    active=info[tick,0]; slot=info[tick,1]; source=info[tick,2]
    width=b_hid.shape[1]; T=b_hid.shape[0]
    nw=w_up.shape[1]//width
    npair=width//128
    @pl.when(active==1)
    def _():
        src_copy=pltpu.make_async_copy(exits.at[slot],b_g,hsem)
        @pl.when(source==0)
        def _(): src_copy.start()
        @pl.when(source==1)
        def _(): b_g[...]=g_in[...]
        @pl.when(source==2)
        def _(): b_g[...]=far_in[...]
        ld=Loads(wsem,DEPTH)
        kg=[]
        for i in range(nw):
            cols=pl.ds(i*width,width)
            kg.append(ld.add(gps.at[slot,:,cols],b_gp.at[i]))
        ks=ld.add(sec.at[slot],b_sec)
        kqkv=ld.add(qkv.at[slot],b_qkv)
        kp=ld.add(prob.at[slot],b_prob)
        kh=ld.add(hid.at[slot],b_hid)
        ld.fill(DEPTH)
        outs=Puts(osem)
        @pl.when(source==0)
        def _(): src_copy.wait()
        outs.add(b_g,o_g.at[slot])
        g=b_g[...]
        acc=None
        for i in range(nw):
            ga=dot_nt(g,w_down[i*width:(i+1)*width,:])
            ld.wait(kg[i])
            pre=(ga*b_gp[i].astype(F32)).astype(BF)
            b_pre[i]=pre
            outs.add(b_pre.at[i],o_pre.at[slot,:,pl.ds(i*width,width)])
            d=dot_nt(pre,w_up[:,i*width:(i+1)*width])
            acc=d if acc is None else acc+d
        ld.wait(ks)
        second=b_sec[...].astype(F32)
        r2=lax.rsqrt(jnp.mean(second*second,axis=1,keepdims=True)+NORM_EPSILON)
        n2=second*r2
        gain_row=jnp.sum(acc*n2,axis=0,keepdims=True)
        gn=acc*gain_mlp[...].astype(F32)
        gs=b_g[...].astype(F32)+r2*(gn-n2*jnp.mean(gn*n2,axis=1,keepdims=True))
        b_second[...]=gs
        b_gattn[...]=gs.astype(BF)
        outs.add(b_gattn,o_gattn.at[slot])
        b_gctx[...]=dot_nt(b_gattn[...],w_out[...]).astype(BF)
        lane=lax.broadcasted_iota(jnp.int32,(T,128),1)
        low=(lane%64)<32
        head0=lane<64
        c_=cos[...]; s_=sin[...]
        ld.wait(kqkv); ld.wait(kp)
        for p in range(npair):
            sl=[slice(i*width+p*128,i*width+(p+1)*128) for i in range(3)]
            q=b_qkv[:,sl[0]]; k=b_qkv[:,sl[1]]; v=b_qkv[:,sl[2]]
            gc=b_gctx[:,p*128:(p+1)*128]
            z=jnp.zeros_like(q)
            qs=jnp.concatenate([jnp.where(head0,q,z),jnp.where(head0,z,q)],axis=0)
            gcs=jnp.concatenate([jnp.where(head0,gc,z),jnp.where(head0,z,gc)],axis=0)
            pl_=b_prob[p]
            b_mixed[:,sl[2]]=dot_tn(pl_,gcs).astype(BF)
            gp=dot_nt(gcs,v)
            pf=pl_.astype(F32)
            gsc=(pf*(gp-jnp.sum(gp*pf,axis=1,keepdims=True))).astype(BF)
            gq=dot(gsc,k)
            gq=jnp.where(head0,gq[:T],gq[T:])*SCORE_SCALE
            gk=dot_tn(gsc,qs)*SCORE_SCALE
            b_mixed[:,sl[0]]=(gq*c_-swap_halves(gq,low)*s_).astype(BF)
            b_mixed[:,sl[1]]=(gk*c_-swap_halves(gk,low)*s_).astype(BF)
        outs.add(b_mixed,o_mixed.at[slot])
        acc=None
        for i in range(3):
            d=dot_nt(b_mixed[:,i*width:(i+1)*width],w_qkv[:,i*width:(i+1)*width])
            acc=d if acc is None else acc+d
        ld.wait(kh)
        first=b_hid[...].astype(F32)+time_rows[pl.ds(slot,1),:]
        r1=lax.rsqrt(jnp.mean(first*first,axis=1,keepdims=True)+NORM_EPSILON)
        n1=first*r1
        attn_row=jnp.sum(acc*n1,axis=0,keepdims=True)
        gm=acc*gain_attn[...].astype(F32)
        gf=b_second[...]+r1*(gm-n1*jnp.mean(gm*n1,axis=1,keepdims=True))
        o_next[...]=gf.astype(BF)
        outs.add(o_next,o_first.at[slot])
        o_vec[...]=jnp.concatenate([attn_row,gain_row,jnp.sum(gf,axis=0,keepdims=True)],axis=0)
        outs.wait()

def grad_shapes(micro,T,width,hidden):
    B=lambda *s: jax.ShapeDtypeStruct((micro,)+s,BF)
    return [B(T,width),B(T,hidden),B(T,width),B(T,3*width),B(T,width)]

def layer_backward(tick,info,g,far,exits,time_rows,ga,gm,cos,sin,w_qkv,w_out,w_up,w_down,saved,stores):
    T,width=g.shape; hidden=w_up.shape[1]; micro=exits.shape[0]; nw=hidden//width; npair=width//128
    V=lambda *s: pltpu.VMEM(s,BF)
    scratch=[V(T,width),
             V(T,width),V(T,3*width),V(npair,2*T,T),V(T,width),V(nw,T,width),V(nw,T,width),V(T,width),V(T,width),pltpu.VMEM((T,width),F32),V(T,3*width),
             pltpu.SemaphoreType.DMA((4+nw,)),pltpu.SemaphoreType.DMA,pltpu.SemaphoreType.DMA((4+nw,))]
    out=pl.pallas_call(functools.partial(bwd_kernel,tick),
        in_specs=[SM,VM,VM,HB,VM,VM,VM,VM,VM]+[VM]*4+[HB]*5+[HB]*5,
        out_specs=[VM,VM]+[HB]*5,
        out_shape=[jax.ShapeDtypeStruct((T,width),BF),jax.ShapeDtypeStruct((3,width),F32)]+[pltpu.HBM(s.shape,s.dtype) for s in grad_shapes(micro,T,width,hidden)],
        input_output_aliases={18+i:2+i for i in range(5)},
        scratch_shapes=scratch,
        compiler_params=pltpu.CompilerParams(vmem_limit_bytes=LAYER_LIMIT),
        cost_estimate=pl.CostEstimate(flops=2*T*width*(4*width+2*hidden),bytes_accessed=2*width*(4*width+2*hidden)+8*1024*1024,transcendentals=0),
        name="layer_bwd",
    )(info,g,far,in_hbm(exits),time_rows,ga,gm,cos,sin,w_qkv,w_out,w_up,w_down,*map(in_hbm,saved),*map(in_hbm,stores))
    return out[0],out[1],out[2:]

def rope_tables(T,head):
    half=head//2
    rates=jnp.exp(-math.log(10000.0)*jnp.arange(half,dtype=F32)/half)
    ang=jnp.arange(T,dtype=F32)[:,None]*rates[None,:]
    c=jnp.cos(ang); s=jnp.sin(ang)
    return jnp.concatenate([c,c,c,c],1),jnp.concatenate([-s,s,-s,s],1)


def rms_scale(values):
    return values * lax.rsqrt(jnp.mean(values * values, axis=-1, keepdims=True) + NORM_EPSILON)


def noise_level(time_index):
    fraction = time_index.astype(jnp.float32) / (NOISE_LEVELS - 1)
    return jnp.exp(SIGMA_LOW_LOG + (SIGMA_HIGH_LOG - SIGMA_LOW_LOG) * fraction)


def time_features(sigma, width):
    half = width // 2
    rates = jnp.exp(-math.log(10000.0) * jnp.arange(half, dtype=jnp.float32) / half)
    angles = jnp.log(sigma)[..., None] * TIME_ANGLE * rates
    return jnp.concatenate([jnp.cos(angles), jnp.sin(angles)], axis=-1)


def head_forward_kernel(table, latent, o_mean, o_stats, top, total, mixed):
    step = pl.program_id(0)

    @pl.when(step == 0)
    def _():
        top[...] = jnp.full_like(top, -jnp.inf)
        total[...] = jnp.zeros_like(total)
        mixed[...] = jnp.zeros_like(mixed)

    rows = table[...]
    logits = dot_nt(rows, latent[...])
    peak = jnp.maximum(top[...], jnp.max(logits, axis=0, keepdims=True))
    fade = jnp.exp(top[...] - peak)
    e = jnp.exp(logits - peak)
    total[...] = total[...] * fade + jnp.sum(e, axis=0, keepdims=True)
    mixed[...] = mixed[...] * fade + dot_tn(rows, e.astype(BF))
    top[...] = peak

    @pl.when(step == pl.num_programs(0) - 1)
    def _():
        o_mean[...] = (mixed[...] / total[...]).astype(BF)
        o_stats[...] = jnp.concatenate([top[...], total[...]], axis=0)


def vocab_tile(rows):
    for tile in (800, 500, 400):
        if rows % tile == 0 and tile % 16 == 0:
            return tile
    return rows


def head_forward(table, latent):
    rows, emb = table.shape
    tokens = latent.shape[0]
    tile = vocab_tile(rows)
    return pl.pallas_call(
        head_forward_kernel,
        grid=(rows // tile,),
        in_specs=[pl.BlockSpec((tile, emb), lambda i: (i, 0)), pl.BlockSpec((tokens, emb), lambda i: (0, 0))],
        out_specs=[pl.BlockSpec((emb, tokens), lambda i: (0, 0)), pl.BlockSpec((2, tokens), lambda i: (0, 0))],
        out_shape=[jax.ShapeDtypeStruct((emb, tokens), BF), jax.ShapeDtypeStruct((2, tokens), F32)],
        scratch_shapes=[pltpu.VMEM((1, tokens), F32), pltpu.VMEM((1, tokens), F32), pltpu.VMEM((emb, tokens), F32)],
        compiler_params=pltpu.CompilerParams(vmem_limit_bytes=VMEM_LIMIT),
        cost_estimate=pl.CostEstimate(flops=4 * rows * emb * tokens, bytes_accessed=2 * rows * emb, transcendentals=rows * tokens),
        name="head_fwd",
    )(table, latent)


def head_backward_kernel(table, latent, log_total, weight, ids, terms, token, o_grad):
    logits = dot_nt(table[...], latent[...])
    g = (jnp.exp(logits - log_total[...]) * weight[...]).astype(BF)
    rows = lax.broadcasted_iota(jnp.int32, g.shape, 0) + pl.program_id(0) * g.shape[0]
    picks = jnp.where(rows == ids[...], 1.0, 0.0).astype(BF)
    o_grad[...] = (dot(g, latent[...]) + dot(picks, terms[...])).astype(BF)


def head_backward(table, latent, log_total, weight, ids, terms, token):
    rows, emb = table.shape
    tokens = latent.shape[0]
    tile = vocab_tile(rows)
    return pl.pallas_call(
        head_backward_kernel,
        grid=(rows // tile,),
        in_specs=[
            pl.BlockSpec((tile, emb), lambda i: (i, 0)),
            pl.BlockSpec((tokens, emb), lambda i: (0, 0)),
            pl.BlockSpec((1, tokens), lambda i: (0, 0)),
            pl.BlockSpec((1, tokens), lambda i: (0, 0)),
            pl.BlockSpec((1, tokens), lambda i: (0, 0)),
            pl.BlockSpec((tokens, emb), lambda i: (0, 0)),
            ANY,
        ],
        out_specs=pl.BlockSpec((tile, emb), lambda i: (i, 0)),
        out_shape=jax.ShapeDtypeStruct((rows, emb), BF),
        compiler_params=pltpu.CompilerParams(vmem_limit_bytes=VMEM_LIMIT),
        cost_estimate=pl.CostEstimate(flops=1, bytes_accessed=1, transcendentals=0),
        name="head_bwd",
    )(table, latent, log_total, weight, ids, terms, token)


def blank_kernel(*refs):
    pass


def blanks(shapes):
    return pl.pallas_call(blank_kernel, out_specs=[HB] * len(shapes), out_shape=shapes, name="blanks")()


def bits_of(size):
    bits = size.bit_length() - 1
    if 1 << bits != size:
        raise ValueError("axis size")
    return bits


def dp_orders(size):
    bits = bits_of(size)
    low = bits // 2
    return (
        list(range(bits)),
        list(range(low, bits)) + list(range(low)),
        [low] + list(range(low)) + list(range(low + 1, bits)),
    )


def swap(x, axis, bit):
    pairs = [(i, i ^ (1 << bit)) for i in range(lax.axis_size(axis))]
    return lax.ppermute(x, axis, pairs)


def gather(x, axis, order):
    index = lax.axis_index(axis)
    held = []
    for bit in order:
        other = swap(x, axis, bit)
        at = sum(1 for b in held if b > bit)
        mine = (index >> bit) & 1
        x = jnp.where(mine == 0, jnp.stack([x, other], at), jnp.stack([other, x], at))
        held.append(bit)
    size = lax.axis_size(axis)
    return x.reshape((size,) + x.shape[len(order):])


def scatter_sum(x, axis, order):
    index = lax.axis_index(axis)
    bits = bits_of(lax.axis_size(axis))
    x = x.reshape((2,) * bits + x.shape[1:])
    left = list(range(bits - 1, -1, -1))
    for n, bit in enumerate(order):
        at = left.index(bit)
        mine = (index >> bit) & 1
        sent = lax.dynamic_index_in_dim(x, 1 - mine, at, keepdims=False)
        kept = lax.dynamic_index_in_dim(x, mine, at, keepdims=False)
        got = swap(sent, axis, bit)
        x = kept.astype(F32) + got.astype(F32)
        if n + 1 < len(order):
            x = x.astype(BF)
        left.remove(bit)
    return x


def zero_of(token):
    return jnp.minimum(jnp.abs(token[(0,) * token.ndim].astype(F32)), 0.0)


def after(x, token):
    return x + zero_of(token).astype(x.dtype)


class Scatter:
    def __init__(self, blocks, order):
        self.order = list(order)
        self.left = list(range(len(order) - 1, -1, -1))
        self.index = lax.axis_index("dp")
        self.terms = [blocks.reshape((2,) * len(order) + blocks.shape[1:])]

    def _side(self, side, at):
        parts = [lax.dynamic_index_in_dim(t, side, at, keepdims=False).astype(F32) for t in self.terms]
        return sum(parts[1:], parts[0])

    def send(self, token):
        bit = self.order.pop(0)
        at = self.left.index(bit)
        self.left.remove(bit)
        mine = (self.index >> bit) & 1
        sent = (self._side(1 - mine, at) + (0.0 if token is None else zero_of(token))).astype(BF)
        self.got = lax.ppermute(sent, "dp", [(i, i ^ (1 << bit)) for i in range(lax.axis_size("dp"))])
        self.terms = [lax.dynamic_index_in_dim(t, mine, at, keepdims=False) for t in self.terms]
        return sent

    def step(self, token):
        self.terms.append(self.got)
        return self.send(token)

    def end(self, token):
        while self.order:
            token = self.step(token)
        parts = [t.astype(F32) for t in self.terms + [self.got]]
        self.total = sum(parts[1:], parts[0]) + zero_of(token)
        return self.total


def product_kernel(ids, *refs):
    left, (right, token, out, mark) = refs[:-4], refs[-4:]
    a = jnp.concatenate([r[...] for r in left], axis=1)
    out[...] = dot_tn(a, right[...]).astype(BF)
    mark[...] = jnp.zeros_like(mark)


def product(left, right, ids, block, part, parts, token):
    rows, columns = left.shape[0], right.shape[1] // parts
    count = ids.shape[0]
    tile = 512 if columns % 512 == 0 else columns
    first = part * columns // tile

    def pick(j):
        return pl.BlockSpec((rows, block), lambda i, ids: (0, ids[j]))

    return pl.pallas_call(
        product_kernel,
        grid_spec=pltpu.PrefetchScalarGridSpec(
            num_scalar_prefetch=1,
            grid=(columns // tile,),
            in_specs=[pick(j) for j in range(count)] + [pl.BlockSpec((rows, tile), lambda i, ids: (0, first + i)), ANY],
            out_specs=[
                pl.BlockSpec((count * block, tile), lambda i, ids: (0, i)),
                pl.BlockSpec((8, 128), lambda i, ids: (0, 0)),
            ],
        ),
        out_shape=[
            jax.ShapeDtypeStruct((count * block, columns), BF),
            jax.ShapeDtypeStruct((8, 128), F32),
        ],
        compiler_params=pltpu.CompilerParams(vmem_limit_bytes=VMEM_LIMIT),
        cost_estimate=pl.CostEstimate(flops=1, bytes_accessed=1, transcendentals=0),
        name="product",
    )(ids, *[left] * count, right, token)


class Product(Scatter):
    def __init__(self, left, right, order, part=0, parts=1):
        self.order = list(order)
        self.bits = len(order)
        self.left = list(range(self.bits - 1, -1, -1))
        self.index = lax.axis_index("dp")
        self.a, self.g = left, right
        self.part, self.parts = part, parts

    def _half(self, side, token):
        rows = self.a.shape[1]
        block = rows >> self.bits
        ids = jnp.array([i for i in range(1 << self.bits) if not (i >> self.bit) & 1], jnp.int32)
        ids = ids + side.astype(jnp.int32) * (1 << self.bit)
        if block % 128 == 0:
            x, mark = product(self.a, self.g, ids, block, self.part, self.parts, token)
        else:
            a = jnp.take(self.a.reshape(self.a.shape[0], -1, block), ids, axis=1).reshape(self.a.shape[0], -1)
            wide = self.g.shape[1] // self.parts
            x = dot_tn(after(a, token), self.g[:, self.part * wide : (self.part + 1) * wide]).astype(BF)
            mark = x
        return x.reshape((2,) * (self.bits - 1) + (block, x.shape[1])), mark

    def send(self, token):
        if len(self.order) == self.bits:
            self.bit = bit = self.order.pop(0)
            self.left.remove(bit)
            self.mine = (self.index >> bit) & 1
            sent, mark = self._half(1 - self.mine, token)
            self.got = lax.ppermute(sent, "dp", [(i, i ^ (1 << bit)) for i in range(lax.axis_size("dp"))])
            return mark
        return super().send(token)

    def keep(self, token):
        kept, mark = self._half(self.mine, token)
        self.terms = [kept]
        return mark


def tick_infos(ticks, offset, micro, source):
    slot = jnp.arange(ticks) - offset
    active = (slot >= 0) & (slot < micro)
    return jnp.stack(
        [active.astype(jnp.int32), jnp.clip(slot, 0, micro - 1), jnp.full((ticks,), source, jnp.int32)], axis=1
    ).astype(jnp.int32)


def sum_all(x, axis):
    for bit in range(bits_of(lax.axis_size(axis))):
        x = x + swap(x, axis, bit)
    return x


def spread(x, axis, root):
    index = lax.axis_index(axis)
    holders = [root]
    for bit in range(bits_of(lax.axis_size(axis))):
        pairs = [(h, h ^ (1 << bit)) for h in holders]
        got = lax.ppermute(x, axis, pairs)
        fresh = [b for a, b in pairs]
        new = jnp.zeros((), jnp.bool_)
        for f in fresh:
            new = new | (index == f)
        x = jnp.where(new, got, x)
        holders = holders + fresh
    return x


def delay(section):
    return section + section // 2


def body(
    token_ids,
    noise,
    loss_mask,
    time_index,
    seq_counts,
    table,
    proj,
    w_time,
    gain_attn,
    w_qkv,
    w_out,
    gain_mlp,
    w_up,
    w_down,
):
    sections = lax.axis_size("section")
    section = lax.axis_index("section")
    groups = lax.axis_size("dp")
    micro, shard = token_ids.shape
    seq_len = shard * sections
    tokens = micro * seq_len
    width = w_qkv.shape[1]
    hidden = w_up.shape[2]
    emb = table.shape[1]
    last = sections - 1
    count = seq_counts[lax.axis_index("dp")]
    count_all = jnp.sum(seq_counts).astype(F32)
    valid = (jnp.arange(micro) < count).astype(F32)
    low_first, high_first, mid_first = dp_orders(groups)
    gather_order = low_first[::-1]
    section_order = list(range(bits_of(sections)))

    own_rows, table_back = jax.vjp(rms_scale, table.astype(F32))
    own_low = own_rows.astype(BF)
    own_count = own_low.shape[0]
    rows_sec = gather(own_low, "dp", gather_order).reshape(groups * own_count, emb)
    vocab_sec = groups * own_count
    proj_sec = gather(proj, "dp", gather_order)
    proj_full = gather(proj_sec, "section", section_order).reshape(emb, width)
    both = gather(jnp.stack([token_ids, loss_mask]), "section", section_order)
    ids_blocks = both[:, 0].reshape(-1) - section * vocab_sec
    both_rows = jnp.transpose(both, (1, 2, 0, 3)).reshape(2, tokens)
    ids_rows = both_rows[0] - section * vocab_sec
    weight = both_rows[1].astype(F32) * jnp.repeat(valid, seq_len)
    onehot = (ids_blocks[:, None] == jnp.arange(vocab_sec)[None, :]).astype(BF)
    partial = dot(onehot, rows_sec).astype(BF).reshape(sections, micro * shard, emb)
    picked = scatter_sum(partial, "section", section_order[::-1])
    sigma = noise_level(time_index)
    shrink = lax.rsqrt(1.0 + sigma * sigma)
    inputs = (
        (picked.reshape(micro, shard, emb) + sigma[:, None, None] * noise) * shrink[:, None, None]
    ).astype(BF)
    inputs_all = gather(inputs, "section", section_order)
    inputs_all = jnp.transpose(inputs_all, (1, 0, 2, 3)).reshape(tokens, emb)
    entry = dot(inputs_all, proj_full).astype(BF).reshape(micro, seq_len, width)
    picked_all = gather(picked.astype(BF).reshape(micro, shard, emb), "section", section_order)
    picked_all = jnp.transpose(picked_all, (1, 0, 2, 3)).reshape(tokens, emb)
    time_low = time_features(sigma, emb).astype(BF)
    time_rows = dot(time_low, w_time[0])
    cosines, sines = rope_tables(seq_len, width // HEADS)
    weights = tuple(pltpu.with_memory_space_constraint(w[0], pltpu.VMEM) for w in (w_qkv, w_out, w_up, w_down))

    stores = blanks(store_shapes(micro, seq_len, width, hidden))
    offset = delay(section)
    ticks = micro + delay(last)
    infos = tick_infos(ticks, offset, micro, jnp.where(section == 0, 0, jnp.where(section % 2 == 1, 1, 2)))
    core_in = x_next = x_in = entry[0]
    tick_sums = []
    finals = []
    for tick in range(ticks):
        sent, sums, stores = layer_forward(
            tick, infos, core_in, x_in, entry, time_rows, gain_attn, gain_mlp, cosines, sines, *weights, stores
        )
        tick_sums.append(sums)
        if tick - delay(last) >= 0:
            finals.append(sent)
        going = [s for s in range(last) if 0 <= tick - delay(s) < micro]
        core_pairs = [(s, s + 1) for s in going if s % 2 == 0]
        x_pairs = [(s, s + 1) for s in going if s % 2 == 1]
        core_in = lax.ppermute(sent, "section", core_pairs) if core_pairs else sent
        x_in = x_next
        x_next = lax.ppermute(sent, "section", x_pairs) if x_pairs else sent

    final = jnp.concatenate(finals, axis=0).astype(F32)
    normalized, head_back = jax.vjp(rms_scale, final)
    feats = normalized.astype(BF)
    latent = (dot_nt(feats, proj_full).astype(BF).astype(F32) * LOGIT_SCALE).astype(BF)
    latent = spread(latent, "section", last)
    mean, stats = head_forward(rows_sec, latent)
    for bit in section_order:
        other_mean, other_stats = swap(mean, "section", bit), swap(stats, "section", bit)
        peak = jnp.maximum(stats[0], other_stats[0])
        mine_part = stats[1] * jnp.exp(stats[0] - peak)
        other_part = other_stats[1] * jnp.exp(other_stats[0] - peak)
        total = mine_part + other_part
        mean = (mean.astype(F32) * (mine_part / total) + other_mean.astype(F32) * (other_part / total))
        if bit != section_order[-1]:
            mean = mean.astype(BF)
        stats = jnp.stack([peak, total])
    log_total = stats[0] + jnp.log(stats[1])
    grad_latent = ((mean.T - picked_all.astype(F32)) * (weight * LOGIT_SCALE)[:, None]).astype(BF)
    grad_final = head_back(dot(grad_latent, proj_full))[0].astype(BF)
    exit_grad = grad_final.reshape(micro, seq_len, width)
    grad_proj = jnp.where(section == last, dot_tn(grad_latent, feats), 0.0)

    saved = [stores[0], stores[2], stores[3], stores[5], stores[7]]
    grads = blanks(grad_shapes(micro, seq_len, width, hidden))
    back_offset = delay(last) - offset
    infos = tick_infos(ticks, back_offset, micro, jnp.where(section == last, 0, jnp.where(section % 2 == 0, 1, 2)))
    core_in = x_next = x_in = exit_grad[0]
    tick_rows = []
    sums = jnp.sum(lax.dynamic_slice_in_dim(jnp.stack(tick_sums), offset, micro, 0), axis=2)
    square_sums = jnp.sum(sums * valid[:, None], axis=0)
    for tick in range(ticks):
        sent, rows, grads = layer_backward(
            tick, infos, core_in, x_in, exit_grad, time_rows, gain_attn, gain_mlp, cosines, sines, *weights, saved, grads
        )
        tick_rows.append(rows)
        if tick < bits_of(groups):
            square_sums = square_sums + after(swap(square_sums, "dp", tick), rows)
        going = [s for s in range(1, sections) if 0 <= tick - (delay(last) - delay(s)) < micro]
        core_pairs = [(s, s - 1) for s in going if s % 2 == 1]
        x_pairs = [(s, s - 1) for s in going if s % 2 == 0]
        core_in = lax.ppermute(sent, "section", core_pairs) if core_pairs else sent
        x_in = x_next
        x_next = lax.ppermute(sent, "section", x_pairs) if x_pairs else sent
    grad_out_all, grad_pre_all, grad_attn_all, grad_mixed_all, grad_first_all = (
        g.reshape(tokens, g.shape[2]) for g in grads
    )
    attn_in_all, context_all, mlp_in_all, activated_all = (
        stores[i].reshape(tokens, stores[i].shape[2]) for i in (1, 4, 6, 8)
    )

    out = Product(context_all, grad_attn_all, high_first)
    down = Product(activated_all, grad_out_all, low_first)
    up = Product(mlp_in_all, grad_pre_all, low_first)
    qkv = [Product(attn_in_all, grad_mixed_all, low_first, part, 2) for part in range(2)]
    token = down.send(square_sums)
    token = up.send(token)
    token = out.send(token)
    token = out.keep(token)
    token = qkv[0].send(token)
    token = qkv[1].send(token)
    token = qkv[0].keep(token)
    token = qkv[1].keep(token)
    token = up.keep(token)
    token = down.keep(token)
    token = out.step(None)
    token = out.step(None)
    token = down.step(token)

    grad_inputs = (dot_nt(grad_first_all, proj_full) + zero_of(token)).astype(BF)
    grad_inputs = spread(grad_inputs, "section", 0).astype(F32)
    row_terms = grad_inputs * jnp.repeat(shrink, seq_len)[:, None] - latent.astype(F32) * weight[:, None]
    grad_table = head_backward(
        rows_sec, latent, log_total[None, :], weight[None, :], ids_rows[None, :], row_terms.astype(BF), token
    )
    tab = Scatter(grad_table.reshape(groups, -1, emb), low_first)
    token = tab.send(token)
    token = down.step(token)
    grad_proj = grad_proj + jnp.where(section == 0, dot_tn(inputs_all, after(grad_first_all, token)), 0.0)
    proj_part = scatter_sum(grad_proj.astype(BF).reshape(sections, emb // sections, width), "section", section_order[::-1])
    rows = lax.dynamic_slice_in_dim(jnp.stack(tick_rows), back_offset, micro, 0)
    rows = after(rows, token)
    w_time_term = jnp.dot(time_low.astype(F32).T, rows[:, 2], precision=PRECISION_MAXIMAL)
    gain_rows = jnp.sum(rows[:, :2], axis=0)
    gain_rows = jnp.transpose(gain_rows.reshape(2, groups, width // groups), (1, 0, 2)).reshape(groups, 1, -1)
    at = [emb // groups, emb // sections // groups]
    pad = -sum(at) % 16 or 16
    gain_rows = jnp.pad(gain_rows, ((0, 0), (0, pad - 1), (0, width - gain_rows.shape[2])))
    packed = jnp.concatenate(
        [
            w_time_term.astype(BF).reshape(groups, -1, width),
            proj_part.astype(BF).reshape(groups, -1, width),
            gain_rows.astype(BF),
        ],
        axis=1,
    )
    pack = Scatter(packed, high_first)
    token = pack.send(token)
    token = up.step(token)
    token = down.end(token)
    token = pack.step(token)
    token = qkv[0].step(token)
    token = up.step(token)
    token = pack.step(token)
    token = qkv[1].step(token)
    token = qkv[0].step(token)
    token = tab.step(token)
    token = qkv[1].step(token)
    token = up.end(token)
    token = out.end(token)
    token = pack.end(token)
    token = qkv[0].end(token)
    token = tab.step(token)
    token = qkv[1].end(token)
    token = tab.end(token)
    target_logit = jnp.sum(latent.astype(F32) * picked_all.astype(F32), axis=1)
    token_loss = (log_total - target_logit) * weight
    seq_loss = jnp.sum(token_loss.reshape(micro, seq_len), axis=1) / seq_len
    layer_rms = jnp.sqrt(square_sums / (count_all * seq_len * width))[None, :]
    packed = pack.total
    w_out_grad = out.total
    w_down_grad = down.total
    w_up_grad = up.total
    w_qkv_grad = jnp.concatenate([qkv[0].total, qkv[1].total], axis=1)
    w_time_grad = packed[: at[0]]
    proj_grad = packed[at[0] : sum(at)]
    gains = packed[sum(at), : 2 * width // groups].reshape(2, width // groups)
    table_grad = table_back(tab.total)[0]
    grad_mine = lax.dynamic_slice_in_dim(
        grad_inputs.reshape(micro, seq_len, emb), section * shard, shard, 1
    )
    noise_grad = grad_mine * (sigma * shrink)[:, None, None]
    return (
        seq_loss,
        layer_rms,
        noise_grad,
        table_grad,
        proj_grad,
        w_time_grad[None],
        gains[0][None],
        w_qkv_grad[None],
        w_out_grad[None],
        gains[1][None],
        w_up_grad[None],
        w_down_grad[None],
    )


def solution(mesh):
    return jax.shard_map(
        body,
        mesh=mesh,
        in_specs=(
            P("dp", "section"),
            P("dp", "section", None),
            P("dp", "section"),
            P("dp"),
            P(),
            P(("section", "dp"), None),
            P(("section", "dp"), None),
            P("section", None, None),
            P("section", None),
            P("section", None, None),
            P("section", None, None),
            P("section", None),
            P("section", None, None),
            P("section", None, None),
        ),
        out_specs=(
            P("dp"),
            P("section", None),
            P("dp", "section", None),
            P(("section", "dp"), None),
            P(("section", "dp"), None),
            P("section", "dp", None),
            P("section", "dp"),
            P("section", "dp", None),
            P("section", "dp", None),
            P("section", "dp"),
            P("section", "dp", None),
            P("section", "dp", None),
        ),
        check_vma=False,
    )
```

```python
import functools, math
import jax
import jax.numpy as jnp
from jax import lax
from jax.experimental import pallas as pl
from jax.experimental.pallas import tpu as pltpu
from jax.sharding import PartitionSpec as P
HEADS=16
NOISE_LEVELS = 1000
LOGIT_SCALE = 0.0625
SIGMA_LOW_LOG = math.log(0.5)
SIGMA_HIGH_LOG = math.log(50.0)
TIME_ANGLE = 64.0
PRECISION_MAXIMAL = lax.Precision.HIGHEST
NORM_EPSILON=1e-6
SCORE_SCALE=0.125
DEPTH=3
F32=jnp.float32; BF=jnp.bfloat16
VMEM_LIMIT=26*1024*1024
HEAD_LIMIT=16*1024*1024
GELU_A=math.sqrt(2.0/math.pi); GELU_B=0.044715

def dot(a,b): return jnp.dot(a,b,preferred_element_type=F32)
def dot_nt(a,b): return lax.dot_general(a,b,(((1,),(1,)),((),())),preferred_element_type=F32)
def dot_tn(a,b): return lax.dot_general(a,b,(((0,),(0,)),((),())),preferred_element_type=F32)

def swap_halves(x,mask):
    return jnp.where(mask,pltpu.roll(x,96,1),pltpu.roll(x,32,1))

class Loads:
    def __init__(self,sem,ahead):
        self.sem,self.ahead,self.copies,self.next=sem,ahead,[],0
    def add(self,src,dst):
        k=len(self.copies); self.copies.append(pltpu.make_async_copy(src,dst,self.sem.at[k])); return k
    def fill(self,upto):
        while self.next<min(upto,len(self.copies)):
            self.copies[self.next].start(); self.next+=1
    def wait(self,k):
        self.fill(k+1)
        self.copies[k].wait()
        self.fill(k+1+self.ahead)
class Puts:
    def __init__(self,sem): self.sem,self.copies=sem,[]
    def add(self,src,dst):
        c=pltpu.make_async_copy(src,dst,self.sem.at[len(self.copies)]); c.start(); self.copies.append(c)
    def wait(self):
        for c in self.copies: c.wait()

def fwd_kernel(tick,info,hid_in,far_in,entry,time_rows,gain_attn,gain_mlp,cos,sin,w_qkv,w_out,w_up,w_down,
               s_hid,s_attn,s_qkv,s_prob,s_ctx,s_second,s_mlp,s_gp,s_act,
               o_next,o_sums,o_hid,o_attn,o_qkv,o_prob,o_ctx,o_second,o_mlp,o_gp,o_act,
               b_hid,b_attn,b_qkv,b_prob,b_ctx,b_second,b_low,b_mlp,b_gp,b_act,hsem,osem):
    active=info[tick,0]; slot=info[tick,1]; source=info[tick,2]
    width=b_hid.shape[1]; T=b_hid.shape[0]
    nw=w_up.shape[1]//width
    npair=width//128
    @pl.when(active==1)
    def _():
        src_copy=pltpu.make_async_copy(entry.at[slot],b_hid,hsem)
        @pl.when(source==0)
        def _(): src_copy.start()
        @pl.when(source==1)
        def _(): b_hid[...]=hid_in[...]
        @pl.when(source==2)
        def _(): pltpu.make_async_copy(far_in,b_hid,hsem).start()
        outs=Puts(osem)
        @pl.when(source!=1)
        def _(): src_copy.wait()
        outs.add(b_hid,o_hid.at[slot])
        first=b_hid[...].astype(F32)+time_rows[pl.ds(slot,1),:]
        r1=lax.rsqrt(jnp.mean(first*first,axis=1,keepdims=True)+NORM_EPSILON)
        b_attn[...]=(first*r1*gain_attn[...].astype(F32)).astype(BF)
        outs.add(b_attn,o_attn.at[slot])
        lane=lax.broadcasted_iota(jnp.int32,(T,128),1)
        low=(lane%64)<32
        head0=lane<64
        c_=cos[...]; s_=sin[...]
        a=b_attn[...]
        for i in range(3):
            m=dot(a,w_qkv[:,i*width:(i+1)*width])
            if i<2:
                for p in range(npair):
                    x=m[:,p*128:(p+1)*128]
                    b_qkv[:,i*width+p*128:i*width+(p+1)*128]=(x*c_+swap_halves(x,low)*s_).astype(BF)
            else:
                b_qkv[:,i*width:(i+1)*width]=m.astype(BF)
        outs.add(b_qkv,o_qkv.at[slot])
        for p in range(npair):
            q=b_qkv[:,p*128:(p+1)*128]; k=b_qkv[:,width+p*128:width+(p+1)*128]; v=b_qkv[:,2*width+p*128:2*width+(p+1)*128]
            z=jnp.zeros_like(q)
            qs=jnp.concatenate([jnp.where(head0,q,z),jnp.where(head0,z,q)],axis=0)
            s=dot_nt(qs,k)*SCORE_SCALE
            e=jnp.exp(s-jnp.max(s,axis=1,keepdims=True))
            pr=(e*(1.0/jnp.sum(e,axis=1,keepdims=True))).astype(BF)
            b_prob[p]=pr
            c=dot(pr,v)
            b_ctx[:,p*128:(p+1)*128]=jnp.where(head0,c[:T],c[T:]).astype(BF)
        outs.add(b_prob,o_prob.at[slot])
        outs.add(b_ctx,o_ctx.at[slot])
        ao=dot(b_ctx[...],w_out[...])
        second=b_hid[...].astype(F32)+time_rows[pl.ds(slot,1),:]+ao
        b_second[...]=second
        b_low[...]=second.astype(BF)
        outs.add(b_low,o_second.at[slot])
        sum_a=jnp.sum(ao*ao,axis=0,keepdims=True)
        r2=lax.rsqrt(jnp.mean(second*second,axis=1,keepdims=True)+NORM_EPSILON)
        b_mlp[...]=(second*r2*gain_mlp[...].astype(F32)).astype(BF)
        outs.add(b_mlp,o_mlp.at[slot])
        acc=None
        for i in range(nw):
            cols=pl.ds(i*width,width)
            u=dot(b_mlp[...],w_up[:,i*width:(i+1)*width])
            u2=u*u
            th=jnp.tanh(GELU_A*(u+GELU_B*u2*u))
            h=0.5*(1.0+th)
            act=(u*h).astype(BF)
            gp=h+0.5*u*(1.0-th*th)*(GELU_A*(1.0+3.0*GELU_B*u2))
            b_act[i]=act
            b_gp[i]=gp.astype(BF)
            outs.add(b_act.at[i],o_act.at[slot,:,cols])
            outs.add(b_gp.at[i],o_gp.at[slot,:,cols])
            d=dot(act,w_down[i*width:(i+1)*width,:])
            acc=d if acc is None else acc+d
        third=b_second[...]+acc
        o_next[...]=third.astype(BF)
        o_sums[...]=jnp.concatenate([jnp.sum(third*third,axis=0,keepdims=True),sum_a,jnp.sum(acc*acc,axis=0,keepdims=True)],axis=0)
        outs.wait()

def store_shapes(micro,T,width,hidden):
    npair=width//128
    B=lambda *s: jax.ShapeDtypeStruct((micro,)+s,BF)
    return [B(T,width),B(T,width),B(T,3*width),B(npair,2*T,T),B(T,width),B(T,width),B(T,width),B(T,hidden),B(T,hidden)]

ANY=pl.BlockSpec(memory_space=pl.ANY)
HB=pl.BlockSpec(memory_space=pltpu.HBM)
LAYER_LIMIT=22*1024*1024
VM=pl.BlockSpec(memory_space=pltpu.VMEM)
SM=pl.BlockSpec(memory_space=pltpu.SMEM)
def in_hbm(x): return pltpu.with_memory_space_constraint(x,pltpu.HBM)

def layer_forward(tick,info,hid,far,entry,time_rows,ga,gm,cos,sin,w_qkv,w_out,w_up,w_down,stores):
    T,width=hid.shape; hidden=w_up.shape[1]; micro=entry.shape[0]; nw=hidden//width; npair=width//128
    V=lambda *s: pltpu.VMEM(s,BF)
    scratch=[V(T,width),
             V(T,width),V(T,3*width),V(npair,2*T,T),V(T,width),pltpu.VMEM((T,width),F32),V(T,width),
             V(T,width),V(nw,T,width),V(nw,T,width),
             pltpu.SemaphoreType.DMA,pltpu.SemaphoreType.DMA((7+2*nw,))]
    out=pl.pallas_call(functools.partial(fwd_kernel,tick),
        in_specs=[SM,VM,HB,HB,VM,VM,VM,VM,VM,VM,VM,VM,VM]+[HB]*9,
        out_specs=[VM,VM]+[HB]*9,
        out_shape=[jax.ShapeDtypeStruct((T,width),BF),jax.ShapeDtypeStruct((3,width),F32)]+[pltpu.HBM(s.shape,s.dtype) for s in store_shapes(micro,T,width,hidden)],
        input_output_aliases={13+i:2+i for i in range(9)},
        scratch_shapes=scratch,
        compiler_params=pltpu.CompilerParams(vmem_limit_bytes=LAYER_LIMIT),
        cost_estimate=pl.CostEstimate(flops=2*T*width*(4*width+2*hidden),bytes_accessed=2*width*(4*width+2*hidden)+8*1024*1024,transcendentals=0),
        name="layer_fwd",
    )(info,hid,in_hbm(far),in_hbm(entry),time_rows,ga,gm,cos,sin,w_qkv,w_out,w_up,w_down,*map(in_hbm,stores))
    return out[0],out[1],out[2:]

def bwd_kernel(tick,info,g_in,far_in,exits,time_rows,gain_attn,gain_mlp,cos,sin,w_qkv,w_out,w_up,w_down,
               hid,qkv,prob,sec,gps,
               s_g,s_pre,s_gattn,s_mixed,s_first,
               o_next,o_vec,o_g,o_pre,o_gattn,o_mixed,o_first,
               b_g,b_hid,b_qkv,b_prob,b_sec,b_gp,b_pre,b_gattn,b_gctx,b_second,b_mixed,wsem,hsem,osem):
    active=info[tick,0]; slot=info[tick,1]; source=info[tick,2]
    width=b_hid.shape[1]; T=b_hid.shape[0]
    nw=w_up.shape[1]//width
    npair=width//128
    @pl.when(active==1)
    def _():
        src_copy=pltpu.make_async_copy(exits.at[slot],b_g,hsem)
        @pl.when(source==0)
        def _(): src_copy.start()
        @pl.when(source==1)
        def _(): b_g[...]=g_in[...]
        @pl.when(source==2)
        def _(): pltpu.make_async_copy(far_in,b_g,hsem).start()
        ld=Loads(wsem,DEPTH)
        kg=[]
        for i in range(nw):
            cols=pl.ds(i*width,width)
            kg.append(ld.add(gps.at[slot,:,cols],b_gp.at[i]))
        ks=ld.add(sec.at[slot],b_sec)
        kqkv=ld.add(qkv.at[slot],b_qkv)
        kp=ld.add(prob.at[slot],b_prob)
        kh=ld.add(hid.at[slot],b_hid)
        ld.fill(DEPTH)
        outs=Puts(osem)
        @pl.when(source!=1)
        def _(): src_copy.wait()
        outs.add(b_g,o_g.at[slot])
        g=b_g[...]
        acc=None
        for i in range(nw):
            ga=dot_nt(g,w_down[i*width:(i+1)*width,:])
            ld.wait(kg[i])
            pre=(ga*b_gp[i].astype(F32)).astype(BF)
            b_pre[i]=pre
            outs.add(b_pre.at[i],o_pre.at[slot,:,pl.ds(i*width,width)])
            d=dot_nt(pre,w_up[:,i*width:(i+1)*width])
            acc=d if acc is None else acc+d
        ld.wait(ks)
        second=b_sec[...].astype(F32)
        r2=lax.rsqrt(jnp.mean(second*second,axis=1,keepdims=True)+NORM_EPSILON)
        n2=second*r2
        gain_row=jnp.sum(acc*n2,axis=0,keepdims=True)
        gn=acc*gain_mlp[...].astype(F32)
        gs=b_g[...].astype(F32)+r2*(gn-n2*jnp.mean(gn*n2,axis=1,keepdims=True))
        b_second[...]=gs
        b_gattn[...]=gs.astype(BF)
        outs.add(b_gattn,o_gattn.at[slot])
        b_gctx[...]=dot_nt(b_gattn[...],w_out[...]).astype(BF)
        lane=lax.broadcasted_iota(jnp.int32,(T,128),1)
        low=(lane%64)<32
        head0=lane<64
        c_=cos[...]; s_=sin[...]
        ld.wait(kqkv); ld.wait(kp)
        for p in range(npair):
            sl=[slice(i*width+p*128,i*width+(p+1)*128) for i in range(3)]
            q=b_qkv[:,sl[0]]; k=b_qkv[:,sl[1]]; v=b_qkv[:,sl[2]]
            gc=b_gctx[:,p*128:(p+1)*128]
            z=jnp.zeros_like(q)
            qs=jnp.concatenate([jnp.where(head0,q,z),jnp.where(head0,z,q)],axis=0)
            gcs=jnp.concatenate([jnp.where(head0,gc,z),jnp.where(head0,z,gc)],axis=0)
            pl_=b_prob[p]
            b_mixed[:,sl[2]]=dot_tn(pl_,gcs).astype(BF)
            gp=dot_nt(gcs,v)
            pf=pl_.astype(F32)
            gsc=(pf*(gp-jnp.sum(gp*pf,axis=1,keepdims=True))).astype(BF)
            gq=dot(gsc,k)
            gq=jnp.where(head0,gq[:T],gq[T:])*SCORE_SCALE
            gk=dot_tn(gsc,qs)*SCORE_SCALE
            b_mixed[:,sl[0]]=(gq*c_-swap_halves(gq,low)*s_).astype(BF)
            b_mixed[:,sl[1]]=(gk*c_-swap_halves(gk,low)*s_).astype(BF)
        outs.add(b_mixed,o_mixed.at[slot])
        acc=None
        for i in range(3):
            d=dot_nt(b_mixed[:,i*width:(i+1)*width],w_qkv[:,i*width:(i+1)*width])
            acc=d if acc is None else acc+d
        ld.wait(kh)
        first=b_hid[...].astype(F32)+time_rows[pl.ds(slot,1),:]
        r1=lax.rsqrt(jnp.mean(first*first,axis=1,keepdims=True)+NORM_EPSILON)
        n1=first*r1
        attn_row=jnp.sum(acc*n1,axis=0,keepdims=True)
        gm=acc*gain_attn[...].astype(F32)
        gf=b_second[...]+r1*(gm-n1*jnp.mean(gm*n1,axis=1,keepdims=True))
        o_next[...]=gf.astype(BF)
        outs.add(o_next,o_first.at[slot])
        o_vec[...]=jnp.concatenate([attn_row,gain_row,jnp.sum(gf,axis=0,keepdims=True)],axis=0)
        outs.wait()

def grad_shapes(micro,T,width,hidden):
    B=lambda *s: jax.ShapeDtypeStruct((micro,)+s,BF)
    return [B(T,width),B(T,hidden),B(T,width),B(T,3*width),B(T,width)]

def layer_backward(tick,info,g,far,exits,time_rows,ga,gm,cos,sin,w_qkv,w_out,w_up,w_down,saved,stores):
    T,width=g.shape; hidden=w_up.shape[1]; micro=exits.shape[0]; nw=hidden//width; npair=width//128
    V=lambda *s: pltpu.VMEM(s,BF)
    scratch=[V(T,width),
             V(T,width),V(T,3*width),V(npair,2*T,T),V(T,width),V(nw,T,width),V(nw,T,width),V(T,width),V(T,width),pltpu.VMEM((T,width),F32),V(T,3*width),
             pltpu.SemaphoreType.DMA((4+nw,)),pltpu.SemaphoreType.DMA,pltpu.SemaphoreType.DMA((4+nw,))]
    out=pl.pallas_call(functools.partial(bwd_kernel,tick),
        in_specs=[SM,VM,HB,HB,VM,VM,VM,VM,VM]+[VM]*4+[HB]*5+[HB]*5,
        out_specs=[VM,VM]+[HB]*5,
        out_shape=[jax.ShapeDtypeStruct((T,width),BF),jax.ShapeDtypeStruct((3,width),F32)]+[pltpu.HBM(s.shape,s.dtype) for s in grad_shapes(micro,T,width,hidden)],
        input_output_aliases={18+i:2+i for i in range(5)},
        scratch_shapes=scratch,
        compiler_params=pltpu.CompilerParams(vmem_limit_bytes=LAYER_LIMIT),
        cost_estimate=pl.CostEstimate(flops=2*T*width*(4*width+2*hidden),bytes_accessed=2*width*(4*width+2*hidden)+8*1024*1024,transcendentals=0),
        name="layer_bwd",
    )(info,g,in_hbm(far),in_hbm(exits),time_rows,ga,gm,cos,sin,w_qkv,w_out,w_up,w_down,*map(in_hbm,saved),*map(in_hbm,stores))
    return out[0],out[1],out[2:]

def rope_tables(T,head):
    half=head//2
    rates=jnp.exp(-math.log(10000.0)*jnp.arange(half,dtype=F32)/half)
    ang=jnp.arange(T,dtype=F32)[:,None]*rates[None,:]
    c=jnp.cos(ang); s=jnp.sin(ang)
    return jnp.concatenate([c,c,c,c],1),jnp.concatenate([-s,s,-s,s],1)


def rms_scale(values):
    return values * lax.rsqrt(jnp.mean(values * values, axis=-1, keepdims=True) + NORM_EPSILON)


def noise_level(time_index):
    fraction = time_index.astype(jnp.float32) / (NOISE_LEVELS - 1)
    return jnp.exp(SIGMA_LOW_LOG + (SIGMA_HIGH_LOG - SIGMA_LOW_LOG) * fraction)


def time_features(sigma, width):
    half = width // 2
    rates = jnp.exp(-math.log(10000.0) * jnp.arange(half, dtype=jnp.float32) / half)
    angles = jnp.log(sigma)[..., None] * TIME_ANGLE * rates
    return jnp.concatenate([jnp.cos(angles), jnp.sin(angles)], axis=-1)


def head_forward_kernel(table, latent, o_mean, o_stats, top, total, mixed):
    step = pl.program_id(0)

    @pl.when(step == 0)
    def _():
        top[...] = jnp.full_like(top, -jnp.inf)
        total[...] = jnp.zeros_like(total)
        mixed[...] = jnp.zeros_like(mixed)

    rows = table[...]
    logits = dot_nt(rows, latent[...])
    peak = jnp.maximum(top[...], jnp.max(logits, axis=0, keepdims=True))
    fade = jnp.exp(top[...] - peak)
    e = jnp.exp(logits - peak)
    total[...] = total[...] * fade + jnp.sum(e, axis=0, keepdims=True)
    mixed[...] = mixed[...] * fade + dot_tn(rows, e.astype(BF))
    top[...] = peak

    @pl.when(step == pl.num_programs(0) - 1)
    def _():
        o_mean[...] = (mixed[...] / total[...]).astype(BF)
        o_stats[...] = jnp.concatenate([top[...], total[...]], axis=0)


def vocab_tile(rows):
    for tile in (800, 500, 400):
        if rows % tile == 0 and tile % 16 == 0:
            return tile
    return rows


def head_forward(table, latent):
    rows, emb = table.shape
    tokens = latent.shape[0]
    tile = vocab_tile(rows)
    return pl.pallas_call(
        head_forward_kernel,
        grid=(rows // tile,),
        in_specs=[pl.BlockSpec((tile, emb), lambda i: (i, 0)), pl.BlockSpec((tokens, emb), lambda i: (0, 0))],
        out_specs=[pl.BlockSpec((emb, tokens), lambda i: (0, 0)), pl.BlockSpec((2, tokens), lambda i: (0, 0))],
        out_shape=[jax.ShapeDtypeStruct((emb, tokens), BF), jax.ShapeDtypeStruct((2, tokens), F32)],
        scratch_shapes=[pltpu.VMEM((1, tokens), F32), pltpu.VMEM((1, tokens), F32), pltpu.VMEM((emb, tokens), F32)],
        compiler_params=pltpu.CompilerParams(vmem_limit_bytes=HEAD_LIMIT),
        cost_estimate=pl.CostEstimate(flops=4 * rows * emb * tokens, bytes_accessed=2 * rows * emb, transcendentals=rows * tokens),
        name="head_fwd",
    )(table, latent)


def head_backward_kernel(table, latent, log_total, weight, ids, terms, token, o_grad):
    logits = dot_nt(table[...], latent[...])
    g = (jnp.exp(logits - log_total[...]) * weight[...]).astype(BF)
    rows = lax.broadcasted_iota(jnp.int32, g.shape, 0) + pl.program_id(0) * g.shape[0]
    picks = jnp.where(rows == ids[...], 1.0, 0.0).astype(BF)
    o_grad[...] = (dot(g, latent[...]) + dot(picks, terms[...])).astype(BF)


def head_backward(table, latent, log_total, weight, ids, terms, token):
    rows, emb = table.shape
    tokens = latent.shape[0]
    tile = vocab_tile(rows)
    return pl.pallas_call(
        head_backward_kernel,
        grid=(rows // tile,),
        in_specs=[
            pl.BlockSpec((tile, emb), lambda i: (i, 0)),
            pl.BlockSpec((tokens, emb), lambda i: (0, 0)),
            pl.BlockSpec((1, tokens), lambda i: (0, 0)),
            pl.BlockSpec((1, tokens), lambda i: (0, 0)),
            pl.BlockSpec((1, tokens), lambda i: (0, 0)),
            pl.BlockSpec((tokens, emb), lambda i: (0, 0)),
            ANY,
        ],
        out_specs=pl.BlockSpec((tile, emb), lambda i: (i, 0)),
        out_shape=jax.ShapeDtypeStruct((rows, emb), BF),
        compiler_params=pltpu.CompilerParams(vmem_limit_bytes=HEAD_LIMIT),
        cost_estimate=pl.CostEstimate(flops=1, bytes_accessed=1, transcendentals=0),
        name="head_bwd",
    )(table, latent, log_total, weight, ids, terms, token)


def blank_kernel(*refs):
    pass


def blanks(shapes):
    return pl.pallas_call(blank_kernel, out_specs=[HB] * len(shapes), out_shape=shapes, name="blanks")()


def bits_of(size):
    bits = size.bit_length() - 1
    if 1 << bits != size:
        raise ValueError("axis size")
    return bits


def dp_orders(size):
    bits = bits_of(size)
    low = bits // 2
    return (
        list(range(bits)),
        list(range(low, bits)) + list(range(low)),
        [low] + list(range(low)) + list(range(low + 1, bits)),
    )


def swap(x, axis, bit):
    pairs = [(i, i ^ (1 << bit)) for i in range(lax.axis_size(axis))]
    return lax.ppermute(x, axis, pairs)


def gather(x, axis, order):
    index = lax.axis_index(axis)
    held = []
    for bit in order:
        other = swap(x, axis, bit)
        at = sum(1 for b in held if b > bit)
        mine = (index >> bit) & 1
        x = jnp.where(mine == 0, jnp.stack([x, other], at), jnp.stack([other, x], at))
        held.append(bit)
    size = lax.axis_size(axis)
    return x.reshape((size,) + x.shape[len(order):])


def gather_rows(x, axis, order):
    rows = x.shape[0]
    piece = -(-rows // 4) // 16 * 16 + 16 if rows >= 512 else rows
    pieces = [x[i : min(i + piece, rows)] for i in range(0, rows, piece)]
    index = lax.axis_index(axis)
    held = []
    token = None
    for bit in order:
        at = sum(1 for b in held if b > bit)
        mine = (index >> bit) & 1
        for n, part in enumerate(pieces):
            other = swap(part, axis, bit)
            if token is not None:
                other = after(other, token)
            token = pieces[n] = jnp.where(mine == 0, jnp.stack([part, other], at), jnp.stack([other, part], at))
        held.append(bit)
    pieces = [p.reshape((-1,) + p.shape[len(order) :]) for p in pieces]
    return jnp.concatenate(pieces, axis=1)


def scatter_sum(x, axis, order):
    index = lax.axis_index(axis)
    bits = bits_of(lax.axis_size(axis))
    x = x.reshape((2,) * bits + x.shape[1:])
    left = list(range(bits - 1, -1, -1))
    for n, bit in enumerate(order):
        at = left.index(bit)
        mine = (index >> bit) & 1
        sent = lax.dynamic_index_in_dim(x, 1 - mine, at, keepdims=False)
        kept = lax.dynamic_index_in_dim(x, mine, at, keepdims=False)
        got = swap(sent, axis, bit)
        x = kept.astype(F32) + got.astype(F32)
        if n + 1 < len(order):
            x = x.astype(BF)
        left.remove(bit)
    return x


def zero_of(token):
    return jnp.minimum(jnp.abs(token[(0,) * token.ndim].astype(F32)), 0.0)


def after(x, token):
    return x + zero_of(token).astype(x.dtype)


class Scatter:
    def __init__(self, blocks, order):
        self.order = list(order)
        self.left = list(range(len(order) - 1, -1, -1))
        self.index = lax.axis_index("dp")
        self.terms = [blocks.reshape((2,) * len(order) + blocks.shape[1:])]

    def _side(self, side, at):
        parts = [lax.dynamic_index_in_dim(t, side, at, keepdims=False).astype(F32) for t in self.terms]
        return sum(parts[1:], parts[0])

    def send(self, token):
        bit = self.order.pop(0)
        at = self.left.index(bit)
        self.left.remove(bit)
        mine = (self.index >> bit) & 1
        sent = (self._side(1 - mine, at) + (0.0 if token is None else zero_of(token))).astype(BF)
        self.got = lax.ppermute(sent, "dp", [(i, i ^ (1 << bit)) for i in range(lax.axis_size("dp"))])
        self.terms = [lax.dynamic_index_in_dim(t, mine, at, keepdims=False) for t in self.terms]
        return sent

    def step(self, token):
        self.terms.append(self.got)
        return self.send(token)

    def end(self, token):
        while self.order:
            token = self.step(token)
        parts = [t.astype(F32) for t in self.terms + [self.got]]
        self.total = sum(parts[1:], parts[0]) + zero_of(token)
        return self.total


def product_kernel(ids, *refs):
    left, (right, token, out, mark) = refs[:-4], refs[-4:]
    a = jnp.concatenate([r[...] for r in left], axis=1)
    out[...] = dot_tn(a, right[...]).astype(BF)
    mark[...] = jnp.zeros_like(mark)


def product(left, right, ids, block, part, parts, token):
    rows, columns = left.shape[0], right.shape[1] // parts
    count = ids.shape[0]
    tile = 512 if columns % 512 == 0 else columns
    first = part * columns // tile

    def pick(j):
        return pl.BlockSpec((rows, block), lambda i, ids: (0, ids[j]))

    return pl.pallas_call(
        product_kernel,
        grid_spec=pltpu.PrefetchScalarGridSpec(
            num_scalar_prefetch=1,
            grid=(columns // tile,),
            in_specs=[pick(j) for j in range(count)] + [pl.BlockSpec((rows, tile), lambda i, ids: (0, first + i)), ANY],
            out_specs=[
                pl.BlockSpec((count * block, tile), lambda i, ids: (0, i)),
                pl.BlockSpec((8, 128), lambda i, ids: (0, 0)),
            ],
        ),
        out_shape=[
            jax.ShapeDtypeStruct((count * block, columns), BF),
            jax.ShapeDtypeStruct((8, 128), F32),
        ],
        compiler_params=pltpu.CompilerParams(vmem_limit_bytes=VMEM_LIMIT),
        cost_estimate=pl.CostEstimate(flops=1, bytes_accessed=1, transcendentals=0),
        name="product",
    )(ids, *[left] * count, right, token)


class Product(Scatter):
    def __init__(self, left, right, order, part=0, parts=1):
        self.order = list(order)
        self.bits = len(order)
        self.left = list(range(self.bits - 1, -1, -1))
        self.index = lax.axis_index("dp")
        self.a, self.g = left, right
        self.part, self.parts = part, parts

    def _half(self, side, token):
        rows = self.a.shape[1]
        block = rows >> self.bits
        ids = jnp.array([i for i in range(1 << self.bits) if not (i >> self.bit) & 1], jnp.int32)
        ids = ids + side.astype(jnp.int32) * (1 << self.bit)
        if block % 128 == 0:
            x, mark = product(self.a, self.g, ids, block, self.part, self.parts, token)
        else:
            a = jnp.take(self.a.reshape(self.a.shape[0], -1, block), ids, axis=1).reshape(self.a.shape[0], -1)
            wide = self.g.shape[1] // self.parts
            x = dot_tn(after(a, token), self.g[:, self.part * wide : (self.part + 1) * wide]).astype(BF)
            mark = x
        return x.reshape((2,) * (self.bits - 1) + (block, x.shape[1])), mark

    def send(self, token):
        if len(self.order) == self.bits:
            self.bit = bit = self.order.pop(0)
            self.left.remove(bit)
            self.mine = (self.index >> bit) & 1
            sent, mark = self._half(1 - self.mine, token)
            self.got = lax.ppermute(sent, "dp", [(i, i ^ (1 << bit)) for i in range(lax.axis_size("dp"))])
            return mark
        return super().send(token)

    def keep(self, token):
        kept, mark = self._half(self.mine, token)
        self.terms = [kept]
        return mark


def tick_infos(ticks, offset, micro, source):
    slot = jnp.arange(ticks) - offset
    active = (slot >= 0) & (slot < micro)
    return jnp.stack(
        [active.astype(jnp.int32), jnp.clip(slot, 0, micro - 1), jnp.full((ticks,), source, jnp.int32)], axis=1
    ).astype(jnp.int32)


def sum_all(x, axis):
    for bit in range(bits_of(lax.axis_size(axis))):
        x = x + swap(x, axis, bit)
    return x


def spread(x, axis, root):
    index = lax.axis_index(axis)
    holders = [root]
    for bit in range(bits_of(lax.axis_size(axis))):
        pairs = [(h, h ^ (1 << bit)) for h in holders]
        got = lax.ppermute(x, axis, pairs)
        fresh = [b for a, b in pairs]
        new = jnp.zeros((), jnp.bool_)
        for f in fresh:
            new = new | (index == f)
        x = jnp.where(new, got, x)
        holders = holders + fresh
    return x


def delay(section):
    return section + section // 2


def body(
    token_ids,
    noise,
    loss_mask,
    time_index,
    seq_counts,
    table,
    proj,
    w_time,
    gain_attn,
    w_qkv,
    w_out,
    gain_mlp,
    w_up,
    w_down,
):
    sections = lax.axis_size("section")
    section = lax.axis_index("section")
    groups = lax.axis_size("dp")
    micro, shard = token_ids.shape
    seq_len = shard * sections
    tokens = micro * seq_len
    width = w_qkv.shape[1]
    hidden = w_up.shape[2]
    emb = table.shape[1]
    last = sections - 1
    count = seq_counts[lax.axis_index("dp")]
    valid = (jnp.arange(micro) < count).astype(F32)
    low_first, high_first, mid_first = dp_orders(groups)
    gather_order = low_first[::-1]
    section_order = list(range(bits_of(sections)))

    own_rows, table_back = jax.vjp(rms_scale, table.astype(F32))
    own_low = own_rows.astype(BF)
    own_count = own_low.shape[0]
    bundle = gather_rows(jnp.concatenate([own_low, proj.reshape(-1, emb)]), "dp", gather_order)
    rows_sec = bundle[:, :own_count].reshape(groups * own_count, emb)
    proj_sec = bundle[:, own_count:].reshape(groups * proj.shape[0], width)
    vocab_sec = groups * own_count
    proj_full = gather(proj_sec, "section", section_order).reshape(emb, width)
    both = gather(jnp.stack([token_ids, loss_mask]), "section", section_order)
    both_rows = jnp.transpose(both, (1, 2, 0, 3)).reshape(2, tokens)
    noise_all = gather(noise, "section", section_order)
    noise_all = jnp.transpose(noise_all, (1, 0, 2, 3)).reshape(micro, seq_len, emb)
    ids_rows = both_rows[0] - section * vocab_sec
    weight = both_rows[1].astype(F32) * jnp.repeat(valid, seq_len)
    onehot = (ids_rows[:, None] == jnp.arange(vocab_sec)[None, :]).astype(BF)
    picked_all = sum_all(dot(onehot, rows_sec).astype(BF), "section")
    sigma = noise_level(time_index)
    shrink = lax.rsqrt(1.0 + sigma * sigma)
    inputs_all = (
        (picked_all.astype(F32).reshape(micro, seq_len, emb) + sigma[:, None, None] * noise_all) * shrink[:, None, None]
    ).astype(BF).reshape(tokens, emb)
    entry = dot(inputs_all, proj_full).astype(BF).reshape(micro, seq_len, width)
    time_low = time_features(sigma, emb).astype(BF)
    time_rows = dot(time_low, w_time[0]) + zero_of(weight)
    cosines, sines = rope_tables(seq_len, width // HEADS)
    weights = tuple(pltpu.with_memory_space_constraint(w[0], pltpu.VMEM) for w in (w_qkv, w_out, w_up, w_down))

    stores = blanks(store_shapes(micro, seq_len, width, hidden))
    offset = delay(section)
    ticks = micro + delay(last)
    infos = tick_infos(ticks, offset, micro, jnp.where(section == 0, 0, jnp.where(section % 2 == 1, 1, 2)))
    core_in = x_next = x_in = entry[0]
    tick_sums = []
    finals = []
    for tick in range(ticks):
        sent, sums, stores = layer_forward(
            tick, infos, core_in, x_in, entry, time_rows, gain_attn, gain_mlp, cosines, sines, *weights, stores
        )
        tick_sums.append(sums)
        if tick - delay(last) >= 0:
            finals.append(sent)
        going = [s for s in range(last) if 0 <= tick - delay(s) < micro]
        core_pairs = [(s, s + 1) for s in going if s % 2 == 0]
        x_pairs = [(s, s + 1) for s in going if s % 2 == 1]
        core_in = lax.ppermute(sent, "section", core_pairs) if core_pairs else sent
        x_in = x_next
        x_next = lax.ppermute(sent, "section", x_pairs) if x_pairs else sent

    final = jnp.concatenate(finals, axis=0).astype(F32)
    normalized, head_back = jax.vjp(rms_scale, final)
    feats = normalized.astype(BF)
    latent = (dot_nt(feats, proj_full).astype(BF).astype(F32) * LOGIT_SCALE).astype(BF)
    latent = spread(latent, "section", last)
    mean, stats = head_forward(rows_sec, latent)
    for bit in section_order:
        other_mean, other_stats = swap(mean, "section", bit), swap(stats, "section", bit)
        peak = jnp.maximum(stats[0], other_stats[0])
        mine_part = stats[1] * jnp.exp(stats[0] - peak)
        other_part = other_stats[1] * jnp.exp(other_stats[0] - peak)
        total = mine_part + other_part
        mean = (mean.astype(F32) * (mine_part / total) + other_mean.astype(F32) * (other_part / total))
        if bit != section_order[-1]:
            mean = mean.astype(BF)
        stats = jnp.stack([peak, total])
    log_total = stats[0] + jnp.log(stats[1])
    grad_latent = ((mean.T - picked_all.astype(F32)) * (weight * LOGIT_SCALE)[:, None]).astype(BF)
    grad_final = head_back(dot(grad_latent, proj_full))[0].astype(BF)
    exit_grad = grad_final.reshape(micro, seq_len, width)
    grad_proj = jnp.where(section == last, dot_tn(grad_latent, feats), 0.0)

    saved = [stores[0], stores[2], stores[3], stores[5], stores[7]]
    grads = blanks(grad_shapes(micro, seq_len, width, hidden))
    back_offset = delay(last) - offset
    infos = tick_infos(ticks, back_offset, micro, jnp.where(section == last, 0, jnp.where(section % 2 == 0, 1, 2)))
    core_in = x_next = x_in = exit_grad[0]
    tick_rows = []
    sums = jnp.sum(lax.dynamic_slice_in_dim(jnp.stack(tick_sums), offset, micro, 0), axis=2)
    square_sums = jnp.sum(sums * valid[:, None], axis=0)
    for tick in range(ticks):
        sent, rows, grads = layer_backward(
            tick, infos, core_in, x_in, exit_grad, time_rows, gain_attn, gain_mlp, cosines, sines, *weights, saved, grads
        )
        tick_rows.append(rows)
        if tick < bits_of(groups):
            square_sums = square_sums + after(swap(square_sums, "dp", tick), rows)
        going = [s for s in range(1, sections) if 0 <= tick - (delay(last) - delay(s)) < micro]
        core_pairs = [(s, s - 1) for s in going if s % 2 == 1]
        x_pairs = [(s, s - 1) for s in going if s % 2 == 0]
        core_in = lax.ppermute(sent, "section", core_pairs) if core_pairs else sent
        x_in = x_next
        x_next = lax.ppermute(sent, "section", x_pairs) if x_pairs else sent
    grad_out_all, grad_pre_all, grad_attn_all, grad_mixed_all, grad_first_all = (
        g.reshape(tokens, g.shape[2]) for g in grads
    )
    attn_in_all, context_all, mlp_in_all, activated_all = (
        stores[i].reshape(tokens, stores[i].shape[2]) for i in (1, 4, 6, 8)
    )

    out = Product(context_all, grad_attn_all, high_first)
    down = Product(activated_all, grad_out_all, low_first)
    up = Product(mlp_in_all, grad_pre_all, low_first)
    qkv = [Product(attn_in_all, grad_mixed_all, low_first, part, 2) for part in range(2)]
    token = down.send(square_sums)
    token = up.send(token)
    token = out.send(token)
    token = out.keep(token)
    token = qkv[0].send(token)
    token = qkv[1].send(token)
    token = qkv[0].keep(token)
    token = qkv[1].keep(token)
    token = up.keep(token)
    token = down.keep(token)
    token = out.step(None)
    token = out.step(None)
    token = down.step(token)

    grad_inputs = (dot_nt(grad_first_all, proj_full) + zero_of(token)).astype(BF)
    grad_inputs = spread(grad_inputs, "section", 0).astype(F32)
    row_terms = grad_inputs * jnp.repeat(shrink, seq_len)[:, None] - latent.astype(F32) * weight[:, None]
    grad_table = head_backward(
        rows_sec, latent, log_total[None, :], weight[None, :], ids_rows[None, :], row_terms.astype(BF), token
    )
    tab = Scatter(grad_table.reshape(groups, -1, emb), low_first)
    token = tab.send(token)
    token = down.step(token)
    grad_proj = grad_proj + jnp.where(section == 0, dot_tn(inputs_all, after(grad_first_all, token)), 0.0)
    proj_part = scatter_sum(grad_proj.astype(BF).reshape(sections, emb // sections, width), "section", section_order[::-1])
    rows = lax.dynamic_slice_in_dim(jnp.stack(tick_rows), back_offset, micro, 0)
    rows = after(rows, token)
    w_time_term = jnp.dot(time_low.astype(F32).T, rows[:, 2], precision=PRECISION_MAXIMAL)
    gain_rows = jnp.sum(rows[:, :2], axis=0)
    gain_rows = jnp.transpose(gain_rows.reshape(2, groups, width // groups), (1, 0, 2)).reshape(groups, 1, -1)
    at = [emb // groups, emb // sections // groups]
    pad = -sum(at) % 16 or 16
    gain_rows = jnp.pad(gain_rows, ((0, 0), (0, pad - 1), (0, width - gain_rows.shape[2])))
    packed = jnp.concatenate(
        [
            w_time_term.astype(BF).reshape(groups, -1, width),
            proj_part.astype(BF).reshape(groups, -1, width),
            gain_rows.astype(BF),
        ],
        axis=1,
    )
    pack = Scatter(packed, high_first)
    token = pack.send(token)
    token = up.step(token)
    token = down.end(token)
    token = pack.step(token)
    token = qkv[0].step(token)
    token = up.step(token)
    token = pack.step(token)
    token = qkv[1].step(token)
    token = qkv[0].step(token)
    token = tab.step(token)
    token = qkv[1].step(token)
    token = up.end(token)
    token = out.end(token)
    token = pack.end(token)
    token = qkv[0].end(token)
    token = tab.step(token)
    token = qkv[1].end(token)
    token = tab.end(token)
    target_logit = jnp.sum(latent.astype(F32) * picked_all.astype(F32), axis=1)
    token_loss = (log_total - target_logit) * weight
    seq_loss = jnp.sum(token_loss.reshape(micro, seq_len), axis=1) / seq_len
    count_all = jnp.sum(after(seq_counts.astype(F32), token))
    layer_rms = jnp.sqrt(square_sums / (count_all * seq_len * width))[None, :]
    packed = pack.total
    w_out_grad = out.total
    w_down_grad = down.total
    w_up_grad = up.total
    w_qkv_grad = jnp.concatenate([qkv[0].total, qkv[1].total], axis=1)
    w_time_grad = packed[: at[0]]
    proj_grad = packed[at[0] : sum(at)]
    gains = packed[sum(at), : 2 * width // groups].reshape(2, width // groups)
    table_grad = table_back(tab.total)[0]
    grad_mine = lax.dynamic_slice_in_dim(
        grad_inputs.reshape(micro, seq_len, emb), section * shard, shard, 1
    )
    noise_grad = grad_mine * (sigma * shrink)[:, None, None]
    return (
        seq_loss,
        layer_rms,
        noise_grad,
        table_grad,
        proj_grad,
        w_time_grad[None],
        gains[0][None],
        w_qkv_grad[None],
        w_out_grad[None],
        gains[1][None],
        w_up_grad[None],
        w_down_grad[None],
    )


def solution(mesh):
    return jax.shard_map(
        body,
        mesh=mesh,
        in_specs=(
            P("dp", "section"),
            P("dp", "section", None),
            P("dp", "section"),
            P("dp"),
            P(),
            P(("section", "dp"), None),
            P(("section", "dp"), None),
            P("section", None, None),
            P("section", None),
            P("section", None, None),
            P("section", None, None),
            P("section", None),
            P("section", None, None),
            P("section", None, None),
        ),
        out_specs=(
            P("dp"),
            P("section", None),
            P("dp", "section", None),
            P(("section", "dp"), None),
            P(("section", "dp"), None),
            P("section", "dp", None),
            P("section", "dp"),
            P("section", "dp", None),
            P("section", "dp", None),
            P("section", "dp"),
            P("section", "dp", None),
            P("section", "dp", None),
        ),
        check_vma=False,
    )
```

```python
import functools, math
import jax
import jax.numpy as jnp
from jax import lax
from jax.experimental import pallas as pl
from jax.experimental.pallas import tpu as pltpu
from jax.sharding import PartitionSpec as P
HEADS=16
NOISE_LEVELS = 1000
LOGIT_SCALE = 0.0625
SIGMA_LOW_LOG = math.log(0.5)
SIGMA_HIGH_LOG = math.log(50.0)
TIME_ANGLE = 64.0
PRECISION_MAXIMAL = lax.Precision.HIGHEST
NORM_EPSILON=1e-6
SCORE_SCALE=0.125
DEPTH=3
F32=jnp.float32; BF=jnp.bfloat16
VMEM_LIMIT=26*1024*1024
HEAD_LIMIT=16*1024*1024
GELU_A=math.sqrt(2.0/math.pi); GELU_B=0.044715

def dot(a,b): return jnp.dot(a,b,preferred_element_type=F32)
def dot_nt(a,b): return lax.dot_general(a,b,(((1,),(1,)),((),())),preferred_element_type=F32)
def dot_tn(a,b): return lax.dot_general(a,b,(((0,),(0,)),((),())),preferred_element_type=F32)

def swap_halves(x,mask):
    return jnp.where(mask,pltpu.roll(x,96,1),pltpu.roll(x,32,1))

class Loads:
    def __init__(self,sem,ahead):
        self.sem,self.ahead,self.copies,self.next=sem,ahead,[],0
    def add(self,src,dst):
        k=len(self.copies); self.copies.append(pltpu.make_async_copy(src,dst,self.sem.at[k])); return k
    def fill(self,upto):
        while self.next<min(upto,len(self.copies)):
            self.copies[self.next].start(); self.next+=1
    def wait(self,k):
        self.fill(k+1)
        self.copies[k].wait()
        self.fill(k+1+self.ahead)
class Puts:
    def __init__(self,sem): self.sem,self.copies=sem,[]
    def add(self,src,dst):
        c=pltpu.make_async_copy(src,dst,self.sem.at[len(self.copies)]); c.start(); self.copies.append(c)
    def wait(self):
        for c in self.copies: c.wait()

def fwd_kernel(tick,info,hid_in,far_in,entry,time_rows,gain_attn,gain_mlp,cos,sin,w_qkv,w_out,w_up,w_down,
               s_hid,s_attn,s_qkv,s_prob,s_ctx,s_second,s_mlp,s_gp,s_act,
               o_next,o_sums,o_hid,o_attn,o_qkv,o_prob,o_ctx,o_second,o_mlp,o_gp,o_act,
               b_hid,b_attn,b_qkv,b_prob,b_ctx,b_second,b_low,b_mlp,b_gp,b_act,hsem,osem):
    active=info[tick,0]; slot=info[tick,1]; source=info[tick,2]
    width=b_hid.shape[1]; T=b_hid.shape[0]
    nw=w_up.shape[1]//width
    npair=width//128
    @pl.when(active==1)
    def _():
        src_copy=pltpu.make_async_copy(entry.at[slot],b_hid,hsem)
        @pl.when(source==0)
        def _(): src_copy.start()
        @pl.when(source==1)
        def _(): b_hid[...]=hid_in[...]
        @pl.when(source==2)
        def _(): pltpu.make_async_copy(far_in,b_hid,hsem).start()
        outs=Puts(osem)
        @pl.when(source!=1)
        def _(): src_copy.wait()
        outs.add(b_hid,o_hid.at[slot])
        first=b_hid[...].astype(F32)+time_rows[pl.ds(slot,1),:]
        r1=lax.rsqrt(jnp.mean(first*first,axis=1,keepdims=True)+NORM_EPSILON)
        b_attn[...]=(first*r1*gain_attn[...].astype(F32)).astype(BF)
        outs.add(b_attn,o_attn.at[slot])
        lane=lax.broadcasted_iota(jnp.int32,(T,128),1)
        low=(lane%64)<32
        head0=lane<64
        c_=cos[...]; s_=sin[...]
        a=b_attn[...]
        for i in range(3):
            m=dot(a,w_qkv[:,i*width:(i+1)*width])
            if i<2:
                for p in range(npair):
                    x=m[:,p*128:(p+1)*128]
                    b_qkv[:,i*width+p*128:i*width+(p+1)*128]=(x*c_+swap_halves(x,low)*s_).astype(BF)
            else:
                b_qkv[:,i*width:(i+1)*width]=m.astype(BF)
        outs.add(b_qkv,o_qkv.at[slot])
        for p in range(npair):
            q=b_qkv[:,p*128:(p+1)*128]; k=b_qkv[:,width+p*128:width+(p+1)*128]; v=b_qkv[:,2*width+p*128:2*width+(p+1)*128]
            z=jnp.zeros_like(q)
            qs=jnp.concatenate([jnp.where(head0,q,z),jnp.where(head0,z,q)],axis=0)
            s=dot_nt(qs,k)*SCORE_SCALE
            e=jnp.exp(s-jnp.max(s,axis=1,keepdims=True))
            pr=(e*(1.0/jnp.sum(e,axis=1,keepdims=True))).astype(BF)
            b_prob[p]=pr
            c=dot(pr,v)
            b_ctx[:,p*128:(p+1)*128]=jnp.where(head0,c[:T],c[T:]).astype(BF)
        outs.add(b_prob,o_prob.at[slot])
        outs.add(b_ctx,o_ctx.at[slot])
        ao=dot(b_ctx[...],w_out[...])
        second=b_hid[...].astype(F32)+time_rows[pl.ds(slot,1),:]+ao
        b_second[...]=second
        b_low[...]=second.astype(BF)
        outs.add(b_low,o_second.at[slot])
        sum_a=jnp.sum(ao*ao,axis=0,keepdims=True)
        r2=lax.rsqrt(jnp.mean(second*second,axis=1,keepdims=True)+NORM_EPSILON)
        b_mlp[...]=(second*r2*gain_mlp[...].astype(F32)).astype(BF)
        outs.add(b_mlp,o_mlp.at[slot])
        acc=None
        for i in range(nw):
            cols=pl.ds(i*width,width)
            u=dot(b_mlp[...],w_up[:,i*width:(i+1)*width])
            u2=u*u
            th=jnp.tanh(GELU_A*(u+GELU_B*u2*u))
            h=0.5*(1.0+th)
            act=(u*h).astype(BF)
            gp=h+0.5*u*(1.0-th*th)*(GELU_A*(1.0+3.0*GELU_B*u2))
            b_act[i]=act
            b_gp[i]=gp.astype(BF)
            outs.add(b_act.at[i],o_act.at[slot,:,cols])
            outs.add(b_gp.at[i],o_gp.at[slot,:,cols])
            d=dot(act,w_down[i*width:(i+1)*width,:])
            acc=d if acc is None else acc+d
        third=b_second[...]+acc
        o_next[...]=third.astype(BF)
        o_sums[...]=jnp.concatenate([jnp.sum(third*third,axis=0,keepdims=True),sum_a,jnp.sum(acc*acc,axis=0,keepdims=True)],axis=0)
        outs.wait()

def store_shapes(micro,T,width,hidden):
    npair=width//128
    B=lambda *s: jax.ShapeDtypeStruct((micro,)+s,BF)
    return [B(T,width),B(T,width),B(T,3*width),B(npair,2*T,T),B(T,width),B(T,width),B(T,width),B(T,hidden),B(T,hidden)]

ANY=pl.BlockSpec(memory_space=pl.ANY)
HB=pl.BlockSpec(memory_space=pltpu.HBM)
LAYER_LIMIT=22*1024*1024
VM=pl.BlockSpec(memory_space=pltpu.VMEM)
SM=pl.BlockSpec(memory_space=pltpu.SMEM)
def in_hbm(x): return pltpu.with_memory_space_constraint(x,pltpu.HBM)

def layer_forward(tick,info,hid,far,entry,time_rows,ga,gm,cos,sin,w_qkv,w_out,w_up,w_down,stores):
    T,width=hid.shape; hidden=w_up.shape[1]; micro=entry.shape[0]; nw=hidden//width; npair=width//128
    V=lambda *s: pltpu.VMEM(s,BF)
    scratch=[V(T,width),
             V(T,width),V(T,3*width),V(npair,2*T,T),V(T,width),pltpu.VMEM((T,width),F32),V(T,width),
             V(T,width),V(nw,T,width),V(nw,T,width),
             pltpu.SemaphoreType.DMA,pltpu.SemaphoreType.DMA((7+2*nw,))]
    out=pl.pallas_call(functools.partial(fwd_kernel,tick),
        in_specs=[SM,VM,HB,HB,VM,VM,VM,VM,VM,VM,VM,VM,VM]+[HB]*9,
        out_specs=[VM,VM]+[HB]*9,
        out_shape=[jax.ShapeDtypeStruct((T,width),BF),jax.ShapeDtypeStruct((3,width),F32)]+[pltpu.HBM(s.shape,s.dtype) for s in store_shapes(micro,T,width,hidden)],
        input_output_aliases={13+i:2+i for i in range(9)},
        scratch_shapes=scratch,
        compiler_params=pltpu.CompilerParams(vmem_limit_bytes=LAYER_LIMIT),
        cost_estimate=pl.CostEstimate(flops=2*T*width*(4*width+2*hidden),bytes_accessed=2*width*(4*width+2*hidden)+8*1024*1024,transcendentals=0),
        name="layer_fwd",
    )(info,hid,in_hbm(far),in_hbm(entry),time_rows,ga,gm,cos,sin,w_qkv,w_out,w_up,w_down,*map(in_hbm,stores))
    return out[0],out[1],out[2:]

def bwd_kernel(tick,info,g_in,far_in,exits,time_rows,gain_attn,gain_mlp,cos,sin,w_qkv,w_out,w_up,w_down,
               hid,qkv,prob,sec,gps,
               s_g,s_pre,s_gattn,s_mixed,s_first,
               o_next,o_vec,o_g,o_pre,o_gattn,o_mixed,o_first,
               b_g,b_hid,b_qkv,b_prob,b_sec,b_gp,b_pre,b_gattn,b_gctx,b_second,b_mixed,wsem,hsem,osem):
    active=info[tick,0]; slot=info[tick,1]; source=info[tick,2]
    width=b_hid.shape[1]; T=b_hid.shape[0]
    nw=w_up.shape[1]//width
    npair=width//128
    @pl.when(active==1)
    def _():
        src_copy=pltpu.make_async_copy(exits.at[slot],b_g,hsem)
        @pl.when(source==0)
        def _(): src_copy.start()
        @pl.when(source==1)
        def _(): b_g[...]=g_in[...]
        @pl.when(source==2)
        def _(): pltpu.make_async_copy(far_in,b_g,hsem).start()
        ld=Loads(wsem,DEPTH)
        kg=[]
        for i in range(nw):
            cols=pl.ds(i*width,width)
            kg.append(ld.add(gps.at[slot,:,cols],b_gp.at[i]))
        ks=ld.add(sec.at[slot],b_sec)
        kqkv=ld.add(qkv.at[slot],b_qkv)
        kp=ld.add(prob.at[slot],b_prob)
        kh=ld.add(hid.at[slot],b_hid)
        ld.fill(DEPTH)
        outs=Puts(osem)
        @pl.when(source!=1)
        def _(): src_copy.wait()
        outs.add(b_g,o_g.at[slot])
        g=b_g[...]
        acc=None
        for i in range(nw):
            ga=dot_nt(g,w_down[i*width:(i+1)*width,:])
            ld.wait(kg[i])
            pre=(ga*b_gp[i].astype(F32)).astype(BF)
            b_pre[i]=pre
            outs.add(b_pre.at[i],o_pre.at[slot,:,pl.ds(i*width,width)])
            d=dot_nt(pre,w_up[:,i*width:(i+1)*width])
            acc=d if acc is None else acc+d
        ld.wait(ks)
        second=b_sec[...].astype(F32)
        r2=lax.rsqrt(jnp.mean(second*second,axis=1,keepdims=True)+NORM_EPSILON)
        n2=second*r2
        gain_row=jnp.sum(acc*n2,axis=0,keepdims=True)
        gn=acc*gain_mlp[...].astype(F32)
        gs=b_g[...].astype(F32)+r2*(gn-n2*jnp.mean(gn*n2,axis=1,keepdims=True))
        b_second[...]=gs
        b_gattn[...]=gs.astype(BF)
        outs.add(b_gattn,o_gattn.at[slot])
        b_gctx[...]=dot_nt(b_gattn[...],w_out[...]).astype(BF)
        lane=lax.broadcasted_iota(jnp.int32,(T,128),1)
        low=(lane%64)<32
        head0=lane<64
        c_=cos[...]; s_=sin[...]
        ld.wait(kqkv); ld.wait(kp)
        for p in range(npair):
            sl=[slice(i*width+p*128,i*width+(p+1)*128) for i in range(3)]
            q=b_qkv[:,sl[0]]; k=b_qkv[:,sl[1]]; v=b_qkv[:,sl[2]]
            gc=b_gctx[:,p*128:(p+1)*128]
            z=jnp.zeros_like(q)
            qs=jnp.concatenate([jnp.where(head0,q,z),jnp.where(head0,z,q)],axis=0)
            gcs=jnp.concatenate([jnp.where(head0,gc,z),jnp.where(head0,z,gc)],axis=0)
            pl_=b_prob[p]
            b_mixed[:,sl[2]]=dot_tn(pl_,gcs).astype(BF)
            gp=dot_nt(gcs,v)
            pf=pl_.astype(F32)
            gsc=(pf*(gp-jnp.sum(gp*pf,axis=1,keepdims=True))).astype(BF)
            gq=dot(gsc,k)
            gq=jnp.where(head0,gq[:T],gq[T:])*SCORE_SCALE
            gk=dot_tn(gsc,qs)*SCORE_SCALE
            b_mixed[:,sl[0]]=(gq*c_-swap_halves(gq,low)*s_).astype(BF)
            b_mixed[:,sl[1]]=(gk*c_-swap_halves(gk,low)*s_).astype(BF)
        outs.add(b_mixed,o_mixed.at[slot])
        acc=None
        for i in range(3):
            d=dot_nt(b_mixed[:,i*width:(i+1)*width],w_qkv[:,i*width:(i+1)*width])
            acc=d if acc is None else acc+d
        ld.wait(kh)
        first=b_hid[...].astype(F32)+time_rows[pl.ds(slot,1),:]
        r1=lax.rsqrt(jnp.mean(first*first,axis=1,keepdims=True)+NORM_EPSILON)
        n1=first*r1
        attn_row=jnp.sum(acc*n1,axis=0,keepdims=True)
        gm=acc*gain_attn[...].astype(F32)
        gf=b_second[...]+r1*(gm-n1*jnp.mean(gm*n1,axis=1,keepdims=True))
        o_next[...]=gf.astype(BF)
        outs.add(o_next,o_first.at[slot])
        o_vec[...]=jnp.concatenate([attn_row,gain_row,jnp.sum(gf,axis=0,keepdims=True)],axis=0)
        outs.wait()

def grad_shapes(micro,T,width,hidden):
    B=lambda *s: jax.ShapeDtypeStruct((micro,)+s,BF)
    return [B(T,width),B(T,hidden),B(T,width),B(T,3*width),B(T,width)]

def layer_backward(tick,info,g,far,exits,time_rows,ga,gm,cos,sin,w_qkv,w_out,w_up,w_down,saved,stores):
    T,width=g.shape; hidden=w_up.shape[1]; micro=exits.shape[0]; nw=hidden//width; npair=width//128
    V=lambda *s: pltpu.VMEM(s,BF)
    scratch=[V(T,width),
             V(T,width),V(T,3*width),V(npair,2*T,T),V(T,width),V(nw,T,width),V(nw,T,width),V(T,width),V(T,width),pltpu.VMEM((T,width),F32),V(T,3*width),
             pltpu.SemaphoreType.DMA((4+nw,)),pltpu.SemaphoreType.DMA,pltpu.SemaphoreType.DMA((4+nw,))]
    out=pl.pallas_call(functools.partial(bwd_kernel,tick),
        in_specs=[SM,VM,HB,HB,VM,VM,VM,VM,VM]+[VM]*4+[HB]*5+[HB]*5,
        out_specs=[VM,VM]+[HB]*5,
        out_shape=[jax.ShapeDtypeStruct((T,width),BF),jax.ShapeDtypeStruct((3,width),F32)]+[pltpu.HBM(s.shape,s.dtype) for s in grad_shapes(micro,T,width,hidden)],
        input_output_aliases={18+i:2+i for i in range(5)},
        scratch_shapes=scratch,
        compiler_params=pltpu.CompilerParams(vmem_limit_bytes=LAYER_LIMIT),
        cost_estimate=pl.CostEstimate(flops=2*T*width*(4*width+2*hidden),bytes_accessed=2*width*(4*width+2*hidden)+8*1024*1024,transcendentals=0),
        name="layer_bwd",
    )(info,g,in_hbm(far),in_hbm(exits),time_rows,ga,gm,cos,sin,w_qkv,w_out,w_up,w_down,*map(in_hbm,saved),*map(in_hbm,stores))
    return out[0],out[1],out[2:]

def rope_tables(T,head):
    half=head//2
    rates=jnp.exp(-math.log(10000.0)*jnp.arange(half,dtype=F32)/half)
    ang=jnp.arange(T,dtype=F32)[:,None]*rates[None,:]
    c=jnp.cos(ang); s=jnp.sin(ang)
    return jnp.concatenate([c,c,c,c],1),jnp.concatenate([-s,s,-s,s],1)


def rms_scale(values):
    return values * lax.rsqrt(jnp.mean(values * values, axis=-1, keepdims=True) + NORM_EPSILON)


def noise_level(time_index):
    fraction = time_index.astype(jnp.float32) / (NOISE_LEVELS - 1)
    return jnp.exp(SIGMA_LOW_LOG + (SIGMA_HIGH_LOG - SIGMA_LOW_LOG) * fraction)


def time_features(sigma, width):
    half = width // 2
    rates = jnp.exp(-math.log(10000.0) * jnp.arange(half, dtype=jnp.float32) / half)
    angles = jnp.log(sigma)[..., None] * TIME_ANGLE * rates
    return jnp.concatenate([jnp.cos(angles), jnp.sin(angles)], axis=-1)


def head_forward_kernel(table, latent, o_mean, o_stats, top, total, mixed):
    step = pl.program_id(0)

    @pl.when(step == 0)
    def _():
        top[...] = jnp.full_like(top, -jnp.inf)
        total[...] = jnp.zeros_like(total)
        mixed[...] = jnp.zeros_like(mixed)

    rows = table[...]
    logits = dot_nt(rows, latent[...])
    peak = jnp.maximum(top[...], jnp.max(logits, axis=0, keepdims=True))
    fade = jnp.exp(top[...] - peak)
    e = jnp.exp(logits - peak)
    total[...] = total[...] * fade + jnp.sum(e, axis=0, keepdims=True)
    mixed[...] = mixed[...] * fade + dot_tn(rows, e.astype(BF))
    top[...] = peak

    @pl.when(step == pl.num_programs(0) - 1)
    def _():
        o_mean[...] = (mixed[...] / total[...]).astype(BF)
        o_stats[...] = jnp.concatenate([top[...], total[...]], axis=0)


def vocab_tile(rows):
    for tile in (800, 500, 400):
        if rows % tile == 0 and tile % 16 == 0:
            return tile
    return rows


def head_forward(table, latent):
    rows, emb = table.shape
    tokens = latent.shape[0]
    tile = vocab_tile(rows)
    return pl.pallas_call(
        head_forward_kernel,
        grid=(rows // tile,),
        in_specs=[pl.BlockSpec((tile, emb), lambda i: (i, 0)), pl.BlockSpec((tokens, emb), lambda i: (0, 0))],
        out_specs=[pl.BlockSpec((emb, tokens), lambda i: (0, 0)), pl.BlockSpec((2, tokens), lambda i: (0, 0))],
        out_shape=[jax.ShapeDtypeStruct((emb, tokens), BF), jax.ShapeDtypeStruct((2, tokens), F32)],
        scratch_shapes=[pltpu.VMEM((1, tokens), F32), pltpu.VMEM((1, tokens), F32), pltpu.VMEM((emb, tokens), F32)],
        compiler_params=pltpu.CompilerParams(vmem_limit_bytes=HEAD_LIMIT),
        cost_estimate=pl.CostEstimate(flops=4 * rows * emb * tokens, bytes_accessed=2 * rows * emb, transcendentals=rows * tokens),
        name="head_fwd",
    )(table, latent)


def head_backward_kernel(table, latent, log_total, weight, ids, terms, token, o_grad):
    logits = dot_nt(table[...], latent[...])
    g = (jnp.exp(logits - log_total[...]) * weight[...]).astype(BF)
    rows = lax.broadcasted_iota(jnp.int32, g.shape, 0) + pl.program_id(0) * g.shape[0]
    picks = jnp.where(rows == ids[...], 1.0, 0.0).astype(BF)
    o_grad[...] = (dot(g, latent[...]) + dot(picks, terms[...])).astype(BF)


def head_backward(table, latent, log_total, weight, ids, terms, token):
    rows, emb = table.shape
    tokens = latent.shape[0]
    tile = vocab_tile(rows)
    return pl.pallas_call(
        head_backward_kernel,
        grid=(rows // tile,),
        in_specs=[
            pl.BlockSpec((tile, emb), lambda i: (i, 0)),
            pl.BlockSpec((tokens, emb), lambda i: (0, 0)),
            pl.BlockSpec((1, tokens), lambda i: (0, 0)),
            pl.BlockSpec((1, tokens), lambda i: (0, 0)),
            pl.BlockSpec((1, tokens), lambda i: (0, 0)),
            pl.BlockSpec((tokens, emb), lambda i: (0, 0)),
            ANY,
        ],
        out_specs=pl.BlockSpec((tile, emb), lambda i: (i, 0)),
        out_shape=jax.ShapeDtypeStruct((rows, emb), BF),
        compiler_params=pltpu.CompilerParams(vmem_limit_bytes=HEAD_LIMIT),
        cost_estimate=pl.CostEstimate(flops=1, bytes_accessed=1, transcendentals=0),
        name="head_bwd",
    )(table, latent, log_total, weight, ids, terms, token)


def blank_kernel(*refs):
    pass


def blanks(shapes):
    return pl.pallas_call(blank_kernel, out_specs=[HB] * len(shapes), out_shape=shapes, name="blanks")()


def bits_of(size):
    bits = size.bit_length() - 1
    if 1 << bits != size:
        raise ValueError("axis size")
    return bits


def dp_orders(size):
    bits = bits_of(size)
    low = bits // 2
    return (
        list(range(bits)),
        list(range(low, bits)) + list(range(low)),
        [low] + list(range(low)) + list(range(low + 1, bits)),
    )


def swap(x, axis, bit):
    pairs = [(i, i ^ (1 << bit)) for i in range(lax.axis_size(axis))]
    return lax.ppermute(x, axis, pairs)


def gather(x, axis, order):
    index = lax.axis_index(axis)
    held = []
    for bit in order:
        other = swap(x, axis, bit)
        at = sum(1 for b in held if b > bit)
        mine = (index >> bit) & 1
        x = jnp.where(mine == 0, jnp.stack([x, other], at), jnp.stack([other, x], at))
        held.append(bit)
    size = lax.axis_size(axis)
    return x.reshape((size,) + x.shape[len(order):])


def gather_rows(x, axis, order):
    rows = x.shape[0]
    piece = -(-rows // 4) // 16 * 16 + 16 if rows >= 512 else rows
    pieces = [x[i : min(i + piece, rows)] for i in range(0, rows, piece)]
    index = lax.axis_index(axis)
    held = []
    token = None
    for bit in order:
        at = sum(1 for b in held if b > bit)
        mine = (index >> bit) & 1
        for n, part in enumerate(pieces):
            other = swap(part, axis, bit)
            if token is not None:
                other = after(other, token)
            token = pieces[n] = jnp.where(mine == 0, jnp.stack([part, other], at), jnp.stack([other, part], at))
        held.append(bit)
    pieces = [p.reshape((-1,) + p.shape[len(order) :]) for p in pieces]
    return jnp.concatenate(pieces, axis=1)


def scatter_sum(x, axis, order):
    index = lax.axis_index(axis)
    bits = bits_of(lax.axis_size(axis))
    x = x.reshape((2,) * bits + x.shape[1:])
    left = list(range(bits - 1, -1, -1))
    for n, bit in enumerate(order):
        at = left.index(bit)
        mine = (index >> bit) & 1
        sent = lax.dynamic_index_in_dim(x, 1 - mine, at, keepdims=False)
        kept = lax.dynamic_index_in_dim(x, mine, at, keepdims=False)
        got = swap(sent, axis, bit)
        x = kept.astype(F32) + got.astype(F32)
        if n + 1 < len(order):
            x = x.astype(BF)
        left.remove(bit)
    return x


def zero_of(token):
    return jnp.minimum(jnp.abs(token[(0,) * token.ndim].astype(F32)), 0.0)


def after(x, token):
    return x + zero_of(token).astype(x.dtype)


class Scatter:
    def __init__(self, blocks, order, index):
        self.order = list(order)
        self.left = list(range(len(order) - 1, -1, -1))
        self.index = index
        self.terms = [blocks.reshape((2,) * len(order) + blocks.shape[1:])]

    def _side(self, side, at):
        parts = [lax.dynamic_index_in_dim(t, side, at, keepdims=False).astype(F32) for t in self.terms]
        return sum(parts[1:], parts[0])

    def send(self, token):
        bit = self.order.pop(0)
        at = self.left.index(bit)
        self.left.remove(bit)
        mine = (self.index >> bit) & 1
        sent = (self._side(1 - mine, at) + (0.0 if token is None else zero_of(token))).astype(BF)
        self.got = lax.ppermute(sent, "dp", [(i, i ^ (1 << bit)) for i in range(lax.axis_size("dp"))])
        self.terms = [lax.dynamic_index_in_dim(t, mine, at, keepdims=False) for t in self.terms]
        return sent

    def step(self, token):
        self.terms.append(self.got)
        return self.send(token)

    def end(self, token):
        while self.order:
            token = self.step(token)
        parts = [t.astype(F32) for t in self.terms + [self.got]]
        self.total = sum(parts[1:], parts[0]) + zero_of(token)
        return self.total


def product_kernel(ids, *refs):
    left, (right, token, out, mark) = refs[:-4], refs[-4:]
    a = jnp.concatenate([r[...] for r in left], axis=1)
    out[...] = dot_tn(a, right[...]).astype(BF)
    mark[...] = jnp.zeros_like(mark)


def product(left, right, ids, row, count, block, part, parts, token):
    rows, columns = left.shape[0], right.shape[1] // parts
    tile = 512 if columns % 512 == 0 else columns
    first = part * columns // tile

    def pick(j):
        return pl.BlockSpec((rows, block), lambda i, ids: (0, ids[row, j]))

    return pl.pallas_call(
        product_kernel,
        grid_spec=pltpu.PrefetchScalarGridSpec(
            num_scalar_prefetch=1,
            grid=(columns // tile,),
            in_specs=[pick(j) for j in range(count)] + [pl.BlockSpec((rows, tile), lambda i, ids: (0, first + i)), ANY],
            out_specs=[
                pl.BlockSpec((count * block, tile), lambda i, ids: (0, i)),
                pl.BlockSpec((8, 128), lambda i, ids: (0, 0)),
            ],
        ),
        out_shape=[
            jax.ShapeDtypeStruct((count * block, columns), BF),
            jax.ShapeDtypeStruct((8, 128), F32),
        ],
        compiler_params=pltpu.CompilerParams(vmem_limit_bytes=VMEM_LIMIT),
        cost_estimate=pl.CostEstimate(flops=1, bytes_accessed=1, transcendentals=0),
        name="product",
    )(ids, *[left] * count, right, token)


class Product(Scatter):
    def __init__(self, left, right, order, index, table, first_row, part=0, parts=1):
        self.table, self.first_row = table, first_row
        self.order = list(order)
        self.bits = len(order)
        self.left = list(range(self.bits - 1, -1, -1))
        self.index = index
        self.a, self.g = left, right
        self.part, self.parts = part, parts

    def _half(self, stays, token):
        rows = self.a.shape[1]
        block = rows >> self.bits
        count = 1 << (self.bits - 1)
        row = self.first_row + 2 * self.bit + stays
        if block % 128 == 0:
            x, mark = product(self.a, self.g, self.table, row, count, block, self.part, self.parts, token)
        else:
            ids = self.table[row, :count]
            a = jnp.take(self.a.reshape(self.a.shape[0], -1, block), ids, axis=1).reshape(self.a.shape[0], -1)
            wide = self.g.shape[1] // self.parts
            x = dot_tn(after(a, token), self.g[:, self.part * wide : (self.part + 1) * wide]).astype(BF)
            mark = x
        return x.reshape((2,) * (self.bits - 1) + (block, x.shape[1])), mark

    def send(self, token):
        if len(self.order) == self.bits:
            self.bit = bit = self.order.pop(0)
            self.left.remove(bit)
            self.mine = (self.index >> bit) & 1
            sent, mark = self._half(0, token)
            self.got = lax.ppermute(sent, "dp", [(i, i ^ (1 << bit)) for i in range(lax.axis_size("dp"))])
            return mark
        return super().send(token)

    def keep(self, token):
        kept, mark = self._half(1, token)
        self.terms = [kept]
        return mark


def tick_infos(ticks, offset, micro, source):
    slot = jnp.arange(ticks) - offset
    active = (slot >= 0) & (slot < micro)
    return jnp.stack(
        [active.astype(jnp.int32), jnp.clip(slot, 0, micro - 1), jnp.full((ticks,), source, jnp.int32)], axis=1
    ).astype(jnp.int32)


def with_halves(infos, groups):
    bits = bits_of(groups)
    index = lax.axis_index("dp")
    rows = []
    for bit in range(bits):
        base = jnp.array([i for i in range(groups) if not (i >> bit) & 1], jnp.int32)
        mine = ((index >> bit) & 1).astype(jnp.int32)
        rows += [base + ((1 - mine) << bit), base + (mine << bit)]
    rows = jnp.stack(rows)
    wide = max(infos.shape[1], rows.shape[1])
    infos = jnp.pad(infos, ((0, 0), (0, wide - infos.shape[1])))
    rows = jnp.pad(rows, ((0, 0), (0, wide - rows.shape[1])))
    return jnp.concatenate([infos, rows])


def sum_all(x, axis):
    for bit in range(bits_of(lax.axis_size(axis))):
        x = x + swap(x, axis, bit)
    return x


def spread(x, axis, root):
    index = lax.axis_index(axis)
    holders = [root]
    for bit in range(bits_of(lax.axis_size(axis))):
        pairs = [(h, h ^ (1 << bit)) for h in holders]
        got = lax.ppermute(x, axis, pairs)
        fresh = [b for a, b in pairs]
        new = jnp.zeros((), jnp.bool_)
        for f in fresh:
            new = new | (index == f)
        x = jnp.where(new, got, x)
        holders = holders + fresh
    return x


def delay(section):
    return section + section // 2


def body(
    token_ids,
    noise,
    loss_mask,
    time_index,
    seq_counts,
    table,
    proj,
    w_time,
    gain_attn,
    w_qkv,
    w_out,
    gain_mlp,
    w_up,
    w_down,
):
    sections = lax.axis_size("section")
    section = lax.axis_index("section")
    groups = lax.axis_size("dp")
    micro, shard = token_ids.shape
    seq_len = shard * sections
    tokens = micro * seq_len
    width = w_qkv.shape[1]
    hidden = w_up.shape[2]
    emb = table.shape[1]
    last = sections - 1
    count = seq_counts[lax.axis_index("dp")]
    valid = (jnp.arange(micro) < count).astype(F32)
    low_first, high_first, mid_first = dp_orders(groups)
    gather_order = low_first[::-1]
    section_order = list(range(bits_of(sections)))

    own_rows, table_back = jax.vjp(rms_scale, table.astype(F32))
    own_low = own_rows.astype(BF)
    own_count = own_low.shape[0]
    bundle = gather_rows(jnp.concatenate([own_low, proj.reshape(-1, emb)]), "dp", gather_order)
    rows_sec = bundle[:, :own_count].reshape(groups * own_count, emb)
    proj_sec = bundle[:, own_count:].reshape(groups * proj.shape[0], width)
    vocab_sec = groups * own_count
    proj_full = gather(proj_sec, "section", section_order).reshape(emb, width)
    both = gather(jnp.stack([token_ids, loss_mask]), "section", section_order)
    both_rows = jnp.transpose(both, (1, 2, 0, 3)).reshape(2, tokens)
    noise_all = gather(noise, "section", section_order)
    noise_all = jnp.transpose(noise_all, (1, 0, 2, 3)).reshape(micro, seq_len, emb)
    ids_rows = both_rows[0] - section * vocab_sec
    weight = both_rows[1].astype(F32) * jnp.repeat(valid, seq_len)
    weight, ids_rows = lax.optimization_barrier((weight, ids_rows))
    onehot = (ids_rows[:, None] == jnp.arange(vocab_sec)[None, :]).astype(BF)
    picked_all = sum_all(dot(onehot, rows_sec).astype(BF), "section")
    sigma = noise_level(time_index)
    shrink = lax.rsqrt(1.0 + sigma * sigma)
    inputs_all = (
        (picked_all.astype(F32).reshape(micro, seq_len, emb) + sigma[:, None, None] * noise_all) * shrink[:, None, None]
    ).astype(BF).reshape(tokens, emb)
    entry = dot(inputs_all, proj_full).astype(BF).reshape(micro, seq_len, width)
    time_low = time_features(sigma, emb).astype(BF)
    time_rows = dot(time_low, w_time[0]) + zero_of(weight)
    cosines, sines = rope_tables(seq_len, width // HEADS)
    weights = tuple(pltpu.with_memory_space_constraint(w[0], pltpu.VMEM) for w in (w_qkv, w_out, w_up, w_down))

    stores = blanks(store_shapes(micro, seq_len, width, hidden) + [jax.ShapeDtypeStruct((seq_len, width), BF)])
    stores, unused = stores[:-1], stores[-1]
    offset = delay(section)
    ticks = micro + delay(last)
    back_offset = delay(last) - offset
    ahead = tick_infos(ticks, offset, micro, jnp.where(section == 0, 0, jnp.where(section % 2 == 1, 1, 2)))
    back = tick_infos(ticks, back_offset, micro, jnp.where(section == last, 0, jnp.where(section % 2 == 0, 1, 2)))
    infos = lax.optimization_barrier(with_halves(jnp.concatenate([ahead, back]), groups))
    core_in = x_next = x_in = unused
    tick_sums = []
    finals = []
    for tick in range(ticks):
        sent, sums, stores = layer_forward(
            tick, infos, core_in, x_in, entry, time_rows, gain_attn, gain_mlp, cosines, sines, *weights, stores
        )
        tick_sums.append(sums)
        if tick - delay(last) >= 0:
            finals.append(sent)
        going = [s for s in range(last) if 0 <= tick - delay(s) < micro]
        core_pairs = [(s, s + 1) for s in going if s % 2 == 0]
        x_pairs = [(s, s + 1) for s in going if s % 2 == 1]
        core_in = lax.ppermute(sent, "section", core_pairs) if core_pairs else sent
        x_in = x_next
        x_next = lax.ppermute(sent, "section", x_pairs) if x_pairs else sent

    final = jnp.concatenate(finals, axis=0).astype(F32)
    normalized, head_back = jax.vjp(rms_scale, final)
    feats = normalized.astype(BF)
    latent = (dot_nt(feats, proj_full).astype(BF).astype(F32) * LOGIT_SCALE).astype(BF)
    latent = spread(latent, "section", last)
    mean, stats = head_forward(rows_sec, latent)
    for bit in section_order:
        other_mean, other_stats = swap(mean, "section", bit), swap(stats, "section", bit)
        peak = jnp.maximum(stats[0], other_stats[0])
        mine_part = stats[1] * jnp.exp(stats[0] - peak)
        other_part = other_stats[1] * jnp.exp(other_stats[0] - peak)
        total = mine_part + other_part
        mean = (mean.astype(F32) * (mine_part / total) + other_mean.astype(F32) * (other_part / total))
        if bit != section_order[-1]:
            mean = mean.astype(BF)
        stats = jnp.stack([peak, total])
    log_total = stats[0] + jnp.log(stats[1])
    grad_latent = ((mean.T - picked_all.astype(F32)) * (weight * LOGIT_SCALE)[:, None]).astype(BF)
    grad_final = head_back(dot(grad_latent, proj_full))[0].astype(BF)
    exit_grad = grad_final.reshape(micro, seq_len, width)
    grad_proj = jnp.where(section == last, dot_tn(grad_latent, feats), 0.0)

    saved = [stores[0], stores[2], stores[3], stores[5], stores[7]]
    grads = blanks(grad_shapes(micro, seq_len, width, hidden))
    core_in = x_next = x_in = unused
    tick_rows = []
    sums = jnp.sum(lax.dynamic_slice_in_dim(jnp.stack(tick_sums), offset, micro, 0), axis=2)
    square_sums = jnp.sum(sums * valid[:, None], axis=0)
    for tick in range(ticks):
        sent, rows, grads = layer_backward(
            ticks + tick, infos, core_in, x_in, exit_grad, time_rows, gain_attn, gain_mlp, cosines, sines, *weights, saved, grads
        )
        tick_rows.append(rows)
        going = [s for s in range(1, sections) if 0 <= tick - (delay(last) - delay(s)) < micro]
        core_pairs = [(s, s - 1) for s in going if s % 2 == 1]
        x_pairs = [(s, s - 1) for s in going if s % 2 == 0]
        core_in = lax.ppermute(sent, "section", core_pairs) if core_pairs else sent
        x_in = x_next
        x_next = lax.ppermute(sent, "section", x_pairs) if x_pairs else sent
    grad_out_all, grad_pre_all, grad_attn_all, grad_mixed_all, grad_first_all = (
        g.reshape(tokens, g.shape[2]) for g in grads
    )
    attn_in_all, context_all, mlp_in_all, activated_all = (
        stores[i].reshape(tokens, stores[i].shape[2]) for i in (1, 4, 6, 8)
    )

    dp_index = lax.axis_index("dp")
    out = Product(context_all, grad_attn_all, high_first, dp_index, infos, 2 * ticks)
    down = [Product(activated_all, grad_out_all, low_first, dp_index, infos, 2 * ticks, part, 2) for part in range(2)]
    up = [Product(mlp_in_all, grad_pre_all, low_first, dp_index, infos, 2 * ticks, part, 2) for part in range(2)]
    qkv = [Product(attn_in_all, grad_mixed_all, low_first, dp_index, infos, 2 * ticks, part, 2) for part in range(2)]
    token = down[0].send(grad_first_all)
    token = down[1].send(token)
    token = out.send(token)
    token = up[0].send(token)
    token = out.keep(token)
    token = down[1].keep(token)
    token = up[0].keep(token)
    token = down[0].keep(token)
    token = down[0].step(None)

    grad_inputs = (dot_nt(grad_first_all, proj_full) + zero_of(token)).astype(BF)
    grad_inputs = spread(grad_inputs, "section", 0).astype(F32)
    row_terms = grad_inputs * jnp.repeat(shrink, seq_len)[:, None] - latent.astype(F32) * weight[:, None]
    zero = zero_of(token)
    grad_table = head_backward(
        rows_sec,
        latent,
        log_total[None, :] + zero,
        (weight + zero)[None, :],
        (ids_rows + zero.astype(jnp.int32))[None, :],
        row_terms.astype(BF),
        token,
    )
    tab = Scatter(grad_table.reshape(groups, -1, emb), low_first, dp_index)
    token = tab.send(token)
    token = up[1].send(token)
    token = up[1].keep(token)
    token = down[1].step(token)
    token = down[0].step(token)
    token = out.step(token)
    for part in qkv:
        token = part.send(token)
        token = part.keep(token)
    token = up[0].step(token)
    token = down[1].step(token)
    token = down[0].end(token)
    token = out.step(token)
    grad_proj = grad_proj + jnp.where(section == 0, dot_tn(inputs_all, after(grad_first_all, token)), 0.0)
    proj_part = scatter_sum(grad_proj.astype(BF).reshape(sections, emb // sections, width), "section", section_order[::-1])
    rows = lax.dynamic_slice_in_dim(jnp.stack(tick_rows), back_offset, micro, 0)
    rows = after(rows, token)
    w_time_term = jnp.dot(time_low.astype(F32).T, rows[:, 2], precision=PRECISION_MAXIMAL)
    gain_rows = jnp.sum(rows[:, :2], axis=0)
    gain_rows = jnp.transpose(gain_rows.reshape(2, groups, width // groups), (1, 0, 2)).reshape(groups, 1, -1)
    at = [emb // groups, emb // sections // groups]
    pad = -sum(at) % 16 or 16
    gain_rows = jnp.pad(gain_rows, ((0, 0), (0, pad - 1), (0, width - gain_rows.shape[2])))
    packed = jnp.concatenate(
        [
            w_time_term.astype(BF).reshape(groups, -1, width),
            proj_part.astype(BF).reshape(groups, -1, width),
            gain_rows.astype(BF),
        ],
        axis=1,
    )
    pack = Scatter(packed, high_first, dp_index)
    token = pack.send(token)
    token = tab.step(token)
    token = up[0].step(token)
    token = down[1].end(token)
    token = pack.step(token)
    token = up[1].step(token)
    token = tab.step(token)
    token = up[0].end(token)
    token = pack.step(token)
    token = qkv[0].step(token)
    token = up[1].step(token)
    token = tab.end(token)
    token = qkv[1].step(token)
    token = qkv[0].step(token)
    token = up[1].end(token)
    square_sums = sum_all(after(square_sums, token), "dp")
    token = qkv[0].end(token)
    token = qkv[1].step(token)
    token = out.end(token)
    token = pack.end(token)
    token = qkv[1].end(token)
    target_logit = jnp.sum(latent.astype(F32) * picked_all.astype(F32), axis=1)
    token_loss = (log_total - target_logit) * weight
    seq_loss = jnp.sum(token_loss.reshape(micro, seq_len), axis=1) / seq_len
    count_all = jnp.sum(after(seq_counts.astype(F32), token))
    layer_rms = jnp.sqrt(square_sums / (count_all * seq_len * width))[None, :]
    packed = pack.total
    w_out_grad = out.total
    w_down_grad = jnp.concatenate([part.total for part in down], axis=1)
    w_up_grad = jnp.concatenate([part.total for part in up], axis=1)
    w_qkv_grad = jnp.concatenate([qkv[0].total, qkv[1].total], axis=1)
    w_time_grad = packed[: at[0]]
    proj_grad = packed[at[0] : sum(at)]
    gains = packed[sum(at), : 2 * width // groups].reshape(2, width // groups)
    table_grad = table_back(tab.total)[0]
    grad_mine = lax.dynamic_slice_in_dim(
        grad_inputs.reshape(micro, seq_len, emb), section * shard, shard, 1
    )
    noise_grad = grad_mine * (sigma * shrink)[:, None, None]
    return (
        seq_loss,
        layer_rms,
        noise_grad,
        table_grad,
        proj_grad,
        w_time_grad[None],
        gains[0][None],
        w_qkv_grad[None],
        w_out_grad[None],
        gains[1][None],
        w_up_grad[None],
        w_down_grad[None],
    )


def solution(mesh):
    return jax.shard_map(
        body,
        mesh=mesh,
        in_specs=(
            P("dp", "section"),
            P("dp", "section", None),
            P("dp", "section"),
            P("dp"),
            P(),
            P(("section", "dp"), None),
            P(("section", "dp"), None),
            P("section", None, None),
            P("section", None),
            P("section", None, None),
            P("section", None, None),
            P("section", None),
            P("section", None, None),
            P("section", None, None),
        ),
        out_specs=(
            P("dp"),
            P("section", None),
            P("dp", "section", None),
            P(("section", "dp"), None),
            P(("section", "dp"), None),
            P("section", "dp", None),
            P("section", "dp"),
            P("section", "dp", None),
            P("section", "dp", None),
            P("section", "dp"),
            P("section", "dp", None),
            P("section", "dp", None),
        ),
        check_vma=False,
    )
```

```python
import functools, math
import jax
import jax.numpy as jnp
from jax import lax
from jax.experimental import pallas as pl
from jax.experimental.pallas import tpu as pltpu
from jax.sharding import PartitionSpec as P
HEADS=16
NOISE_LEVELS = 1000
LOGIT_SCALE = 0.0625
SIGMA_LOW_LOG = math.log(0.5)
SIGMA_HIGH_LOG = math.log(50.0)
TIME_ANGLE = 64.0
PRECISION_MAXIMAL = lax.Precision.HIGHEST
NORM_EPSILON=1e-6
SCORE_SCALE=0.125
DEPTH=3
F32=jnp.float32; BF=jnp.bfloat16
VMEM_LIMIT=26*1024*1024
HEAD_LIMIT=20*1024*1024
GELU_A=math.sqrt(2.0/math.pi); GELU_B=0.044715

def dot(a,b): return jnp.dot(a,b,preferred_element_type=F32)
def dot_nt(a,b): return lax.dot_general(a,b,(((1,),(1,)),((),())),preferred_element_type=F32)
def dot_tn(a,b): return lax.dot_general(a,b,(((0,),(0,)),((),())),preferred_element_type=F32)

def swap_halves(x,mask):
    return jnp.where(mask,pltpu.roll(x,96,1),pltpu.roll(x,32,1))

class Loads:
    def __init__(self,sem,ahead):
        self.sem,self.ahead,self.copies,self.next=sem,ahead,[],0
    def add(self,src,dst):
        k=len(self.copies); self.copies.append(pltpu.make_async_copy(src,dst,self.sem.at[k])); return k
    def fill(self,upto):
        while self.next<min(upto,len(self.copies)):
            self.copies[self.next].start(); self.next+=1
    def wait(self,k):
        self.fill(k+1)
        self.copies[k].wait()
        self.fill(k+1+self.ahead)
class Puts:
    def __init__(self,sem): self.sem,self.copies=sem,[]
    def add(self,src,dst):
        c=pltpu.make_async_copy(src,dst,self.sem.at[len(self.copies)]); c.start(); self.copies.append(c)
    def wait(self):
        for c in self.copies: c.wait()

def fwd_kernel(tick,info,hid_in,far_in,entry,time_rows,gain_attn,gain_mlp,cos,sin,w_qkv,w_out,w_up,w_down,
               s_hid,s_attn,s_qkv,s_prob,s_ctx,s_second,s_mlp,s_gp,s_act,
               o_next,o_sums,o_hid,o_attn,o_qkv,o_prob,o_ctx,o_second,o_mlp,o_gp,o_act,
               b_hid,b_attn,b_qkv,b_prob,b_ctx,b_second,b_low,b_mlp,b_gp,b_act,hsem,osem):
    active=info[tick,0]; slot=info[tick,1]; source=info[tick,2]
    width=b_hid.shape[1]; T=b_hid.shape[0]
    nw=w_up.shape[1]//width
    npair=width//128
    @pl.when(active==1)
    def _():
        src_copy=pltpu.make_async_copy(entry.at[slot],b_hid,hsem)
        @pl.when(source==0)
        def _(): src_copy.start()
        @pl.when(source==1)
        def _(): b_hid[...]=hid_in[...]
        @pl.when(source==2)
        def _(): pltpu.make_async_copy(far_in,b_hid,hsem).start()
        outs=Puts(osem)
        @pl.when(source!=1)
        def _(): src_copy.wait()
        outs.add(b_hid,o_hid.at[slot])
        first=b_hid[...].astype(F32)+time_rows[pl.ds(slot,1),:]
        r1=lax.rsqrt(jnp.mean(first*first,axis=1,keepdims=True)+NORM_EPSILON)
        b_attn[...]=(first*r1*gain_attn[...].astype(F32)).astype(BF)
        outs.add(b_attn,o_attn.at[slot])
        lane=lax.broadcasted_iota(jnp.int32,(T,128),1)
        low=(lane%64)<32
        head0=lane<64
        c_=cos[...]; s_=sin[...]
        a=b_attn[...]
        for i in range(3):
            m=dot(a,w_qkv[:,i*width:(i+1)*width])
            if i<2:
                for p in range(npair):
                    x=m[:,p*128:(p+1)*128]
                    b_qkv[:,i*width+p*128:i*width+(p+1)*128]=(x*c_+swap_halves(x,low)*s_).astype(BF)
            else:
                b_qkv[:,i*width:(i+1)*width]=m.astype(BF)
        outs.add(b_qkv,o_qkv.at[slot])
        for p in range(npair):
            q=b_qkv[:,p*128:(p+1)*128]; k=b_qkv[:,width+p*128:width+(p+1)*128]; v=b_qkv[:,2*width+p*128:2*width+(p+1)*128]
            z=jnp.zeros_like(q)
            qs=jnp.concatenate([jnp.where(head0,q,z),jnp.where(head0,z,q)],axis=0)
            s=dot_nt(qs,k)*SCORE_SCALE
            e=jnp.exp(s-jnp.max(s,axis=1,keepdims=True))
            pr=(e*(1.0/jnp.sum(e,axis=1,keepdims=True))).astype(BF)
            b_prob[p]=pr
            c=dot(pr,v)
            b_ctx[:,p*128:(p+1)*128]=jnp.where(head0,c[:T],c[T:]).astype(BF)
        outs.add(b_prob,o_prob.at[slot])
        outs.add(b_ctx,o_ctx.at[slot])
        ao=dot(b_ctx[...],w_out[...])
        second=b_hid[...].astype(F32)+time_rows[pl.ds(slot,1),:]+ao
        b_second[...]=second
        b_low[...]=second.astype(BF)
        outs.add(b_low,o_second.at[slot])
        sum_a=jnp.sum(ao*ao,axis=0,keepdims=True)
        r2=lax.rsqrt(jnp.mean(second*second,axis=1,keepdims=True)+NORM_EPSILON)
        b_mlp[...]=(second*r2*gain_mlp[...].astype(F32)).astype(BF)
        outs.add(b_mlp,o_mlp.at[slot])
        acc=None
        for i in range(nw):
            cols=pl.ds(i*width,width)
            u=dot(b_mlp[...],w_up[:,i*width:(i+1)*width])
            u2=u*u
            th=jnp.tanh(GELU_A*(u+GELU_B*u2*u))
            h=0.5*(1.0+th)
            act=(u*h).astype(BF)
            gp=h+0.5*u*(1.0-th*th)*(GELU_A*(1.0+3.0*GELU_B*u2))
            b_act[i]=act
            b_gp[i]=gp.astype(BF)
            outs.add(b_act.at[i],o_act.at[slot,:,cols])
            outs.add(b_gp.at[i],o_gp.at[slot,:,cols])
            d=dot(act,w_down[i*width:(i+1)*width,:])
            acc=d if acc is None else acc+d
        third=b_second[...]+acc
        o_next[...]=third.astype(BF)
        o_sums[...]=jnp.concatenate([jnp.sum(third*third,axis=0,keepdims=True),sum_a,jnp.sum(acc*acc,axis=0,keepdims=True)],axis=0)
        outs.wait()

def store_shapes(micro,T,width,hidden):
    npair=width//128
    B=lambda *s: jax.ShapeDtypeStruct((micro,)+s,BF)
    return [B(T,width),B(T,width),B(T,3*width),B(npair,2*T,T),B(T,width),B(T,width),B(T,width),B(T,hidden),B(T,hidden)]

ANY=pl.BlockSpec(memory_space=pl.ANY)
HB=pl.BlockSpec(memory_space=pltpu.HBM)
LAYER_LIMIT=22*1024*1024
VM=pl.BlockSpec(memory_space=pltpu.VMEM)
SM=pl.BlockSpec(memory_space=pltpu.SMEM)
def in_hbm(x): return pltpu.with_memory_space_constraint(x,pltpu.HBM)

def layer_forward(tick,info,hid,far,entry,time_rows,ga,gm,cos,sin,w_qkv,w_out,w_up,w_down,stores):
    T,width=hid.shape; hidden=w_up.shape[1]; micro=entry.shape[0]; nw=hidden//width; npair=width//128
    V=lambda *s: pltpu.VMEM(s,BF)
    scratch=[V(T,width),
             V(T,width),V(T,3*width),V(npair,2*T,T),V(T,width),pltpu.VMEM((T,width),F32),V(T,width),
             V(T,width),V(nw,T,width),V(nw,T,width),
             pltpu.SemaphoreType.DMA,pltpu.SemaphoreType.DMA((7+2*nw,))]
    out=pl.pallas_call(functools.partial(fwd_kernel,tick),
        in_specs=[SM,VM,HB,HB,VM,VM,VM,VM,VM,VM,VM,VM,VM]+[HB]*9,
        out_specs=[VM,VM]+[HB]*9,
        out_shape=[jax.ShapeDtypeStruct((T,width),BF),jax.ShapeDtypeStruct((3,width),F32)]+[pltpu.HBM(s.shape,s.dtype) for s in store_shapes(micro,T,width,hidden)],
        input_output_aliases={13+i:2+i for i in range(9)},
        scratch_shapes=scratch,
        compiler_params=pltpu.CompilerParams(vmem_limit_bytes=LAYER_LIMIT),
        cost_estimate=pl.CostEstimate(flops=2*T*width*(4*width+2*hidden),bytes_accessed=2*width*(4*width+2*hidden)+8*1024*1024,transcendentals=0),
        name="layer_fwd",
    )(info,hid,in_hbm(far),in_hbm(entry),time_rows,ga,gm,cos,sin,w_qkv,w_out,w_up,w_down,*map(in_hbm,stores))
    return out[0],out[1],out[2:]

def bwd_kernel(tick,info,g_in,far_in,exits,time_rows,gain_attn,gain_mlp,cos,sin,w_qkv,w_out,w_up,w_down,
               hid,qkv,prob,sec,gps,
               s_g,s_pre,s_gattn,s_mixed,s_first,
               o_next,o_vec,o_g,o_pre,o_gattn,o_mixed,o_first,
               b_g,b_hid,b_qkv,b_prob,b_sec,b_gp,b_pre,b_gattn,b_gctx,b_second,b_mixed,wsem,hsem,osem):
    active=info[tick,0]; slot=info[tick,1]; source=info[tick,2]
    width=b_hid.shape[1]; T=b_hid.shape[0]
    nw=w_up.shape[1]//width
    npair=width//128
    @pl.when(active==1)
    def _():
        src_copy=pltpu.make_async_copy(exits.at[slot],b_g,hsem)
        @pl.when(source==0)
        def _(): src_copy.start()
        @pl.when(source==1)
        def _(): b_g[...]=g_in[...]
        @pl.when(source==2)
        def _(): pltpu.make_async_copy(far_in,b_g,hsem).start()
        ld=Loads(wsem,DEPTH)
        kg=[]
        for i in range(nw):
            cols=pl.ds(i*width,width)
            kg.append(ld.add(gps.at[slot,:,cols],b_gp.at[i]))
        ks=ld.add(sec.at[slot],b_sec)
        kqkv=ld.add(qkv.at[slot],b_qkv)
        kp=ld.add(prob.at[slot],b_prob)
        kh=ld.add(hid.at[slot],b_hid)
        ld.fill(DEPTH)
        outs=Puts(osem)
        @pl.when(source!=1)
        def _(): src_copy.wait()
        outs.add(b_g,o_g.at[slot])
        g=b_g[...]
        acc=None
        for i in range(nw):
            ga=dot_nt(g,w_down[i*width:(i+1)*width,:])
            ld.wait(kg[i])
            pre=(ga*b_gp[i].astype(F32)).astype(BF)
            b_pre[i]=pre
            outs.add(b_pre.at[i],o_pre.at[slot,:,pl.ds(i*width,width)])
            d=dot_nt(pre,w_up[:,i*width:(i+1)*width])
            acc=d if acc is None else acc+d
        ld.wait(ks)
        second=b_sec[...].astype(F32)
        r2=lax.rsqrt(jnp.mean(second*second,axis=1,keepdims=True)+NORM_EPSILON)
        n2=second*r2
        gain_row=jnp.sum(acc*n2,axis=0,keepdims=True)
        gn=acc*gain_mlp[...].astype(F32)
        gs=b_g[...].astype(F32)+r2*(gn-n2*jnp.mean(gn*n2,axis=1,keepdims=True))
        b_second[...]=gs
        b_gattn[...]=gs.astype(BF)
        outs.add(b_gattn,o_gattn.at[slot])
        b_gctx[...]=dot_nt(b_gattn[...],w_out[...]).astype(BF)
        lane=lax.broadcasted_iota(jnp.int32,(T,128),1)
        low=(lane%64)<32
        head0=lane<64
        c_=cos[...]; s_=sin[...]
        ld.wait(kqkv); ld.wait(kp)
        for p in range(npair):
            sl=[slice(i*width+p*128,i*width+(p+1)*128) for i in range(3)]
            q=b_qkv[:,sl[0]]; k=b_qkv[:,sl[1]]; v=b_qkv[:,sl[2]]
            gc=b_gctx[:,p*128:(p+1)*128]
            z=jnp.zeros_like(q)
            qs=jnp.concatenate([jnp.where(head0,q,z),jnp.where(head0,z,q)],axis=0)
            gcs=jnp.concatenate([jnp.where(head0,gc,z),jnp.where(head0,z,gc)],axis=0)
            pl_=b_prob[p]
            b_mixed[:,sl[2]]=dot_tn(pl_,gcs).astype(BF)
            gp=dot_nt(gcs,v)
            pf=pl_.astype(F32)
            gsc=(pf*(gp-jnp.sum(gp*pf,axis=1,keepdims=True))).astype(BF)
            gq=dot(gsc,k)
            gq=jnp.where(head0,gq[:T],gq[T:])*SCORE_SCALE
            gk=dot_tn(gsc,qs)*SCORE_SCALE
            b_mixed[:,sl[0]]=(gq*c_-swap_halves(gq,low)*s_).astype(BF)
            b_mixed[:,sl[1]]=(gk*c_-swap_halves(gk,low)*s_).astype(BF)
        outs.add(b_mixed,o_mixed.at[slot])
        acc=None
        for i in range(3):
            d=dot_nt(b_mixed[:,i*width:(i+1)*width],w_qkv[:,i*width:(i+1)*width])
            acc=d if acc is None else acc+d
        ld.wait(kh)
        first=b_hid[...].astype(F32)+time_rows[pl.ds(slot,1),:]
        r1=lax.rsqrt(jnp.mean(first*first,axis=1,keepdims=True)+NORM_EPSILON)
        n1=first*r1
        attn_row=jnp.sum(acc*n1,axis=0,keepdims=True)
        gm=acc*gain_attn[...].astype(F32)
        gf=b_second[...]+r1*(gm-n1*jnp.mean(gm*n1,axis=1,keepdims=True))
        o_next[...]=gf.astype(BF)
        outs.add(o_next,o_first.at[slot])
        o_vec[...]=jnp.concatenate([attn_row,gain_row,jnp.sum(gf,axis=0,keepdims=True)],axis=0)
        outs.wait()

def grad_shapes(micro,T,width,hidden):
    B=lambda *s: jax.ShapeDtypeStruct((micro,)+s,BF)
    return [B(T,width),B(T,hidden),B(T,width),B(T,3*width),B(T,width)]

def layer_backward(tick,info,g,far,exits,time_rows,ga,gm,cos,sin,w_qkv,w_out,w_up,w_down,saved,stores):
    T,width=g.shape; hidden=w_up.shape[1]; micro=exits.shape[0]; nw=hidden//width; npair=width//128
    V=lambda *s: pltpu.VMEM(s,BF)
    scratch=[V(T,width),
             V(T,width),V(T,3*width),V(npair,2*T,T),V(T,width),V(nw,T,width),V(nw,T,width),V(T,width),V(T,width),pltpu.VMEM((T,width),F32),V(T,3*width),
             pltpu.SemaphoreType.DMA((4+nw,)),pltpu.SemaphoreType.DMA,pltpu.SemaphoreType.DMA((4+nw,))]
    out=pl.pallas_call(functools.partial(bwd_kernel,tick),
        in_specs=[SM,VM,HB,HB,VM,VM,VM,VM,VM]+[VM]*4+[HB]*5+[HB]*5,
        out_specs=[VM,VM]+[HB]*5,
        out_shape=[jax.ShapeDtypeStruct((T,width),BF),jax.ShapeDtypeStruct((3,width),F32)]+[pltpu.HBM(s.shape,s.dtype) for s in grad_shapes(micro,T,width,hidden)],
        input_output_aliases={18+i:2+i for i in range(5)},
        scratch_shapes=scratch,
        compiler_params=pltpu.CompilerParams(vmem_limit_bytes=LAYER_LIMIT),
        cost_estimate=pl.CostEstimate(flops=2*T*width*(4*width+2*hidden),bytes_accessed=2*width*(4*width+2*hidden)+8*1024*1024,transcendentals=0),
        name="layer_bwd",
    )(info,g,in_hbm(far),in_hbm(exits),time_rows,ga,gm,cos,sin,w_qkv,w_out,w_up,w_down,*map(in_hbm,saved),*map(in_hbm,stores))
    return out[0],out[1],out[2:]

def rope_tables(T,head):
    half=head//2
    rates=jnp.exp(-math.log(10000.0)*jnp.arange(half,dtype=F32)/half)
    ang=jnp.arange(T,dtype=F32)[:,None]*rates[None,:]
    c=jnp.cos(ang); s=jnp.sin(ang)
    return jnp.concatenate([c,c,c,c],1),jnp.concatenate([-s,s,-s,s],1)


def rms_scale(values):
    return values * lax.rsqrt(jnp.mean(values * values, axis=-1, keepdims=True) + NORM_EPSILON)


def noise_level(time_index):
    fraction = time_index.astype(jnp.float32) / (NOISE_LEVELS - 1)
    return jnp.exp(SIGMA_LOW_LOG + (SIGMA_HIGH_LOG - SIGMA_LOW_LOG) * fraction)


def time_features(sigma, width):
    half = width // 2
    rates = jnp.exp(-math.log(10000.0) * jnp.arange(half, dtype=jnp.float32) / half)
    angles = jnp.log(sigma)[..., None] * TIME_ANGLE * rates
    return jnp.concatenate([jnp.cos(angles), jnp.sin(angles)], axis=-1)


def head_forward_kernel(table, latent, o_mean, o_stats, top, total, mixed):
    step = pl.program_id(0)

    @pl.when(step == 0)
    def _():
        top[...] = jnp.full_like(top, -jnp.inf)
        total[...] = jnp.zeros_like(total)
        mixed[...] = jnp.zeros_like(mixed)

    rows = table[...]
    logits = dot_nt(rows, latent[...])
    peak = jnp.maximum(top[...], jnp.max(logits, axis=0, keepdims=True))
    fade = jnp.exp(top[...] - peak)
    e = jnp.exp(logits - peak)
    total[...] = total[...] * fade + jnp.sum(e, axis=0, keepdims=True)
    mixed[...] = mixed[...] * fade + dot_tn(rows, e.astype(BF))
    top[...] = peak

    @pl.when(step == pl.num_programs(0) - 1)
    def _():
        o_mean[...] = (mixed[...] / total[...]).astype(BF)
        o_stats[...] = jnp.concatenate([top[...], total[...]], axis=0)


def vocab_tile(rows):
    for tile in (1600, 800, 400):
        if rows % tile == 0 and tile % 16 == 0:
            return tile
    return rows


def head_forward(table, latent):
    rows, emb = table.shape
    tokens = latent.shape[0]
    tile = vocab_tile(rows)
    return pl.pallas_call(
        head_forward_kernel,
        grid=(rows // tile,),
        in_specs=[pl.BlockSpec((tile, emb), lambda i: (i, 0)), pl.BlockSpec((tokens, emb), lambda i: (0, 0))],
        out_specs=[pl.BlockSpec((emb, tokens), lambda i: (0, 0)), pl.BlockSpec((2, tokens), lambda i: (0, 0))],
        out_shape=[jax.ShapeDtypeStruct((emb, tokens), BF), jax.ShapeDtypeStruct((2, tokens), F32)],
        scratch_shapes=[pltpu.VMEM((1, tokens), F32), pltpu.VMEM((1, tokens), F32), pltpu.VMEM((emb, tokens), F32)],
        compiler_params=pltpu.CompilerParams(vmem_limit_bytes=HEAD_LIMIT),
        cost_estimate=pl.CostEstimate(flops=4 * rows * emb * tokens, bytes_accessed=2 * rows * emb, transcendentals=rows * tokens),
        name="head_fwd",
    )(table, latent)


def head_backward_kernel(table, latent, log_total, weight, ids, terms, token, o_grad):
    logits = dot_nt(table[...], latent[...])
    g = (jnp.exp(logits - log_total[...]) * weight[...]).astype(BF)
    rows = lax.broadcasted_iota(jnp.int32, g.shape, 0) + pl.program_id(0) * g.shape[0]
    picks = jnp.where(rows == ids[...], 1.0, 0.0).astype(BF)
    o_grad[...] = (dot(g, latent[...]) + dot(picks, terms[...])).astype(BF)


def head_backward(table, latent, log_total, weight, ids, terms, token):
    rows, emb = table.shape
    tokens = latent.shape[0]
    tile = vocab_tile(rows)
    return pl.pallas_call(
        head_backward_kernel,
        grid=(rows // tile,),
        in_specs=[
            pl.BlockSpec((tile, emb), lambda i: (i, 0)),
            pl.BlockSpec((tokens, emb), lambda i: (0, 0)),
            pl.BlockSpec((1, tokens), lambda i: (0, 0)),
            pl.BlockSpec((1, tokens), lambda i: (0, 0)),
            pl.BlockSpec((1, tokens), lambda i: (0, 0)),
            pl.BlockSpec((tokens, emb), lambda i: (0, 0)),
            ANY,
        ],
        out_specs=pl.BlockSpec((tile, emb), lambda i: (i, 0)),
        out_shape=jax.ShapeDtypeStruct((rows, emb), BF),
        compiler_params=pltpu.CompilerParams(vmem_limit_bytes=HEAD_LIMIT),
        cost_estimate=pl.CostEstimate(flops=1, bytes_accessed=1, transcendentals=0),
        name="head_bwd",
    )(table, latent, log_total, weight, ids, terms, token)


def blank_kernel(*refs):
    pass


def blanks(shapes):
    return pl.pallas_call(blank_kernel, out_specs=[HB] * len(shapes), out_shape=shapes, name="blanks")()


def bits_of(size):
    bits = size.bit_length() - 1
    if 1 << bits != size:
        raise ValueError("axis size")
    return bits


def dp_orders(size):
    bits = bits_of(size)
    low = bits // 2
    return (
        list(range(bits)),
        list(range(low, bits)) + list(range(low)),
        [low] + list(range(low)) + list(range(low + 1, bits)),
    )


def swap(x, axis, bit):
    pairs = [(i, i ^ (1 << bit)) for i in range(lax.axis_size(axis))]
    return lax.ppermute(x, axis, pairs)


def gather(x, axis, order):
    index = lax.axis_index(axis)
    held = []
    for bit in order:
        other = swap(x, axis, bit)
        at = sum(1 for b in held if b > bit)
        mine = (index >> bit) & 1
        x = jnp.where(mine == 0, jnp.stack([x, other], at), jnp.stack([other, x], at))
        held.append(bit)
    size = lax.axis_size(axis)
    return x.reshape((size,) + x.shape[len(order):])


def gather_rows(x, axis, order):
    rows = x.shape[0]
    piece = -(-rows // 4) // 16 * 16 + 16 if rows >= 512 else rows
    pieces = [x[i : min(i + piece, rows)] for i in range(0, rows, piece)]
    index = lax.axis_index(axis)
    held = []
    token = None
    for bit in order:
        at = sum(1 for b in held if b > bit)
        mine = (index >> bit) & 1
        for n, part in enumerate(pieces):
            other = swap(part, axis, bit)
            if token is not None:
                other = after(other, token)
            token = pieces[n] = jnp.where(mine == 0, jnp.stack([part, other], at), jnp.stack([other, part], at))
        held.append(bit)
    pieces = [p.reshape((-1,) + p.shape[len(order) :]) for p in pieces]
    return jnp.concatenate(pieces, axis=1)


def scatter_sum(x, axis, order):
    index = lax.axis_index(axis)
    bits = bits_of(lax.axis_size(axis))
    x = x.reshape((2,) * bits + x.shape[1:])
    left = list(range(bits - 1, -1, -1))
    for n, bit in enumerate(order):
        at = left.index(bit)
        mine = (index >> bit) & 1
        sent = lax.dynamic_index_in_dim(x, 1 - mine, at, keepdims=False)
        kept = lax.dynamic_index_in_dim(x, mine, at, keepdims=False)
        got = swap(sent, axis, bit)
        x = kept.astype(F32) + got.astype(F32)
        if n + 1 < len(order):
            x = x.astype(BF)
        left.remove(bit)
    return x


def zero_of(token):
    return jnp.minimum(jnp.abs(token[(0,) * token.ndim].astype(F32)), 0.0)


def after(x, token):
    return x + zero_of(token).astype(x.dtype)


class Scatter:
    def __init__(self, blocks, order, index):
        self.order = list(order)
        self.left = list(range(len(order) - 1, -1, -1))
        self.index = index
        self.terms = [blocks.reshape((2,) * len(order) + blocks.shape[1:])]

    def _side(self, side, at):
        parts = [lax.dynamic_index_in_dim(t, side, at, keepdims=False).astype(F32) for t in self.terms]
        return sum(parts[1:], parts[0])

    def send(self, token):
        bit = self.order.pop(0)
        at = self.left.index(bit)
        self.left.remove(bit)
        mine = (self.index >> bit) & 1
        sent = (self._side(1 - mine, at) + (0.0 if token is None else zero_of(token))).astype(BF)
        self.got = lax.ppermute(sent, "dp", [(i, i ^ (1 << bit)) for i in range(lax.axis_size("dp"))])
        self.terms = [lax.dynamic_index_in_dim(t, mine, at, keepdims=False) for t in self.terms]
        return sent

    def step(self, token):
        self.terms.append(self.got)
        return self.send(token)

    def end(self, token):
        while self.order:
            token = self.step(token)
        parts = [t.astype(F32) for t in self.terms + [self.got]]
        self.total = sum(parts[1:], parts[0]) + zero_of(token)
        return self.total


def product_kernel(ids, *refs):
    left, (right, token, out, mark) = refs[:-4], refs[-4:]
    a = jnp.concatenate([r[...] for r in left], axis=1)
    out[...] = dot_tn(a, right[...]).astype(BF)
    mark[...] = jnp.zeros_like(mark)


def product(left, right, ids, row, count, block, part, parts, token):
    rows, columns = left.shape[0], right.shape[1] // parts
    tile = 512 if columns % 512 == 0 else columns
    first = part * columns // tile

    def pick(j):
        return pl.BlockSpec((rows, block), lambda i, ids: (0, ids[row, j]))

    return pl.pallas_call(
        product_kernel,
        grid_spec=pltpu.PrefetchScalarGridSpec(
            num_scalar_prefetch=1,
            grid=(columns // tile,),
            in_specs=[pick(j) for j in range(count)] + [pl.BlockSpec((rows, tile), lambda i, ids: (0, first + i)), ANY],
            out_specs=[
                pl.BlockSpec((count * block, tile), lambda i, ids: (0, i)),
                pl.BlockSpec((8, 128), lambda i, ids: (0, 0)),
            ],
        ),
        out_shape=[
            jax.ShapeDtypeStruct((count * block, columns), BF),
            jax.ShapeDtypeStruct((8, 128), F32),
        ],
        compiler_params=pltpu.CompilerParams(vmem_limit_bytes=VMEM_LIMIT),
        cost_estimate=pl.CostEstimate(flops=1, bytes_accessed=1, transcendentals=0),
        name="product",
    )(ids, *[left] * count, right, token)


class Product(Scatter):
    def __init__(self, left, right, order, index, table, first_row, part=0, parts=1):
        self.table, self.first_row = table, first_row
        self.order = list(order)
        self.bits = len(order)
        self.left = list(range(self.bits - 1, -1, -1))
        self.index = index
        self.a, self.g = left, right
        self.part, self.parts = part, parts

    def _half(self, stays, token):
        rows = self.a.shape[1]
        block = rows >> self.bits
        count = 1 << (self.bits - 1)
        row = self.first_row + 2 * self.bit + stays
        if block % 128 == 0:
            x, mark = product(self.a, self.g, self.table, row, count, block, self.part, self.parts, token)
        else:
            ids = self.table[row, :count]
            a = jnp.take(self.a.reshape(self.a.shape[0], -1, block), ids, axis=1).reshape(self.a.shape[0], -1)
            wide = self.g.shape[1] // self.parts
            x = dot_tn(after(a, token), self.g[:, self.part * wide : (self.part + 1) * wide]).astype(BF)
            mark = x
        return x.reshape((2,) * (self.bits - 1) + (block, x.shape[1])), mark

    def send(self, token):
        if len(self.order) == self.bits:
            self.bit = bit = self.order.pop(0)
            self.left.remove(bit)
            self.mine = (self.index >> bit) & 1
            sent, mark = self._half(0, token)
            self.got = lax.ppermute(sent, "dp", [(i, i ^ (1 << bit)) for i in range(lax.axis_size("dp"))])
            return mark
        return super().send(token)

    def keep(self, token):
        kept, mark = self._half(1, token)
        self.terms = [kept]
        return mark


def tick_infos(ticks, offset, micro, source):
    slot = jnp.arange(ticks) - offset
    active = (slot >= 0) & (slot < micro)
    return jnp.stack(
        [active.astype(jnp.int32), jnp.clip(slot, 0, micro - 1), jnp.full((ticks,), source, jnp.int32)], axis=1
    ).astype(jnp.int32)


def with_halves(infos, groups):
    bits = bits_of(groups)
    index = lax.axis_index("dp")
    rows = []
    for bit in range(bits):
        base = jnp.array([i for i in range(groups) if not (i >> bit) & 1], jnp.int32)
        mine = ((index >> bit) & 1).astype(jnp.int32)
        rows += [base + ((1 - mine) << bit), base + (mine << bit)]
    rows = jnp.stack(rows)
    wide = max(infos.shape[1], rows.shape[1])
    infos = jnp.pad(infos, ((0, 0), (0, wide - infos.shape[1])))
    rows = jnp.pad(rows, ((0, 0), (0, wide - rows.shape[1])))
    return jnp.concatenate([infos, rows])


def sum_all(x, axis):
    for bit in range(bits_of(lax.axis_size(axis))):
        x = x + swap(x, axis, bit)
    return x


def spread(x, axis, root):
    index = lax.axis_index(axis)
    holders = [root]
    for bit in range(bits_of(lax.axis_size(axis))):
        pairs = [(h, h ^ (1 << bit)) for h in holders]
        got = lax.ppermute(x, axis, pairs)
        fresh = [b for a, b in pairs]
        new = jnp.zeros((), jnp.bool_)
        for f in fresh:
            new = new | (index == f)
        x = jnp.where(new, got, x)
        holders = holders + fresh
    return x


def delay(section):
    return section + section // 2


def body(
    token_ids,
    noise,
    loss_mask,
    time_index,
    seq_counts,
    table,
    proj,
    w_time,
    gain_attn,
    w_qkv,
    w_out,
    gain_mlp,
    w_up,
    w_down,
):
    sections = lax.axis_size("section")
    section = lax.axis_index("section")
    groups = lax.axis_size("dp")
    micro, shard = token_ids.shape
    seq_len = shard * sections
    tokens = micro * seq_len
    width = w_qkv.shape[1]
    hidden = w_up.shape[2]
    emb = table.shape[1]
    last = sections - 1
    count = seq_counts[lax.axis_index("dp")]
    valid = (jnp.arange(micro) < count).astype(F32)
    low_first, high_first, mid_first = dp_orders(groups)
    gather_order = low_first[::-1]
    section_order = list(range(bits_of(sections)))

    own_rows, table_back = jax.vjp(rms_scale, table.astype(F32))
    own_low = own_rows.astype(BF)
    own_count = own_low.shape[0]
    bundle = gather_rows(jnp.concatenate([own_low, proj.reshape(-1, emb)]), "dp", gather_order)
    rows_sec = bundle[:, :own_count].reshape(groups * own_count, emb)
    proj_sec = bundle[:, own_count:].reshape(groups * proj.shape[0], width)
    vocab_sec = groups * own_count
    proj_full = gather(proj_sec, "section", section_order).reshape(emb, width)
    both = gather(jnp.stack([token_ids, loss_mask]), "section", section_order)
    both_rows = jnp.transpose(both, (1, 2, 0, 3)).reshape(2, tokens)
    noise_all = gather(noise, "section", section_order)
    noise_all = jnp.transpose(noise_all, (1, 0, 2, 3)).reshape(micro, seq_len, emb)
    ids_rows = both_rows[0] - section * vocab_sec
    weight = both_rows[1].astype(F32) * jnp.repeat(valid, seq_len)
    weight, ids_rows = lax.optimization_barrier((weight, ids_rows))
    onehot = (ids_rows[:, None] == jnp.arange(vocab_sec)[None, :]).astype(BF)
    picked_all = sum_all(dot(onehot, rows_sec).astype(BF), "section")
    sigma = noise_level(time_index)
    shrink = lax.rsqrt(1.0 + sigma * sigma)
    inputs_all = (
        (picked_all.astype(F32).reshape(micro, seq_len, emb) + sigma[:, None, None] * noise_all) * shrink[:, None, None]
    ).astype(BF).reshape(tokens, emb)
    entry = dot(inputs_all, proj_full).astype(BF).reshape(micro, seq_len, width)
    time_low = time_features(sigma, emb).astype(BF)
    time_rows = dot(time_low, w_time[0]) + zero_of(weight)
    cosines, sines = rope_tables(seq_len, width // HEADS)
    weights = tuple(pltpu.with_memory_space_constraint(w[0], pltpu.VMEM) for w in (w_qkv, w_out, w_up, w_down))

    stores = blanks(store_shapes(micro, seq_len, width, hidden) + [jax.ShapeDtypeStruct((seq_len, width), BF)])
    stores, unused = stores[:-1], stores[-1]
    offset = delay(section)
    ticks = micro + delay(last)
    back_offset = delay(last) - offset
    ahead = tick_infos(ticks, offset, micro, jnp.where(section == 0, 0, jnp.where(section % 2 == 1, 1, 2)))
    back = tick_infos(ticks, back_offset, micro, jnp.where(section == last, 0, jnp.where(section % 2 == 0, 1, 2)))
    infos = lax.optimization_barrier(with_halves(jnp.concatenate([ahead, back]), groups))
    core_in = x_next = x_in = unused
    tick_sums = []
    finals = []
    for tick in range(ticks):
        sent, sums, stores = layer_forward(
            tick, infos, core_in, x_in, entry, time_rows, gain_attn, gain_mlp, cosines, sines, *weights, stores
        )
        tick_sums.append(sums)
        if tick - delay(last) >= 0:
            finals.append(sent)
        going = [s for s in range(last) if 0 <= tick - delay(s) < micro]
        core_pairs = [(s, s + 1) for s in going if s % 2 == 0]
        x_pairs = [(s, s + 1) for s in going if s % 2 == 1]
        core_in = lax.ppermute(sent, "section", core_pairs) if core_pairs else sent
        x_in = x_next
        x_next = lax.ppermute(sent, "section", x_pairs) if x_pairs else sent

    final = jnp.concatenate(finals, axis=0).astype(F32)
    normalized, head_back = jax.vjp(rms_scale, final)
    feats = normalized.astype(BF)
    latent = (dot_nt(feats, proj_full).astype(BF).astype(F32) * LOGIT_SCALE).astype(BF)
    latent = spread(latent, "section", last)
    mean, stats = head_forward(rows_sec, latent)
    for bit in section_order:
        other_mean, other_stats = swap(mean, "section", bit), swap(stats, "section", bit)
        peak = jnp.maximum(stats[0], other_stats[0])
        mine_part = stats[1] * jnp.exp(stats[0] - peak)
        other_part = other_stats[1] * jnp.exp(other_stats[0] - peak)
        total = mine_part + other_part
        mean = (mean.astype(F32) * (mine_part / total) + other_mean.astype(F32) * (other_part / total))
        if bit != section_order[-1]:
            mean = mean.astype(BF)
        stats = jnp.stack([peak, total])
    log_total = stats[0] + jnp.log(stats[1])
    grad_latent = ((mean.T - picked_all.astype(F32)) * (weight * LOGIT_SCALE)[:, None]).astype(BF)
    grad_final = head_back(dot(grad_latent, proj_full))[0].astype(BF)
    exit_grad = grad_final.reshape(micro, seq_len, width)
    grad_proj = jnp.where(section == last, dot_tn(grad_latent, feats), 0.0)

    saved = [stores[0], stores[2], stores[3], stores[5], stores[7]]
    grads = blanks(grad_shapes(micro, seq_len, width, hidden))
    core_in = x_next = x_in = unused
    tick_rows = []
    sums = jnp.sum(lax.dynamic_slice_in_dim(jnp.stack(tick_sums), offset, micro, 0), axis=2)
    square_sums = jnp.sum(sums * valid[:, None], axis=0)
    for tick in range(ticks):
        sent, rows, grads = layer_backward(
            ticks + tick, infos, core_in, x_in, exit_grad, time_rows, gain_attn, gain_mlp, cosines, sines, *weights, saved, grads
        )
        tick_rows.append(rows)
        going = [s for s in range(1, sections) if 0 <= tick - (delay(last) - delay(s)) < micro]
        core_pairs = [(s, s - 1) for s in going if s % 2 == 1]
        x_pairs = [(s, s - 1) for s in going if s % 2 == 0]
        core_in = lax.ppermute(sent, "section", core_pairs) if core_pairs else sent
        x_in = x_next
        x_next = lax.ppermute(sent, "section", x_pairs) if x_pairs else sent
    grad_out_all, grad_pre_all, grad_attn_all, grad_mixed_all, grad_first_all = (
        g.reshape(tokens, g.shape[2]) for g in grads
    )
    attn_in_all, context_all, mlp_in_all, activated_all = (
        stores[i].reshape(tokens, stores[i].shape[2]) for i in (1, 4, 6, 8)
    )

    dp_index = lax.axis_index("dp")
    out = Product(context_all, grad_attn_all, high_first, dp_index, infos, 2 * ticks)
    down = [Product(activated_all, grad_out_all, low_first, dp_index, infos, 2 * ticks, part, 2) for part in range(2)]
    up = [Product(mlp_in_all, grad_pre_all, low_first, dp_index, infos, 2 * ticks, part, 2) for part in range(2)]
    qkv = [Product(attn_in_all, grad_mixed_all, low_first, dp_index, infos, 2 * ticks, part, 2) for part in range(2)]
    token = down[0].send(grad_first_all)
    token = down[1].send(token)
    token = out.send(token)
    token = up[0].send(token)
    token = out.keep(token)
    token = down[1].keep(token)
    token = up[0].keep(token)
    token = down[0].keep(token)
    token = down[0].step(None)

    grad_inputs = (dot_nt(grad_first_all, proj_full) + zero_of(token)).astype(BF)
    grad_inputs = spread(grad_inputs, "section", 0).astype(F32)
    row_terms = grad_inputs * jnp.repeat(shrink, seq_len)[:, None] - latent.astype(F32) * weight[:, None]
    zero = zero_of(token)
    grad_table = head_backward(
        rows_sec,
        latent,
        log_total[None, :] + zero,
        (weight + zero)[None, :],
        (ids_rows + zero.astype(jnp.int32))[None, :],
        row_terms.astype(BF),
        token,
    )
    tab = Scatter(grad_table.reshape(groups, -1, emb), low_first, dp_index)
    token = tab.send(token)
    token = up[1].send(token)
    token = up[1].keep(token)
    token = down[1].step(token)
    token = down[0].step(token)
    token = out.step(token)
    for part in qkv:
        token = part.send(token)
        token = part.keep(token)
    token = up[0].step(token)
    token = down[1].step(token)
    token = down[0].end(token)
    token = out.step(token)
    grad_proj = grad_proj + jnp.where(section == 0, dot_tn(inputs_all, after(grad_first_all, token)), 0.0)
    proj_part = scatter_sum(grad_proj.astype(BF).reshape(sections, emb // sections, width), "section", section_order[::-1])
    rows = lax.dynamic_slice_in_dim(jnp.stack(tick_rows), back_offset, micro, 0)
    rows = after(rows, token)
    w_time_term = jnp.dot(time_low.astype(F32).T, rows[:, 2], precision=PRECISION_MAXIMAL)
    gain_rows = jnp.sum(rows[:, :2], axis=0)
    gain_rows = jnp.transpose(gain_rows.reshape(2, groups, width // groups), (1, 0, 2)).reshape(groups, 1, -1)
    at = [emb // groups, emb // sections // groups]
    pad = -sum(at) % 16 or 16
    gain_rows = jnp.pad(gain_rows, ((0, 0), (0, pad - 1), (0, width - gain_rows.shape[2])))
    packed = jnp.concatenate(
        [
            w_time_term.astype(BF).reshape(groups, -1, width),
            proj_part.astype(BF).reshape(groups, -1, width),
            gain_rows.astype(BF),
        ],
        axis=1,
    )
    pack = Scatter(packed, high_first, dp_index)
    token = pack.send(token)
    token = tab.step(token)
    token = up[0].step(token)
    token = down[1].end(token)
    token = pack.step(token)
    token = up[1].step(token)
    token = tab.step(token)
    token = up[0].end(token)
    token = pack.step(token)
    token = qkv[0].step(token)
    token = up[1].step(token)
    token = tab.end(token)
    token = qkv[0].step(token)
    token = qkv[1].step(token)
    token = up[1].end(token)
    token = qkv[1].step(token)
    token = qkv[0].end(token)
    token = out.end(token)
    token = pack.end(token)
    square_sums = sum_all(after(square_sums, token), "dp")
    token = qkv[1].end(token)
    target_logit = jnp.sum(latent.astype(F32) * picked_all.astype(F32), axis=1)
    token_loss = (log_total - target_logit) * weight
    seq_loss = jnp.sum(token_loss.reshape(micro, seq_len), axis=1) / seq_len
    count_all = jnp.sum(after(seq_counts.astype(F32), token))
    layer_rms = jnp.sqrt(square_sums / (count_all * seq_len * width))[None, :]
    packed = pack.total
    w_out_grad = out.total
    w_down_grad = jnp.concatenate([part.total for part in down], axis=1)
    w_up_grad = jnp.concatenate([part.total for part in up], axis=1)
    w_qkv_grad = jnp.concatenate([qkv[0].total, qkv[1].total], axis=1)
    w_time_grad = packed[: at[0]]
    proj_grad = packed[at[0] : sum(at)]
    gains = packed[sum(at), : 2 * width // groups].reshape(2, width // groups)
    table_grad = table_back(tab.total)[0]
    grad_mine = lax.dynamic_slice_in_dim(
        grad_inputs.reshape(micro, seq_len, emb), section * shard, shard, 1
    )
    noise_grad = grad_mine * (sigma * shrink)[:, None, None]
    return (
        seq_loss,
        layer_rms,
        noise_grad,
        table_grad,
        proj_grad,
        w_time_grad[None],
        gains[0][None],
        w_qkv_grad[None],
        w_out_grad[None],
        gains[1][None],
        w_up_grad[None],
        w_down_grad[None],
    )


def solution(mesh):
    return jax.shard_map(
        body,
        mesh=mesh,
        in_specs=(
            P("dp", "section"),
            P("dp", "section", None),
            P("dp", "section"),
            P("dp"),
            P(),
            P(("section", "dp"), None),
            P(("section", "dp"), None),
            P("section", None, None),
            P("section", None),
            P("section", None, None),
            P("section", None, None),
            P("section", None),
            P("section", None, None),
            P("section", None, None),
        ),
        out_specs=(
            P("dp"),
            P("section", None),
            P("dp", "section", None),
            P(("section", "dp"), None),
            P(("section", "dp"), None),
            P("section", "dp", None),
            P("section", "dp"),
            P("section", "dp", None),
            P("section", "dp", None),
            P("section", "dp"),
            P("section", "dp", None),
            P("section", "dp", None),
        ),
        check_vma=False,
    )
```

```python
import functools, math
import jax
import jax.numpy as jnp
from jax import lax
from jax.experimental import pallas as pl
from jax.experimental.pallas import tpu as pltpu
from jax.sharding import PartitionSpec as P
HEADS=16
NOISE_LEVELS = 1000
LOGIT_SCALE = 0.0625
SIGMA_LOW_LOG = math.log(0.5)
SIGMA_HIGH_LOG = math.log(50.0)
TIME_ANGLE = 64.0
PRECISION_MAXIMAL = lax.Precision.HIGHEST
NORM_EPSILON=1e-6
SCORE_SCALE=0.125
DEPTH=3
F32=jnp.float32; BF=jnp.bfloat16
VMEM_LIMIT=26*1024*1024
HEAD_LIMIT=20*1024*1024
GELU_A=math.sqrt(2.0/math.pi); GELU_B=0.044715

def dot(a,b): return jnp.dot(a,b,preferred_element_type=F32)
def dot_nt(a,b): return lax.dot_general(a,b,(((1,),(1,)),((),())),preferred_element_type=F32)
def dot_tn(a,b): return lax.dot_general(a,b,(((0,),(0,)),((),())),preferred_element_type=F32)

def swap_halves(x,mask):
    return jnp.where(mask,pltpu.roll(x,96,1),pltpu.roll(x,32,1))

class Loads:
    def __init__(self,sem,ahead):
        self.sem,self.ahead,self.copies,self.next=sem,ahead,[],0
    def add(self,src,dst):
        k=len(self.copies); self.copies.append(pltpu.make_async_copy(src,dst,self.sem.at[k])); return k
    def fill(self,upto):
        while self.next<min(upto,len(self.copies)):
            self.copies[self.next].start(); self.next+=1
    def wait(self,k):
        self.fill(k+1)
        self.copies[k].wait()
        self.fill(k+1+self.ahead)
class Puts:
    def __init__(self,sem): self.sem,self.copies=sem,[]
    def add(self,src,dst):
        c=pltpu.make_async_copy(src,dst,self.sem.at[len(self.copies)]); c.start(); self.copies.append(c)
    def wait(self):
        for c in self.copies: c.wait()

def fwd_kernel(tick,info,hid_in,far_in,entry,time_rows,gain_attn,gain_mlp,cos,sin,w_qkv,w_out,w_up,w_down,
               s_hid,s_attn,s_qkv,s_prob,s_ctx,s_second,s_mlp,s_gp,s_act,
               o_next,o_sums,o_hid,o_attn,o_qkv,o_prob,o_ctx,o_second,o_mlp,o_gp,o_act,
               b_hid,b_attn,b_qkv,b_prob,b_ctx,b_second,b_low,b_mlp,b_gp,b_act,hsem,osem):
    active=info[tick,0]; slot=info[tick,1]; source=info[tick,2]
    width=b_hid.shape[1]; T=b_hid.shape[0]
    nw=w_up.shape[1]//width
    npair=width//128
    @pl.when(active==1)
    def _():
        src_copy=pltpu.make_async_copy(entry.at[slot],b_hid,hsem)
        @pl.when(source==0)
        def _(): src_copy.start()
        @pl.when(source==1)
        def _(): b_hid[...]=hid_in[...]
        @pl.when(source==2)
        def _(): pltpu.make_async_copy(far_in,b_hid,hsem).start()
        outs=Puts(osem)
        @pl.when(source!=1)
        def _(): src_copy.wait()
        outs.add(b_hid,o_hid.at[slot])
        first=b_hid[...].astype(F32)+time_rows[pl.ds(slot,1),:]
        r1=lax.rsqrt(jnp.mean(first*first,axis=1,keepdims=True)+NORM_EPSILON)
        b_attn[...]=(first*r1*gain_attn[...].astype(F32)).astype(BF)
        outs.add(b_attn,o_attn.at[slot])
        lane=lax.broadcasted_iota(jnp.int32,(T,128),1)
        low=(lane%64)<32
        head0=lane<64
        c_=cos[...]; s_=sin[...]
        a=b_attn[...]
        for i in range(3):
            m=dot(a,w_qkv[:,i*width:(i+1)*width])
            if i<2:
                for p in range(npair):
                    x=m[:,p*128:(p+1)*128]
                    b_qkv[:,i*width+p*128:i*width+(p+1)*128]=(x*c_+swap_halves(x,low)*s_).astype(BF)
            else:
                b_qkv[:,i*width:(i+1)*width]=m.astype(BF)
        outs.add(b_qkv,o_qkv.at[slot])
        for p in range(npair):
            q=b_qkv[:,p*128:(p+1)*128]; k=b_qkv[:,width+p*128:width+(p+1)*128]; v=b_qkv[:,2*width+p*128:2*width+(p+1)*128]
            z=jnp.zeros_like(q)
            qs=jnp.concatenate([jnp.where(head0,q,z),jnp.where(head0,z,q)],axis=0)
            s=dot_nt(qs,k)*SCORE_SCALE
            e=jnp.exp(s-jnp.max(s,axis=1,keepdims=True))
            pr=(e*(1.0/jnp.sum(e,axis=1,keepdims=True))).astype(BF)
            b_prob[p]=pr
            c=dot(pr,v)
            b_ctx[:,p*128:(p+1)*128]=jnp.where(head0,c[:T],c[T:]).astype(BF)
        outs.add(b_prob,o_prob.at[slot])
        outs.add(b_ctx,o_ctx.at[slot])
        ao=dot(b_ctx[...],w_out[...])
        second=b_hid[...].astype(F32)+time_rows[pl.ds(slot,1),:]+ao
        b_second[...]=second
        b_low[...]=second.astype(BF)
        outs.add(b_low,o_second.at[slot])
        sum_a=jnp.sum(ao*ao,axis=0,keepdims=True)
        r2=lax.rsqrt(jnp.mean(second*second,axis=1,keepdims=True)+NORM_EPSILON)
        b_mlp[...]=(second*r2*gain_mlp[...].astype(F32)).astype(BF)
        outs.add(b_mlp,o_mlp.at[slot])
        acc=None
        for i in range(nw):
            cols=pl.ds(i*width,width)
            u=dot(b_mlp[...],w_up[:,i*width:(i+1)*width])
            u2=u*u
            th=jnp.tanh(GELU_A*(u+GELU_B*u2*u))
            h=0.5*(1.0+th)
            act=(u*h).astype(BF)
            gp=h+0.5*u*(1.0-th*th)*(GELU_A*(1.0+3.0*GELU_B*u2))
            b_act[i]=act
            b_gp[i]=gp.astype(BF)
            outs.add(b_act.at[i],o_act.at[slot,:,cols])
            outs.add(b_gp.at[i],o_gp.at[slot,:,cols])
            d=dot(act,w_down[i*width:(i+1)*width,:])
            acc=d if acc is None else acc+d
        third=b_second[...]+acc
        o_next[...]=third.astype(BF)
        o_sums[...]=jnp.concatenate([jnp.sum(third*third,axis=0,keepdims=True),sum_a,jnp.sum(acc*acc,axis=0,keepdims=True)],axis=0)
        outs.wait()

def store_shapes(micro,T,width,hidden):
    npair=width//128
    B=lambda *s: jax.ShapeDtypeStruct((micro,)+s,BF)
    return [B(T,width),B(T,width),B(T,3*width),B(npair,2*T,T),B(T,width),B(T,width),B(T,width),B(T,hidden),B(T,hidden)]

ANY=pl.BlockSpec(memory_space=pl.ANY)
HB=pl.BlockSpec(memory_space=pltpu.HBM)
LAYER_LIMIT=22*1024*1024
VM=pl.BlockSpec(memory_space=pltpu.VMEM)
SM=pl.BlockSpec(memory_space=pltpu.SMEM)
def in_hbm(x): return pltpu.with_memory_space_constraint(x,pltpu.HBM)

def layer_forward(tick,info,hid,far,entry,time_rows,ga,gm,cos,sin,w_qkv,w_out,w_up,w_down,stores):
    T,width=hid.shape; hidden=w_up.shape[1]; micro=entry.shape[0]; nw=hidden//width; npair=width//128
    V=lambda *s: pltpu.VMEM(s,BF)
    scratch=[V(T,width),
             V(T,width),V(T,3*width),V(npair,2*T,T),V(T,width),pltpu.VMEM((T,width),F32),V(T,width),
             V(T,width),V(nw,T,width),V(nw,T,width),
             pltpu.SemaphoreType.DMA,pltpu.SemaphoreType.DMA((7+2*nw,))]
    out=pl.pallas_call(functools.partial(fwd_kernel,tick),
        in_specs=[SM,VM,HB,HB,VM,VM,VM,VM,VM,VM,VM,VM,VM]+[HB]*9,
        out_specs=[VM,VM]+[HB]*9,
        out_shape=[jax.ShapeDtypeStruct((T,width),BF),jax.ShapeDtypeStruct((3,width),F32)]+[pltpu.HBM(s.shape,s.dtype) for s in store_shapes(micro,T,width,hidden)],
        input_output_aliases={13+i:2+i for i in range(9)},
        scratch_shapes=scratch,
        compiler_params=pltpu.CompilerParams(vmem_limit_bytes=LAYER_LIMIT),
        cost_estimate=pl.CostEstimate(flops=2*T*width*(4*width+2*hidden),bytes_accessed=2*width*(4*width+2*hidden)+8*1024*1024,transcendentals=0),
        name="layer_fwd",
    )(info,hid,in_hbm(far),in_hbm(entry),time_rows,ga,gm,cos,sin,w_qkv,w_out,w_up,w_down,*map(in_hbm,stores))
    return out[0],out[1],out[2:]

def bwd_kernel(tick,info,g_in,far_in,exits,time_rows,gain_attn,gain_mlp,cos,sin,w_qkv,w_out,w_up,w_down,
               hid,qkv,prob,sec,gps,
               s_g,s_pre,s_gattn,s_mixed,s_first,
               o_next,o_vec,o_g,o_pre,o_gattn,o_mixed,o_first,
               b_g,b_hid,b_qkv,b_prob,b_sec,b_gp,b_pre,b_gattn,b_gctx,b_second,b_mixed,wsem,hsem,osem):
    active=info[tick,0]; slot=info[tick,1]; source=info[tick,2]
    width=b_hid.shape[1]; T=b_hid.shape[0]
    nw=w_up.shape[1]//width
    npair=width//128
    @pl.when(active==1)
    def _():
        src_copy=pltpu.make_async_copy(exits.at[slot],b_g,hsem)
        @pl.when(source==0)
        def _(): src_copy.start()
        @pl.when(source==1)
        def _(): b_g[...]=g_in[...]
        @pl.when(source==2)
        def _(): pltpu.make_async_copy(far_in,b_g,hsem).start()
        ld=Loads(wsem,DEPTH)
        kg=[]
        for i in range(nw):
            cols=pl.ds(i*width,width)
            kg.append(ld.add(gps.at[slot,:,cols],b_gp.at[i]))
        ks=ld.add(sec.at[slot],b_sec)
        kqkv=ld.add(qkv.at[slot],b_qkv)
        kp=ld.add(prob.at[slot],b_prob)
        kh=ld.add(hid.at[slot],b_hid)
        ld.fill(DEPTH)
        outs=Puts(osem)
        @pl.when(source!=1)
        def _(): src_copy.wait()
        outs.add(b_g,o_g.at[slot])
        g=b_g[...]
        acc=None
        for i in range(nw):
            ga=dot_nt(g,w_down[i*width:(i+1)*width,:])
            ld.wait(kg[i])
            pre=(ga*b_gp[i].astype(F32)).astype(BF)
            b_pre[i]=pre
            outs.add(b_pre.at[i],o_pre.at[slot,:,pl.ds(i*width,width)])
            d=dot_nt(pre,w_up[:,i*width:(i+1)*width])
            acc=d if acc is None else acc+d
        ld.wait(ks)
        second=b_sec[...].astype(F32)
        r2=lax.rsqrt(jnp.mean(second*second,axis=1,keepdims=True)+NORM_EPSILON)
        n2=second*r2
        gain_row=jnp.sum(acc*n2,axis=0,keepdims=True)
        gn=acc*gain_mlp[...].astype(F32)
        gs=b_g[...].astype(F32)+r2*(gn-n2*jnp.mean(gn*n2,axis=1,keepdims=True))
        b_second[...]=gs
        b_gattn[...]=gs.astype(BF)
        outs.add(b_gattn,o_gattn.at[slot])
        b_gctx[...]=dot_nt(b_gattn[...],w_out[...]).astype(BF)
        lane=lax.broadcasted_iota(jnp.int32,(T,128),1)
        low=(lane%64)<32
        head0=lane<64
        c_=cos[...]; s_=sin[...]
        ld.wait(kqkv); ld.wait(kp)
        for p in range(npair):
            sl=[slice(i*width+p*128,i*width+(p+1)*128) for i in range(3)]
            q=b_qkv[:,sl[0]]; k=b_qkv[:,sl[1]]; v=b_qkv[:,sl[2]]
            gc=b_gctx[:,p*128:(p+1)*128]
            z=jnp.zeros_like(q)
            qs=jnp.concatenate([jnp.where(head0,q,z),jnp.where(head0,z,q)],axis=0)
            gcs=jnp.concatenate([jnp.where(head0,gc,z),jnp.where(head0,z,gc)],axis=0)
            pl_=b_prob[p]
            b_mixed[:,sl[2]]=dot_tn(pl_,gcs).astype(BF)
            gp=dot_nt(gcs,v)
            pf=pl_.astype(F32)
            gsc=(pf*(gp-jnp.sum(gp*pf,axis=1,keepdims=True))).astype(BF)
            gq=dot(gsc,k)
            gq=jnp.where(head0,gq[:T],gq[T:])*SCORE_SCALE
            gk=dot_tn(gsc,qs)*SCORE_SCALE
            b_mixed[:,sl[0]]=(gq*c_-swap_halves(gq,low)*s_).astype(BF)
            b_mixed[:,sl[1]]=(gk*c_-swap_halves(gk,low)*s_).astype(BF)
        outs.add(b_mixed,o_mixed.at[slot])
        acc=None
        for i in range(3):
            d=dot_nt(b_mixed[:,i*width:(i+1)*width],w_qkv[:,i*width:(i+1)*width])
            acc=d if acc is None else acc+d
        ld.wait(kh)
        first=b_hid[...].astype(F32)+time_rows[pl.ds(slot,1),:]
        r1=lax.rsqrt(jnp.mean(first*first,axis=1,keepdims=True)+NORM_EPSILON)
        n1=first*r1
        attn_row=jnp.sum(acc*n1,axis=0,keepdims=True)
        gm=acc*gain_attn[...].astype(F32)
        gf=b_second[...]+r1*(gm-n1*jnp.mean(gm*n1,axis=1,keepdims=True))
        o_next[...]=gf.astype(BF)
        outs.add(o_next,o_first.at[slot])
        o_vec[...]=jnp.concatenate([attn_row,gain_row,jnp.sum(gf,axis=0,keepdims=True)],axis=0)
        outs.wait()

def grad_shapes(micro,T,width,hidden):
    B=lambda *s: jax.ShapeDtypeStruct((micro,)+s,BF)
    return [B(T,width),B(T,hidden),B(T,width),B(T,3*width),B(T,width)]

def layer_backward(tick,info,g,far,exits,time_rows,ga,gm,cos,sin,w_qkv,w_out,w_up,w_down,saved,stores):
    T,width=g.shape; hidden=w_up.shape[1]; micro=exits.shape[0]; nw=hidden//width; npair=width//128
    V=lambda *s: pltpu.VMEM(s,BF)
    scratch=[V(T,width),
             V(T,width),V(T,3*width),V(npair,2*T,T),V(T,width),V(nw,T,width),V(nw,T,width),V(T,width),V(T,width),pltpu.VMEM((T,width),F32),V(T,3*width),
             pltpu.SemaphoreType.DMA((4+nw,)),pltpu.SemaphoreType.DMA,pltpu.SemaphoreType.DMA((4+nw,))]
    out=pl.pallas_call(functools.partial(bwd_kernel,tick),
        in_specs=[SM,VM,HB,HB,VM,VM,VM,VM,VM]+[VM]*4+[HB]*5+[HB]*5,
        out_specs=[VM,VM]+[HB]*5,
        out_shape=[jax.ShapeDtypeStruct((T,width),BF),jax.ShapeDtypeStruct((3,width),F32)]+[pltpu.HBM(s.shape,s.dtype) for s in grad_shapes(micro,T,width,hidden)],
        input_output_aliases={18+i:2+i for i in range(5)},
        scratch_shapes=scratch,
        compiler_params=pltpu.CompilerParams(vmem_limit_bytes=LAYER_LIMIT),
        cost_estimate=pl.CostEstimate(flops=2*T*width*(4*width+2*hidden),bytes_accessed=2*width*(4*width+2*hidden)+8*1024*1024,transcendentals=0),
        name="layer_bwd",
    )(info,g,in_hbm(far),in_hbm(exits),time_rows,ga,gm,cos,sin,w_qkv,w_out,w_up,w_down,*map(in_hbm,saved),*map(in_hbm,stores))
    return out[0],out[1],out[2:]

def rope_tables(T,head):
    half=head//2
    rates=jnp.exp(-math.log(10000.0)*jnp.arange(half,dtype=F32)/half)
    ang=jnp.arange(T,dtype=F32)[:,None]*rates[None,:]
    c=jnp.cos(ang); s=jnp.sin(ang)
    return jnp.concatenate([c,c,c,c],1),jnp.concatenate([-s,s,-s,s],1)


def rms_scale(values):
    return values * lax.rsqrt(jnp.mean(values * values, axis=-1, keepdims=True) + NORM_EPSILON)


def noise_level(time_index):
    fraction = time_index.astype(jnp.float32) / (NOISE_LEVELS - 1)
    return jnp.exp(SIGMA_LOW_LOG + (SIGMA_HIGH_LOG - SIGMA_LOW_LOG) * fraction)


def time_features(sigma, width):
    half = width // 2
    rates = jnp.exp(-math.log(10000.0) * jnp.arange(half, dtype=jnp.float32) / half)
    angles = jnp.log(sigma)[..., None] * TIME_ANGLE * rates
    return jnp.concatenate([jnp.cos(angles), jnp.sin(angles)], axis=-1)


def head_forward_kernel(table, latent, o_mean, o_stats, top, total, mixed):
    step = pl.program_id(0)

    @pl.when(step == 0)
    def _():
        top[...] = jnp.full_like(top, -jnp.inf)
        total[...] = jnp.zeros_like(total)
        mixed[...] = jnp.zeros_like(mixed)

    rows = table[...]
    logits = dot_nt(rows, latent[...])
    peak = jnp.maximum(top[...], jnp.max(logits, axis=0, keepdims=True))
    fade = jnp.exp(top[...] - peak)
    e = jnp.exp(logits - peak)
    total[...] = total[...] * fade + jnp.sum(e, axis=0, keepdims=True)
    mixed[...] = mixed[...] * fade + dot_tn(rows, e.astype(BF))
    top[...] = peak

    @pl.when(step == pl.num_programs(0) - 1)
    def _():
        o_mean[...] = (mixed[...] / total[...]).astype(BF)
        o_stats[...] = jnp.concatenate([top[...], total[...]], axis=0)


def vocab_tile(rows):
    for tile in (1600, 800, 400):
        if rows % tile == 0 and tile % 16 == 0:
            return tile
    return rows


def head_forward(table, latent):
    rows, emb = table.shape
    tokens = latent.shape[0]
    tile = vocab_tile(rows)
    return pl.pallas_call(
        head_forward_kernel,
        grid=(rows // tile,),
        in_specs=[pl.BlockSpec((tile, emb), lambda i: (i, 0)), pl.BlockSpec((tokens, emb), lambda i: (0, 0))],
        out_specs=[pl.BlockSpec((emb, tokens), lambda i: (0, 0)), pl.BlockSpec((2, tokens), lambda i: (0, 0))],
        out_shape=[jax.ShapeDtypeStruct((emb, tokens), BF), jax.ShapeDtypeStruct((2, tokens), F32)],
        scratch_shapes=[pltpu.VMEM((1, tokens), F32), pltpu.VMEM((1, tokens), F32), pltpu.VMEM((emb, tokens), F32)],
        compiler_params=pltpu.CompilerParams(vmem_limit_bytes=HEAD_LIMIT),
        cost_estimate=pl.CostEstimate(flops=4 * rows * emb * tokens, bytes_accessed=2 * rows * emb, transcendentals=rows * tokens),
        name="head_fwd",
    )(table, latent)


def head_backward_kernel(table, latent, log_total, weight, ids, terms, token, o_grad):
    logits = dot_nt(table[...], latent[...])
    g = (jnp.exp(logits - log_total[...]) * weight[...]).astype(BF)
    rows = lax.broadcasted_iota(jnp.int32, g.shape, 0) + pl.program_id(0) * g.shape[0]
    picks = jnp.where(rows == ids[...], 1.0, 0.0).astype(BF)
    o_grad[...] = (dot(g, latent[...]) + dot(picks, terms[...])).astype(BF)


def head_backward(table, latent, log_total, weight, ids, terms, token):
    rows, emb = table.shape
    tokens = latent.shape[0]
    tile = vocab_tile(rows)
    return pl.pallas_call(
        head_backward_kernel,
        grid=(rows // tile,),
        in_specs=[
            pl.BlockSpec((tile, emb), lambda i: (i, 0)),
            pl.BlockSpec((tokens, emb), lambda i: (0, 0)),
            pl.BlockSpec((1, tokens), lambda i: (0, 0)),
            pl.BlockSpec((1, tokens), lambda i: (0, 0)),
            pl.BlockSpec((1, tokens), lambda i: (0, 0)),
            pl.BlockSpec((tokens, emb), lambda i: (0, 0)),
            ANY,
        ],
        out_specs=pl.BlockSpec((tile, emb), lambda i: (i, 0)),
        out_shape=jax.ShapeDtypeStruct((rows, emb), BF),
        compiler_params=pltpu.CompilerParams(vmem_limit_bytes=HEAD_LIMIT),
        cost_estimate=pl.CostEstimate(flops=1, bytes_accessed=1, transcendentals=0),
        name="head_bwd",
    )(table, latent, log_total, weight, ids, terms, token)


def blank_kernel(*refs):
    pass


def blanks(shapes):
    return pl.pallas_call(blank_kernel, out_specs=[HB] * len(shapes), out_shape=shapes, name="blanks")()


def bits_of(size):
    bits = size.bit_length() - 1
    if 1 << bits != size:
        raise ValueError("axis size")
    return bits


def dp_orders(size):
    bits = bits_of(size)
    low = bits // 2
    return (
        list(range(bits)),
        list(range(low, bits)) + list(range(low)),
        [low] + list(range(low)) + list(range(low + 1, bits)),
    )


def swap(x, axis, bit):
    pairs = [(i, i ^ (1 << bit)) for i in range(lax.axis_size(axis))]
    return lax.ppermute(x, axis, pairs)


def gather(x, axis, order):
    index = lax.axis_index(axis)
    held = []
    for bit in order:
        other = swap(x, axis, bit)
        at = sum(1 for b in held if b > bit)
        mine = (index >> bit) & 1
        x = jnp.where(mine == 0, jnp.stack([x, other], at), jnp.stack([other, x], at))
        held.append(bit)
    size = lax.axis_size(axis)
    return x.reshape((size,) + x.shape[len(order):])


def gather_rows(x, axis, order):
    rows = x.shape[0]
    piece = -(-rows // 4) // 16 * 16 + 16 if rows >= 512 else rows
    pieces = [x[i : min(i + piece, rows)] for i in range(0, rows, piece)]
    index = lax.axis_index(axis)
    held = []
    token = None
    for bit in order:
        at = sum(1 for b in held if b > bit)
        mine = (index >> bit) & 1
        for n, part in enumerate(pieces):
            other = swap(part, axis, bit)
            if token is not None:
                other = after(other, token)
            token = pieces[n] = jnp.where(mine == 0, jnp.stack([part, other], at), jnp.stack([other, part], at))
        held.append(bit)
    pieces = [p.reshape((-1,) + p.shape[len(order) :]) for p in pieces]
    return jnp.concatenate(pieces, axis=1)


def scatter_sum(x, axis, order):
    index = lax.axis_index(axis)
    bits = bits_of(lax.axis_size(axis))
    x = x.reshape((2,) * bits + x.shape[1:])
    left = list(range(bits - 1, -1, -1))
    for n, bit in enumerate(order):
        at = left.index(bit)
        mine = (index >> bit) & 1
        sent = lax.dynamic_index_in_dim(x, 1 - mine, at, keepdims=False)
        kept = lax.dynamic_index_in_dim(x, mine, at, keepdims=False)
        got = swap(sent, axis, bit)
        x = kept.astype(F32) + got.astype(F32)
        if n + 1 < len(order):
            x = x.astype(BF)
        left.remove(bit)
    return x


def zero_of(token):
    return jnp.minimum(jnp.abs(token[(0,) * token.ndim].astype(F32)), 0.0)


def after(x, token):
    return x + zero_of(token).astype(x.dtype)


class Scatter:
    def __init__(self, blocks, order, index):
        self.order = list(order)
        self.left = list(range(len(order) - 1, -1, -1))
        self.index = index
        self.terms = [blocks.reshape((2,) * len(order) + blocks.shape[1:])]

    def _side(self, side, at):
        parts = [lax.dynamic_index_in_dim(t, side, at, keepdims=False).astype(F32) for t in self.terms]
        return sum(parts[1:], parts[0])

    def send(self, token):
        bit = self.order.pop(0)
        at = self.left.index(bit)
        self.left.remove(bit)
        mine = (self.index >> bit) & 1
        sent = (self._side(1 - mine, at) + (0.0 if token is None else zero_of(token))).astype(BF)
        self.got = lax.ppermute(sent, "dp", [(i, i ^ (1 << bit)) for i in range(lax.axis_size("dp"))])
        self.terms = [lax.dynamic_index_in_dim(t, mine, at, keepdims=False) for t in self.terms]
        return sent

    def step(self, token):
        self.terms.append(self.got)
        return self.send(token)

    def end(self, token):
        while self.order:
            token = self.step(token)
        parts = [t.astype(F32) for t in self.terms + [self.got]]
        self.total = sum(parts[1:], parts[0]) + zero_of(token)
        return self.total


def product_kernel(ids, *refs):
    left, (right, token, out, mark) = refs[:-4], refs[-4:]
    a = jnp.concatenate([r[...] for r in left], axis=1)
    out[...] = dot_tn(a, right[...]).astype(BF)
    mark[...] = jnp.zeros_like(mark)


def product(left, right, ids, row, count, block, part, parts, token):
    rows, columns = left.shape[0], right.shape[1] // parts
    tile = 512 if columns % 512 == 0 else columns
    first = part * columns // tile

    def pick(j):
        return pl.BlockSpec((rows, block), lambda i, ids: (0, ids[row, j]))

    return pl.pallas_call(
        product_kernel,
        grid_spec=pltpu.PrefetchScalarGridSpec(
            num_scalar_prefetch=1,
            grid=(columns // tile,),
            in_specs=[pick(j) for j in range(count)] + [pl.BlockSpec((rows, tile), lambda i, ids: (0, first + i)), ANY],
            out_specs=[
                pl.BlockSpec((count * block, tile), lambda i, ids: (0, i)),
                pl.BlockSpec((8, 128), lambda i, ids: (0, 0)),
            ],
        ),
        out_shape=[
            jax.ShapeDtypeStruct((count * block, columns), BF),
            jax.ShapeDtypeStruct((8, 128), F32),
        ],
        compiler_params=pltpu.CompilerParams(vmem_limit_bytes=VMEM_LIMIT),
        cost_estimate=pl.CostEstimate(flops=1, bytes_accessed=1, transcendentals=0),
        name="product",
    )(ids, *[left] * count, right, token)


class Product(Scatter):
    def __init__(self, left, right, order, index, table, first_row, part=0, parts=1):
        self.table, self.first_row = table, first_row
        self.order = list(order)
        self.bits = len(order)
        self.left = list(range(self.bits - 1, -1, -1))
        self.index = index
        self.a, self.g = left, right
        self.part, self.parts = part, parts

    def _half(self, stays, token):
        rows = self.a.shape[1]
        block = rows >> self.bits
        count = 1 << (self.bits - 1)
        row = self.first_row + 2 * self.bit + stays
        if block % 128 == 0:
            x, mark = product(self.a, self.g, self.table, row, count, block, self.part, self.parts, token)
        else:
            ids = self.table[row, :count]
            a = jnp.take(self.a.reshape(self.a.shape[0], -1, block), ids, axis=1).reshape(self.a.shape[0], -1)
            wide = self.g.shape[1] // self.parts
            x = dot_tn(after(a, token), self.g[:, self.part * wide : (self.part + 1) * wide]).astype(BF)
            mark = x
        return x.reshape((2,) * (self.bits - 1) + (block, x.shape[1])), mark

    def send(self, token):
        if len(self.order) == self.bits:
            self.bit = bit = self.order.pop(0)
            self.left.remove(bit)
            self.mine = (self.index >> bit) & 1
            sent, mark = self._half(0, token)
            self.got = lax.ppermute(sent, "dp", [(i, i ^ (1 << bit)) for i in range(lax.axis_size("dp"))])
            return mark
        return super().send(token)

    def keep(self, token):
        kept, mark = self._half(1, token)
        self.terms = [kept]
        return mark


def tick_infos(ticks, offset, micro, source):
    slot = jnp.arange(ticks) - offset
    active = (slot >= 0) & (slot < micro)
    return jnp.stack(
        [active.astype(jnp.int32), jnp.clip(slot, 0, micro - 1), jnp.full((ticks,), source, jnp.int32)], axis=1
    ).astype(jnp.int32)


def with_halves(infos, groups):
    bits = bits_of(groups)
    index = lax.axis_index("dp")
    rows = []
    for bit in range(bits):
        base = jnp.array([i for i in range(groups) if not (i >> bit) & 1], jnp.int32)
        mine = ((index >> bit) & 1).astype(jnp.int32)
        rows += [base + ((1 - mine) << bit), base + (mine << bit)]
    rows = jnp.stack(rows)
    wide = max(infos.shape[1], rows.shape[1])
    infos = jnp.pad(infos, ((0, 0), (0, wide - infos.shape[1])))
    rows = jnp.pad(rows, ((0, 0), (0, wide - rows.shape[1])))
    return jnp.concatenate([infos, rows])


def sum_all(x, axis):
    for bit in range(bits_of(lax.axis_size(axis))):
        x = x + swap(x, axis, bit)
    return x


def spread(x, axis, root):
    index = lax.axis_index(axis)
    holders = [root]
    for bit in range(bits_of(lax.axis_size(axis))):
        pairs = [(h, h ^ (1 << bit)) for h in holders]
        got = lax.ppermute(x, axis, pairs)
        fresh = [b for a, b in pairs]
        new = jnp.zeros((), jnp.bool_)
        for f in fresh:
            new = new | (index == f)
        x = jnp.where(new, got, x)
        holders = holders + fresh
    return x


def delay(section):
    return section + section // 2


def body(
    token_ids,
    noise,
    loss_mask,
    time_index,
    seq_counts,
    table,
    proj,
    w_time,
    gain_attn,
    w_qkv,
    w_out,
    gain_mlp,
    w_up,
    w_down,
):
    sections = lax.axis_size("section")
    section = lax.axis_index("section")
    groups = lax.axis_size("dp")
    micro, shard = token_ids.shape
    seq_len = shard * sections
    tokens = micro * seq_len
    width = w_qkv.shape[1]
    hidden = w_up.shape[2]
    emb = table.shape[1]
    last = sections - 1
    count = seq_counts[lax.axis_index("dp")]
    valid = (jnp.arange(micro) < count).astype(F32)
    low_first, high_first, mid_first = dp_orders(groups)
    gather_order = low_first[::-1]
    section_order = list(range(bits_of(sections)))

    own_rows, table_back = jax.vjp(rms_scale, table.astype(F32))
    own_low = own_rows.astype(BF)
    own_count = own_low.shape[0]
    bundle = gather_rows(jnp.concatenate([own_low, proj.reshape(-1, emb)]), "dp", gather_order)
    rows_sec = bundle[:, :own_count].reshape(groups * own_count, emb)
    proj_sec = bundle[:, own_count:].reshape(groups * proj.shape[0], width)
    vocab_sec = groups * own_count
    proj_full = gather(proj_sec, "section", section_order).reshape(emb, width)
    both = gather(jnp.stack([token_ids, loss_mask]), "section", section_order)
    both_rows = jnp.transpose(both, (1, 2, 0, 3)).reshape(2, tokens)
    noise_all = gather(noise, "section", section_order)
    noise_all = jnp.transpose(noise_all, (1, 0, 2, 3)).reshape(micro, seq_len, emb)
    ids_rows = both_rows[0] - section * vocab_sec
    weight = both_rows[1].astype(F32) * jnp.repeat(valid, seq_len)
    weight, ids_rows = lax.optimization_barrier((weight, ids_rows))
    onehot = (ids_rows[:, None] == jnp.arange(vocab_sec)[None, :]).astype(BF)
    picked_all = sum_all(dot(onehot, rows_sec).astype(BF), "section")
    sigma = noise_level(time_index)
    shrink = lax.rsqrt(1.0 + sigma * sigma)
    inputs_all = (
        (picked_all.astype(F32).reshape(micro, seq_len, emb) + sigma[:, None, None] * noise_all) * shrink[:, None, None]
    ).astype(BF).reshape(tokens, emb)
    entry = dot(inputs_all, proj_full).astype(BF).reshape(micro, seq_len, width)
    time_low = time_features(sigma, emb).astype(BF)
    time_rows = dot(time_low, w_time[0]) + zero_of(weight)
    cosines, sines = rope_tables(seq_len, width // HEADS)
    weights = tuple(pltpu.with_memory_space_constraint(w[0], pltpu.VMEM) for w in (w_qkv, w_out, w_up, w_down))

    stores = blanks(store_shapes(micro, seq_len, width, hidden) + [jax.ShapeDtypeStruct((seq_len, width), BF)])
    stores, unused = stores[:-1], stores[-1]
    offset = delay(section)
    ticks = micro + delay(last)
    back_offset = delay(last) - offset
    ahead = tick_infos(ticks, offset, micro, jnp.where(section == 0, 0, jnp.where(section % 2 == 1, 1, 2)))
    back = tick_infos(ticks, back_offset, micro, jnp.where(section == last, 0, jnp.where(section % 2 == 0, 1, 2)))
    infos = lax.optimization_barrier(with_halves(jnp.concatenate([ahead, back]), groups))
    core_in = x_next = x_in = unused
    tick_sums = []
    finals = []
    for tick in range(ticks):
        sent, sums, stores = layer_forward(
            tick, infos, core_in, x_in, entry, time_rows, gain_attn, gain_mlp, cosines, sines, *weights, stores
        )
        tick_sums.append(sums)
        if tick - delay(last) >= 0:
            finals.append(sent)
        going = [s for s in range(last) if 0 <= tick - delay(s) < micro]
        core_pairs = [(s, s + 1) for s in going if s % 2 == 0]
        x_pairs = [(s, s + 1) for s in going if s % 2 == 1]
        core_in = lax.ppermute(sent, "section", core_pairs) if core_pairs else sent
        x_in = x_next
        x_next = lax.ppermute(sent, "section", x_pairs) if x_pairs else sent

    final = jnp.concatenate(finals, axis=0).astype(F32)
    normalized, head_back = jax.vjp(rms_scale, final)
    feats = normalized.astype(BF)
    latent = (dot_nt(feats, proj_full).astype(BF).astype(F32) * LOGIT_SCALE).astype(BF)
    latent = spread(latent, "section", last)
    mean, stats = head_forward(rows_sec, latent)
    for bit in section_order:
        other_mean, other_stats = swap(mean, "section", bit), swap(stats, "section", bit)
        peak = jnp.maximum(stats[0], other_stats[0])
        mine_part = stats[1] * jnp.exp(stats[0] - peak)
        other_part = other_stats[1] * jnp.exp(other_stats[0] - peak)
        total = mine_part + other_part
        mean = (mean.astype(F32) * (mine_part / total) + other_mean.astype(F32) * (other_part / total))
        if bit != section_order[-1]:
            mean = mean.astype(BF)
        stats = jnp.stack([peak, total])
    log_total = stats[0] + jnp.log(stats[1])
    grad_latent = ((mean.T - picked_all.astype(F32)) * (weight * LOGIT_SCALE)[:, None]).astype(BF)
    grad_final = head_back(dot(grad_latent, proj_full))[0].astype(BF)
    exit_grad = grad_final.reshape(micro, seq_len, width)
    grad_proj = jnp.where(section == last, dot_tn(grad_latent, feats), 0.0)

    saved = [stores[0], stores[2], stores[3], stores[5], stores[7]]
    grads = blanks(grad_shapes(micro, seq_len, width, hidden))
    core_in = x_next = x_in = unused
    tick_rows = []
    sums = jnp.sum(lax.dynamic_slice_in_dim(jnp.stack(tick_sums), offset, micro, 0), axis=2)
    square_sums = jnp.sum(sums * valid[:, None], axis=0)
    for tick in range(ticks):
        sent, rows, grads = layer_backward(
            ticks + tick, infos, core_in, x_in, exit_grad, time_rows, gain_attn, gain_mlp, cosines, sines, *weights, saved, grads
        )
        tick_rows.append(rows)
        going = [s for s in range(1, sections) if 0 <= tick - (delay(last) - delay(s)) < micro]
        core_pairs = [(s, s - 1) for s in going if s % 2 == 1]
        x_pairs = [(s, s - 1) for s in going if s % 2 == 0]
        core_in = lax.ppermute(sent, "section", core_pairs) if core_pairs else sent
        x_in = x_next
        x_next = lax.ppermute(sent, "section", x_pairs) if x_pairs else sent
    grad_out_all, grad_pre_all, grad_attn_all, grad_mixed_all, grad_first_all = (
        g.reshape(tokens, g.shape[2]) for g in grads
    )
    attn_in_all, context_all, mlp_in_all, activated_all = (
        stores[i].reshape(tokens, stores[i].shape[2]) for i in (1, 4, 6, 8)
    )

    dp_index = lax.axis_index("dp")
    out = Product(context_all, grad_attn_all, high_first, dp_index, infos, 2 * ticks)
    down = [Product(activated_all, grad_out_all, low_first, dp_index, infos, 2 * ticks, part, 2) for part in range(2)]
    up = [Product(mlp_in_all, grad_pre_all, low_first, dp_index, infos, 2 * ticks, part, 2) for part in range(2)]
    qkv = [Product(attn_in_all, grad_mixed_all, low_first, dp_index, infos, 2 * ticks, part, 2) for part in range(2)]
    token = down[0].send(grad_first_all)
    token = down[1].send(token)
    token = out.send(token)
    token = up[0].send(token)
    token = out.keep(token)
    token = down[1].keep(token)
    token = up[0].keep(token)
    token = down[0].keep(token)
    token = down[0].step(None)

    grad_inputs = (dot_nt(grad_first_all, proj_full) + zero_of(token)).astype(BF)
    grad_inputs = spread(grad_inputs, "section", 0).astype(F32)
    row_terms = grad_inputs * jnp.repeat(shrink, seq_len)[:, None] - latent.astype(F32) * weight[:, None]
    zero = zero_of(token)
    grad_table = head_backward(
        rows_sec,
        latent,
        log_total[None, :] + zero,
        (weight + zero)[None, :],
        (ids_rows + zero.astype(jnp.int32))[None, :],
        row_terms.astype(BF),
        token,
    )
    tab = Scatter(grad_table.reshape(groups, -1, emb), low_first, dp_index)
    token = tab.send(token)
    token = up[1].send(token)
    token = up[1].keep(token)
    token = down[1].step(token)
    token = down[0].step(token)
    token = out.step(token)
    for part in qkv:
        token = part.send(token)
        token = part.keep(token)
    token = up[0].step(token)
    token = down[1].step(token)
    token = down[0].end(token)
    token = out.step(token)
    grad_proj = grad_proj + jnp.where(section == 0, dot_tn(inputs_all, after(grad_first_all, token)), 0.0)
    proj_part = scatter_sum(grad_proj.astype(BF).reshape(sections, emb // sections, width), "section", section_order[::-1])
    rows = lax.dynamic_slice_in_dim(jnp.stack(tick_rows), back_offset, micro, 0)
    rows = after(rows, token)
    w_time_term = jnp.dot(time_low.astype(F32).T, rows[:, 2], precision=PRECISION_MAXIMAL)
    gain_rows = jnp.sum(rows[:, :2], axis=0)
    gain_rows = jnp.transpose(gain_rows.reshape(2, groups, width // groups), (1, 0, 2)).reshape(groups, 1, -1)
    at = [emb // groups, emb // sections // groups]
    pad = -sum(at) % 16 or 16
    gain_rows = jnp.pad(gain_rows, ((0, 0), (0, pad - 1), (0, width - gain_rows.shape[2])))
    packed = jnp.concatenate(
        [
            w_time_term.astype(BF).reshape(groups, -1, width),
            proj_part.astype(BF).reshape(groups, -1, width),
            gain_rows.astype(BF),
        ],
        axis=1,
    )
    pack = Scatter(packed, high_first, dp_index)
    token = pack.send(token)
    token = tab.step(token)
    token = up[0].step(token)
    token = down[1].end(token)
    token = pack.step(token)
    token = up[1].step(token)
    token = tab.step(token)
    token = up[0].end(token)
    token = pack.step(token)
    token = qkv[0].step(token)
    token = up[1].step(token)
    token = tab.end(token)
    token = qkv[0].step(token)
    token = qkv[1].step(token)
    square_sums = after(square_sums, token)
    square_got = swap(square_sums, "dp", low_first[0])
    token = up[1].end(token)
    square_sums = square_sums + after(square_got, token)
    token = qkv[1].step(square_sums)
    token = qkv[0].end(token)
    token = out.end(token)
    token = pack.end(token)
    for bit in low_first[1:]:
        square_sums = square_sums + swap(square_sums, "dp", bit)
    token = qkv[1].end(after(square_sums, token))
    target_logit = jnp.sum(latent.astype(F32) * picked_all.astype(F32), axis=1)
    token_loss = (log_total - target_logit) * weight
    seq_loss = jnp.sum(token_loss.reshape(micro, seq_len), axis=1) / seq_len
    count_all = jnp.sum(after(seq_counts.astype(F32), token))
    layer_rms = jnp.sqrt(square_sums / (count_all * seq_len * width))[None, :]
    packed = pack.total
    w_out_grad = out.total
    w_down_grad = jnp.concatenate([part.total for part in down], axis=1)
    w_up_grad = jnp.concatenate([part.total for part in up], axis=1)
    w_qkv_grad = jnp.concatenate([qkv[0].total, qkv[1].total], axis=1)
    w_time_grad = packed[: at[0]]
    proj_grad = packed[at[0] : sum(at)]
    gains = packed[sum(at), : 2 * width // groups].reshape(2, width // groups)
    table_grad = table_back(tab.total)[0]
    grad_mine = lax.dynamic_slice_in_dim(
        grad_inputs.reshape(micro, seq_len, emb), section * shard, shard, 1
    )
    noise_grad = grad_mine * (sigma * shrink)[:, None, None]
    return (
        seq_loss,
        layer_rms,
        noise_grad,
        table_grad,
        proj_grad,
        w_time_grad[None],
        gains[0][None],
        w_qkv_grad[None],
        w_out_grad[None],
        gains[1][None],
        w_up_grad[None],
        w_down_grad[None],
    )


def solution(mesh):
    return jax.shard_map(
        body,
        mesh=mesh,
        in_specs=(
            P("dp", "section"),
            P("dp", "section", None),
            P("dp", "section"),
            P("dp"),
            P(),
            P(("section", "dp"), None),
            P(("section", "dp"), None),
            P("section", None, None),
            P("section", None),
            P("section", None, None),
            P("section", None, None),
            P("section", None),
            P("section", None, None),
            P("section", None, None),
        ),
        out_specs=(
            P("dp"),
            P("section", None),
            P("dp", "section", None),
            P(("section", "dp"), None),
            P(("section", "dp"), None),
            P("section", "dp", None),
            P("section", "dp"),
            P("section", "dp", None),
            P("section", "dp", None),
            P("section", "dp"),
            P("section", "dp", None),
            P("section", "dp", None),
        ),
        check_vma=False,
    )
```
